32 devices in a mesh: lon: 16 (over z, x, core), lat: 2 (over y).
Axes of the slice: x: 2, y: 2, z: 4, core: 2. Of those that a mesh axis runs over, the one named last changes fastest.
Arguments:
- tokens: bfloat16 [32, 1024, 768], P('lat', 'lon'), may hold values from -6 to 6
- qkv_weight: bfloat16 [768, 2304], replicated, may hold values from -0.21875 to 0.21875
- out_weight: bfloat16 [768, 768], replicated, may hold values from -0.5 to 0.5
- bias_table: float32 [465, 6], replicated, may hold values from -6 to 256
- position_index: int32 [128, 128], replicated, may hold values from 0 to 464
- region_label: int32 [32, 1024], P('lat', 'lon'), may hold values from 0 to 3
Outputs:
- updated: bfloat16 [32, 1024, 768], P('lat', 'lon')
The draws below stay inside these ranges and needn't reach their ends.
All inputs are finite; a program needn't handle non-finite values.
Results may differ from the reference program's by a relative error of at most 0.007.
Values may be sent and summed in bfloat16 or wider, within the bound.
No kernel may reach another device: no remote copies, remote signals or barrier semaphores. Data moves between devices by JAX's collectives and lax.ppermute only.
A program may use at most 64 MiB of HBM per device.

```python
import jax
import jax.numpy as jnp
from jax import lax

D = 768
HEADS = 6
HEAD = 128
WLAT = 8
WLON = 16
WIN = 128
NBIAS = 465
SLAT = 4
SLON = 8
NLAT = 32
NLON = 1024


def draw_bias_table(key, part):
    key = jax.random.fold_in(key, 11)
    first = jax.random.fold_in(key, 0)
    shape = (NBIAS, HEADS)
    return jnp.clip(1.5 * jax.random.normal(first, shape, jnp.float32), -6.0, 6.0)


def with_ends(array, own_key, low, top_value):
    extent = array.shape
    place = [jax.random.randint(jax.random.fold_in(own_key, axis), (), 0, extent[axis]) for axis in range(len(extent))]
    array = array.at[tuple(place)].set(low)
    longest = extent.index(max(extent))
    place[longest] = (place[longest] + 1) % extent[longest]
    return array.at[tuple(place)].set(top_value)


def shard_levels(key, extent, cuts, smallest, high):
    level, own = 1.0, jax.random.fold_in(key, 6)
    for position, blocks in cuts:
        heights = jnp.exp(jax.random.uniform(jax.random.fold_in(own, position), (blocks,), jnp.float32, smallest / len(cuts), high / len(cuts)))
        level = level * jnp.repeat(heights, extent[position] // blocks).reshape([-1 if axis == position else 1 for axis in range(len(extent))])
    return level


def gaussian(rng, shape, width, limit, shards=(), dtype=jnp.bfloat16):
    result = width * jax.random.normal(rng, shape, jnp.float32)
    if shards:
        result = result * shard_levels(rng, shape, shards, -0.22, 0.18)
    return jnp.clip(result, -limit, limit).astype(dtype)


def setup_inputs(seed: int = 0) -> dict:
    keys = jax.random.split(jax.random.key(seed), 7)
    return {
        "tokens": gaussian(keys[0], (NLAT, NLON, D), 1.0, 6.0, ((0, 2), (1, 16))),
        "qkv_weight": gaussian(keys[1], (D, 3 * D), D ** -0.5, 0.21875),
        "out_weight": gaussian(keys[2], (D, D), HEAD ** -0.5, 0.5),
        "bias_table": draw_bias_table(jax.random.fold_in(keys[6], 71), 0),
        "position_index": with_ends(jax.random.randint(keys[4], (WIN, WIN), 0, NBIAS), jax.random.fold_in(keys[4], 1), 0, NBIAS - 1).astype(jnp.int32),
        "region_label": with_ends(jax.random.randint(keys[5], (NLAT, NLON), 0, 4), jax.random.fold_in(keys[5], 1), 0, 3).astype(jnp.int32),
    }


def normalize(values):
    floats = values.astype(jnp.float32)
    center = lax.optimization_barrier(jnp.mean(floats, axis=-1, keepdims=True))
    spread = lax.optimization_barrier(jnp.mean(jnp.square(floats - center), axis=-1, keepdims=True))
    return ((floats - center) * lax.rsqrt(spread + 1e-05)).astype(jnp.bfloat16)

def attend(qkv, labels, bias_heads, out_weight):
    row_count, column_count, triple = qkv.shape
    feature_count = triple // 3
    head_size = feature_count // HEADS
    band_count = row_count // WLAT
    strip_count = column_count // WLON
    windows = qkv.reshape(band_count, WLAT, strip_count, WLON, triple).transpose(0, 2, 1, 3, 4)
    windows = windows.reshape(band_count * strip_count, WLAT * WLON, triple).astype(jnp.float32)
    queries = windows[:, :, :feature_count].reshape(-1, WLAT * WLON, HEADS, head_size)
    key_part = windows[:, :, feature_count:2 * feature_count].reshape(-1, WLAT * WLON, HEADS, head_size)
    values = windows[:, :, 2 * feature_count:].reshape(-1, WLAT * WLON, HEADS, head_size)
    label_windows = labels.reshape(band_count, WLAT, strip_count, WLON).transpose(0, 2, 1, 3)
    label_windows = label_windows.reshape(band_count * strip_count, WLAT * WLON)
    matching = (label_windows[:, :, None] == label_windows[:, None, :])[:, None]
    scores = jnp.einsum('wqhd,wkhd->whqk', queries, key_part)
    scores = scores * (1.0 / jnp.sqrt(jnp.float32(head_size))) + bias_heads[None]
    largest = lax.optimization_barrier(jnp.max(jnp.where(matching, scores, -jnp.inf), axis=-1, keepdims=True))
    numerators = jnp.exp(jnp.where(matching, scores - largest, -jnp.inf))
    weights = (numerators / lax.optimization_barrier(jnp.sum(numerators, axis=-1, keepdims=True))).astype(jnp.bfloat16)
    attended = jnp.einsum('whqk,wkhd->wqhd', weights.astype(jnp.float32), values).astype(jnp.bfloat16)
    attended = attended.reshape(band_count, strip_count, WLAT, WLON, feature_count).transpose(0, 2, 1, 3, 4)
    attended = attended.reshape(row_count, column_count, feature_count)
    return jnp.dot(attended, out_weight, preferred_element_type=jnp.float32).astype(jnp.bfloat16)

def reference(tokens, qkv_weight, out_weight, bias_table, position_index, region_label):
    bias_heads = jnp.take(bias_table, position_index, axis=0).transpose(2, 0, 1).astype(jnp.float32)
    shifted = jnp.roll(tokens, (-SLAT, -SLON), axis=(0, 1))
    band_cells = shifted.reshape(NLAT // WLAT, WLAT, NLON, D)
    band_labels = region_label.reshape(NLAT // WLAT, WLAT, NLON)

    def one_band(operands):
        cells, labels = operands
        qkv = jnp.dot(normalize(cells), qkv_weight, preferred_element_type=jnp.float32).astype(jnp.bfloat16)
        return attend(qkv, labels, bias_heads, out_weight)
    branch = lax.map(one_band, (band_cells, band_labels)).reshape(NLAT, NLON, D)
    returned = jnp.roll(branch, (SLAT, SLON), axis=(0, 1))
    return (tokens.astype(jnp.float32) + returned.astype(jnp.float32)).astype(jnp.bfloat16)
```

```python
import functools

import jax
import jax.numpy as jnp
from jax import lax
from jax.experimental import pallas as pl
from jax.experimental.pallas import tpu as pltpu
from jax.sharding import PartitionSpec as P

HEADS = 6
HEAD = 128
WLAT = 8
WLON = 16
WIN = WLAT * WLON
HALF_LAT = WLAT // 2
HALF_LON = WLON // 2
LOG2E = 1.4426950408889634
SCALE = LOG2E / HEAD**0.5
EXCLUDED = -1e30
VMEM_LIMIT = 24 * 2**20
VMEM = pl.BlockSpec(memory_space=pltpu.VMEM)

TOP, MIDDLE, BOTTOM = (HALF_LAT, WLAT), (0, WLAT), (0, HALF_LAT)
LEFT, INNER, RIGHT = (HALF_LON, WLON), (0, WLON), (0, HALF_LON)


def moved(block, axis, distance):
    count = lax.axis_size(axis)
    route = [((i - distance) % count, i) for i in range(count)]
    return lax.ppermute(block, axis, route)


def lat_halo(first, last):
    if lax.axis_size("lat") == 2:
        both = moved(jnp.concatenate([last, first], axis=0), "lat", 1)
        return both[:HALF_LAT], both[HALF_LAT:]
    return moved(last, "lat", 1), moved(first, "lat", -1)


def bias_kernel(table_ref, index_ref, out_ref):
    table = table_ref[...]
    for row in range(0, WIN, 8):
        index = index_ref[row : row + 8, :]
        low, high = index & 127, index >> 7
        for head in range(HEADS):
            value = jnp.zeros((8, WIN), jnp.float32)
            for part in range(4):
                source = jnp.broadcast_to(table[head : head + 1, part * 128 : part * 128 + 128], (8, 128))
                taken = jnp.take_along_axis(source, low, axis=1)
                value = jnp.where(high == part, taken, value)
            out_ref[head, row : row + 8, :] = value * LOG2E


def bias_lookup(bias_table, position_index):
    table = jnp.pad(bias_table.T, ((0, 8 - HEADS), (0, 512 - bias_table.shape[0])))
    return pl.pallas_call(
        bias_kernel,
        out_shape=jax.ShapeDtypeStruct((HEADS, WIN, WIN), jnp.float32),
        in_specs=[VMEM, VMEM],
        out_specs=VMEM,
        compiler_params=pltpu.CompilerParams(vmem_limit_bytes=VMEM_LIMIT),
        cost_estimate=pl.CostEstimate(flops=10**6, bytes_accessed=10**6, transcendentals=0),
    )(table, position_index)


def window_kernel(parts, x_ref, label_ref, bias_ref, qkv_weight_ref, out_weight_ref, out_ref, keys_ref, queries_ref, attended_ref):
    feature = x_ref.shape[-1]
    counts = [(r[1] - r[0]) * (c[1] - c[0]) for r, c in parts]
    starts = [sum(counts[:i]) for i in range(len(parts))]
    for w, (rows, columns) in enumerate(parts):
        floats = x_ref[w].astype(jnp.float32)
        center = jnp.mean(floats, axis=-1, keepdims=True)
        floats = floats - center
        spread = jnp.mean(jnp.square(floats), axis=-1, keepdims=True)
        normed = floats * lax.rsqrt(spread + 1e-05)
        keys_ref[w * WIN : (w + 1) * WIN, :] = normed.reshape(WIN, feature).astype(jnp.bfloat16)
        own = normed[rows[0] : rows[1], columns[0] : columns[1]].reshape(counts[w], feature)
        queries_ref[starts[w] : starts[w] + counts[w], :] = own.astype(jnp.bfloat16)

    def own_rows(array, w):
        rows, columns = parts[w]
        if array.shape[0] == counts[w]:
            return array
        array = array.reshape(WLAT, WLON, array.shape[-1])
        return array[rows[0] : rows[1], columns[0] : columns[1]].reshape(counts[w], array.shape[-1])

    labels = label_ref[...].astype(jnp.float32)
    label_columns = labels.T
    excluded = []
    for w in range(len(parts)):
        same = label_columns[:, w : w + 1] == labels[w : w + 1, :]
        excluded.append(own_rows(jnp.where(same, 0.0, EXCLUDED), w))

    def project(source_ref, first):
        weight = qkv_weight_ref[:, first : first + 2 * HEAD]
        return jnp.dot(source_ref[...], weight, preferred_element_type=jnp.float32).astype(jnp.bfloat16)

    for pair in range(HEADS // 2):
        queries = project(queries_ref, pair * 2 * HEAD)
        keys = project(keys_ref, feature + pair * 2 * HEAD)
        values = project(keys_ref, 2 * feature + pair * 2 * HEAD)
        for w in range(len(parts)):
            mine = slice(starts[w], starts[w] + counts[w])
            whole = slice(w * WIN, (w + 1) * WIN)
            for side in range(2):
                head = pair * 2 + side
                lanes = slice(side * HEAD, (side + 1) * HEAD)
                scores = lax.dot_general(
                    queries[mine, lanes], keys[whole, lanes], (((1,), (1,)), ((), ())), preferred_element_type=jnp.float32
                )
                scores = scores * SCALE + (own_rows(bias_ref[head], w) + excluded[w])
                numerators = jnp.exp2(scores - jnp.max(scores, axis=-1, keepdims=True))
                total = jnp.sum(numerators, axis=-1, keepdims=True)
                summed = jnp.dot(numerators.astype(jnp.bfloat16), values[whole, lanes], preferred_element_type=jnp.float32)
                attended_ref[mine, head * HEAD : (head + 1) * HEAD] = (summed / total).astype(jnp.bfloat16)

    branch = jnp.dot(attended_ref[...], out_weight_ref[...], preferred_element_type=jnp.float32).astype(jnp.bfloat16)
    for w, (rows, columns) in enumerate(parts):
        mine = slice(starts[w], starts[w] + counts[w])
        own = x_ref[w].astype(jnp.float32)[rows[0] : rows[1], columns[0] : columns[1]].reshape(counts[w], feature)
        out_ref[mine, :] = (own + branch[mine].astype(jnp.float32)).astype(jnp.bfloat16)


def attend(windows, labels, bias, qkv_weight, out_weight, parts):
    feature = windows[0].shape[-1]
    x = jnp.stack(windows)
    labels = jnp.pad(jnp.stack(labels), ((0, 8 - len(labels)), (0, 0)))
    sizes = [(r[1] - r[0], c[1] - c[0]) for r, c in parts]
    total = sum(r * c for r, c in sizes)
    flops = 2 * feature * feature * (2 * len(parts) * WIN + 2 * total) + 4 * total * WIN * feature
    updated = pl.pallas_call(
        functools.partial(window_kernel, parts),
        out_shape=jax.ShapeDtypeStruct((total, feature), jnp.bfloat16),
        in_specs=[VMEM] * 5,
        out_specs=VMEM,
        scratch_shapes=[
            pltpu.VMEM((len(parts) * WIN, feature), jnp.bfloat16),
            pltpu.VMEM((total, feature), jnp.bfloat16),
            pltpu.VMEM((total, feature), jnp.bfloat16),
        ],
        compiler_params=pltpu.CompilerParams(vmem_limit_bytes=VMEM_LIMIT),
        cost_estimate=pl.CostEstimate(flops=flops, bytes_accessed=10**6, transcendentals=total * WIN * HEADS),
    )(x, labels, bias, qkv_weight, out_weight)
    blocks, start = [], 0
    for r, c in sizes:
        blocks.append(updated[start : start + r * c].reshape(r, c, feature))
        start += r * c
    return blocks


def shards(tokens, qkv_weight, out_weight, bias_table, position_index, region_label):
    row_count, column_count, feature = tokens.shape
    bands, strips = row_count // WLAT, column_count // WLON
    lat_rows = [(row_count - HALF_LAT, row_count), (0, HALF_LAT)]
    label_windows = region_label.reshape(bands, WLAT, strips, WLON).transpose(0, 2, 1, 3).reshape(bands, strips, WIN)

    first, last = tokens[:HALF_LAT], tokens[-HALF_LAT:]
    ends = lambda block: jnp.concatenate([block[:, :HALF_LON], block[:, -HALF_LON:]], axis=1)
    above_ends, below_ends = lat_halo(ends(first), ends(last))
    above, below = lat_halo(first[:, HALF_LON:-HALF_LON], last[:, HALF_LON:-HALF_LON])
    label_above = moved(label_windows[-1:], "lat", 1)
    labels = jnp.concatenate([label_above, label_windows], axis=0)

    column = lambda part: jnp.concatenate([above_ends[:, part], tokens[:, part], below_ends[:, part]], axis=0)
    own_left, own_right = column(slice(None, HALF_LON)), column(slice(-HALF_LON, None))
    from_left = moved(own_right, "lon", 1)
    from_right = moved(own_left, "lon", -1)
    label_left = moved(labels[:, -1:], "lon", 1)
    labels = jnp.concatenate([label_left, labels], axis=1)

    bias = bias_lookup(bias_table, position_index)
    call = functools.partial(attend, bias=bias, qkv_weight=qkv_weight, out_weight=out_weight)

    inner_rows = [slice(HALF_LAT + b * WLAT, HALF_LAT + (b + 1) * WLAT) for b in range(bands - 1)]
    inner_columns = [slice(HALF_LON + s * WLON, HALF_LON + (s + 1) * WLON) for s in range(strips - 1)]
    grid = {}

    def work(places):
        windows, names, parts = [], [], []
        for b, s in places:
            rows = TOP if b == 0 else BOTTOM if b == bands else MIDDLE
            columns = LEFT if s == 0 else RIGHT if s == strips else INNER
            if s in (0, strips):
                block = jnp.concatenate([from_left, own_left] if s == 0 else [own_right, from_right], axis=1)
                window = block[b * WLAT : (b + 1) * WLAT]
            elif b in (0, bands):
                part = inner_columns[s - 1]
                halo = slice((s - 1) * WLON, s * WLON)
                pieces = [above[:, halo], first[:, part]] if b == 0 else [last[:, part], below[:, halo]]
                window = jnp.concatenate(pieces, axis=0)
            else:
                window = tokens[inner_rows[b - 1], inner_columns[s - 1]]
            windows.append(window)
            names.append(labels[b, s])
            parts.append((rows, columns))
        for place, block in zip(places, call(windows, names, parts=tuple(parts))):
            grid[place] = block

    for b in range(1, bands):
        work([(b, s) for s in range(1, strips)])
    work([(b, s) for b in range(bands + 1) for s in (0, strips)])
    work([(b, s) for b in (0, bands) for s in range(1, strips)])
    return jnp.concatenate(
        [jnp.concatenate([grid[b, s] for s in range(strips + 1)], axis=1) for b in range(bands + 1)], axis=0
    )


def solution(mesh):
    in_specs = (P("lat", "lon", None), P(), P(), P(), P(), P("lat", "lon"))
    out_specs = P("lat", "lon", None)
    return jax.shard_map(shards, mesh=mesh, in_specs=in_specs, out_specs=out_specs, check_vma=False)
```

```python
import functools

import jax
import jax.numpy as jnp
from jax import lax
from jax.experimental import pallas as pl
from jax.experimental.pallas import tpu as pltpu
from jax.sharding import PartitionSpec as P

HEADS = 6
HEAD = 128
WLAT = 8
WLON = 16
WIN = WLAT * WLON
HALF_LAT = WLAT // 2
HALF_LON = WLON // 2
LOG2E = 1.4426950408889634
SCALE = LOG2E / HEAD**0.5
EXCLUDED = -1e30
VMEM_LIMIT = 24 * 2**20
VMEM = pl.BlockSpec(memory_space=pltpu.VMEM)
HBM = pl.BlockSpec(memory_space=pl.ANY)
F32 = jnp.float32
BF16 = jnp.bfloat16


def moved(block, axis, distance):
    count = lax.axis_size(axis)
    route = [((i - distance) % count, i) for i in range(count)]
    return lax.ppermute(block, axis, route)


def lat_exchange(message):
    if lax.axis_size("lat") == 2:
        return moved(message, "lat", 1)
    return jnp.concatenate([moved(message[:HALF_LAT], "lat", -1), moved(message[HALF_LAT:], "lat", 1)], axis=0)


def run(kernel, outs, operands, flops=10**6, exponentials=0, scratch=(), specs=None, out_specs=None, aliases=None, side=False):
    return pl.pallas_call(
        kernel,
        out_shape=outs,
        in_specs=specs or [VMEM] * len(operands),
        out_specs=out_specs or [VMEM] * len(outs),
        scratch_shapes=scratch,
        input_output_aliases=aliases or {},
        compiler_params=pltpu.CompilerParams(vmem_limit_bytes=VMEM_LIMIT),
        cost_estimate=pl.CostEstimate(flops=flops, bytes_accessed=10**6, transcendentals=exponentials),
    )(*operands)


def shape(*extent, dtype=BF16):
    return jax.ShapeDtypeStruct(extent, dtype)


def normalize(floats):
    floats = floats - jnp.mean(floats, axis=-1, keepdims=True)
    return floats * lax.rsqrt(jnp.mean(jnp.square(floats), axis=-1, keepdims=True) + 1e-05)


def label_rows(labels, strips):
    rows, columns = labels.shape
    labels = labels.astype(BF16)
    source = lax.broadcasted_iota(jnp.int32, (columns, WIN), 0)
    cell = lax.broadcasted_iota(jnp.int32, (columns, WIN), 1)
    at_row = lax.broadcasted_iota(jnp.int32, (rows, WIN), 0) % WLAT == lax.broadcasted_iota(jnp.int32, (rows, WIN), 1) // WLON
    place = lax.broadcasted_iota(jnp.int32, (rows // WLAT * strips, WIN), 0)
    result = jnp.zeros((rows // WLAT * strips, WIN), F32)
    for strip in range(strips):
        spread = jnp.dot(labels, (source == strip * WLON + cell % WLON).astype(BF16), preferred_element_type=F32)
        spread = jnp.where(at_row, spread, 0.0)
        for band in range(rows // WLAT):
            row = jnp.sum(spread[band * WLAT : (band + 1) * WLAT], axis=0, keepdims=True)
            result = jnp.where(place == band * strips + strip, row, result)
    return result


def message_kernel(strips, tokens_ref, label_ref, ends_ref, inner_ref, rows_ref, edge_ref, sems):
    row_count, column_count, feature = tokens_ref.shape
    copies = [
        pltpu.make_async_copy(tokens_ref.at[pl.ds(0, HALF_LAT)], edge_ref.at[pl.ds(0, HALF_LAT)], sems.at[0]),
        pltpu.make_async_copy(tokens_ref.at[pl.ds(row_count - HALF_LAT, HALF_LAT)], edge_ref.at[pl.ds(HALF_LAT, HALF_LAT)], sems.at[1]),
    ]
    for copy in copies:
        copy.start()
    rows = label_rows(label_ref[...], strips)
    rows_ref[...] = rows
    padded = jnp.concatenate([rows, jnp.zeros((2 * HALF_LON - rows.shape[0], WIN), F32)], axis=0)
    ends_ref[WLAT] = jnp.concatenate([padded, jnp.zeros((2 * HALF_LON, feature - WIN), F32)], axis=1).astype(BF16)
    for copy in copies:
        copy.wait()
    for row in range(WLAT):
        floats = edge_ref[row].astype(F32)
        ends_ref[row] = jnp.concatenate([floats[:HALF_LON], floats[-HALF_LON:]], axis=0).astype(BF16)
        inner_ref[row] = floats[HALF_LON:-HALF_LON].astype(BF16)


def bias_kernel(table_ref, index_ref, out_ref):
    table = table_ref[...]
    for row in range(0, WIN, 8):
        index = index_ref[row : row + 8, :]
        low, high = index & 127, index >> 7
        for head in range(HEADS):
            value = jnp.zeros((8, WIN), F32)
            for part in range(4):
                source = jnp.broadcast_to(table[head : head + 1, part * 128 : part * 128 + 128], (8, 128))
                value = jnp.where(high == part, jnp.take_along_axis(source, low, axis=1), value)
            out_ref[head, row : row + 8, :] = value * LOG2E


def column_kernel(strips, tokens_ref, ends_ref, rows_ref, left_ref, right_ref, labels_ref):
    row_count, column_count, feature = tokens_ref.shape
    for row in range(row_count + WLAT):
        if row < HALF_LAT or row >= row_count + HALF_LAT:
            floats = ends_ref[(row + HALF_LAT) if row < HALF_LAT else row - row_count - HALF_LAT].astype(F32)
            left, right = floats[:HALF_LON], floats[HALF_LON:]
        else:
            left = tokens_ref[row - HALF_LAT, :WLON, :].astype(F32)[:HALF_LON]
            right = tokens_ref[row - HALF_LAT, column_count - WLON :, :].astype(F32)[HALF_LON:]
        left_ref[row] = left.astype(BF16)
        right_ref[row] = right.astype(BF16)
    own = rows_ref[...]
    above = ends_ref[WLAT].astype(F32)[own.shape[0] - strips : own.shape[0], :WIN]
    labels = jnp.concatenate([above, own, jnp.zeros((16 - strips - own.shape[0], WIN), F32)], axis=0)
    labels_ref[...] = labels
    filler = jnp.zeros((HALF_LON, feature - 2 * WIN), F32)
    right_ref[row_count + WLAT] = jnp.concatenate([labels[:8], labels[8:], filler], axis=1).astype(BF16)


def excluded(columns, row):
    return jnp.where(columns == row, 0.0, EXCLUDED)


def attention(entries):
    scores = []
    for queries, keys, _, bias, _ in entries:
        product = lax.dot_general(queries(), keys(), (((1,), (1,)), ((), ())), preferred_element_type=F32)
        scores.append(product * SCALE + bias())
    numerators = [jnp.exp2(score - jnp.max(score, axis=-1, keepdims=True)) for score in scores]
    for (_, _, values, _, store), numerator in zip(entries, numerators):
        total = jnp.sum(numerator, axis=-1, keepdims=True)
        summed = jnp.dot(numerator.astype(BF16), values(), preferred_element_type=F32)
        store((summed * (1.0 / total)).astype(BF16))


def project(source, weight_ref, first, count):
    return jnp.dot(source, weight_ref[:, first : first + count], preferred_element_type=F32).astype(BF16)


def out_project(attended_ref, weight_ref):
    return jnp.dot(attended_ref[...], weight_ref[...], preferred_element_type=F32).astype(BF16).astype(F32)


def lanes(head):
    return slice(head * HEAD, (head + 1) * HEAD)


def storer(ref, rows, head):
    def store(value):
        ref[rows, lanes(head)] = value

    return store


def inner_kernel(strips, tokens_ref, rows_ref, bias_ref, qkv_weight_ref, out_weight_ref, out_ref, cells_ref, qkv_ref, attended_ref):
    row_count, column_count, feature = tokens_ref.shape
    floats = []
    for strip in range(strips - 1):
        columns = slice(HALF_LON + strip * WLON, HALF_LON + (strip + 1) * WLON)
        window = tokens_ref[HALF_LAT : HALF_LAT + WLAT, :, :].astype(F32)[:, columns].reshape(WIN, feature)
        floats.append(window)
        cells_ref[strip * WIN : (strip + 1) * WIN, :] = normalize(window).astype(BF16)
    qkv_ref[...] = project(cells_ref[...], qkv_weight_ref, 0, 3 * feature)
    labels = rows_ref[...]
    label_columns = labels.T
    entries = []
    for strip in range(strips - 1):
        mine = slice(strip * WIN, (strip + 1) * WIN)
        mask = excluded(label_columns[:, strip : strip + 1], labels[strip : strip + 1])
        for head in range(HEADS):
            entries.append(
                (
                    lambda mine=mine, head=head: qkv_ref[mine, lanes(head)],
                    lambda mine=mine, head=head: qkv_ref[mine, lanes(HEADS + head)],
                    lambda mine=mine, head=head: qkv_ref[mine, lanes(2 * HEADS + head)],
                    lambda mask=mask, head=head: bias_ref[head] + mask,
                    storer(attended_ref, mine, head),
                )
            )
    attention(entries)
    branch = out_project(attended_ref, out_weight_ref)
    for strip in range(strips - 1):
        mine = slice(strip * WIN, (strip + 1) * WIN)
        out_ref[mine, :] = (floats[strip] + branch[mine]).astype(BF16)


def rows_kernel(strips, tokens_ref, qkv_weight_ref, order_ref, out_ref, cells_ref):
    row_count, column_count, feature = tokens_ref.shape
    half = HALF_LAT * WLON
    for side, first in enumerate((0, row_count - HALF_LAT)):
        floats = tokens_ref[first : first + HALF_LAT, :, :].astype(F32)
        for strip in range(strips - 1):
            block = floats[:, HALF_LON + strip * WLON : HALF_LON + (strip + 1) * WLON].reshape(half, feature)
            start = (side * (strips - 1) + strip) * half
            cells_ref[start : start + half, :] = normalize(block).astype(BF16)
    out_ref[...] = project(cells_ref[...], qkv_weight_ref, 0, 3 * feature)


def side_kernel(strips, tokens_ref, from_left_ref, from_right_ref, ends_ref, labels_ref, bias_ref, qkv_weight_ref, out_weight_ref,
                inner_ref, out_ref, corner_ref, cells_ref, own_ref, queries_ref, keys_ref, attended_ref, block_ref, sem):
    row_count, column_count, feature = tokens_ref.shape
    bands = row_count // WLAT
    labels = labels_ref[...]
    received = from_left_ref[row_count + WLAT].astype(F32)
    label_columns = labels.T
    left_columns = (received[:, :WIN].T, received[:, WIN : 2 * WIN].T)
    windows = []
    start = 0
    for band in range(bands + 1):
        count = HALF_LON * (WLAT if 0 < band < bands else HALF_LAT)
        for side in range(2):
            windows.append((band, side, start, count))
            start += count
    tokens_of = {}
    for at, (band, side, start, count) in enumerate(windows):
        halo, own = [], []
        for row in range(band * WLAT, (band + 1) * WLAT):
            if row < HALF_LAT or row >= row_count + HALF_LAT:
                floats = ends_ref[(row + HALF_LAT) if row < HALF_LAT else row - row_count - HALF_LAT].astype(F32)
                own.append(floats[HALF_LON:] if side else floats[:HALF_LON])
            elif side:
                own.append(tokens_ref[row - HALF_LAT, column_count - WLON :, :].astype(F32)[HALF_LON:])
            else:
                own.append(tokens_ref[row - HALF_LAT, :WLON, :].astype(F32)[:HALF_LON])
            halo.append((from_right_ref if side else from_left_ref)[row].astype(F32))
        mine = slice(HALF_LAT if band == 0 else 0, HALF_LAT if band == bands else WLAT)
        tokens_of[band, side] = own[mine]
        own = normalize(jnp.stack(own))
        halo = normalize(jnp.stack(halo))
        window = jnp.concatenate([own, halo] if side else [halo, own], axis=1)
        cells_ref[at * WIN : (at + 1) * WIN, :] = window.reshape(WIN, feature).astype(BF16)
        own_ref[start : start + count, :] = own[mine].reshape(count, feature).astype(BF16)
    queries_ref[...] = project(own_ref[...], qkv_weight_ref, 0, feature)
    keys_ref[...] = project(cells_ref[...], qkv_weight_ref, feature, 2 * feature)

    def own_rows(array, band, side):
        array = array.reshape(WLAT, WLON, WIN)
        array = array[HALF_LAT if band == 0 else 0 : HALF_LAT if band == bands else WLAT]
        array = array[:, :HALF_LON] if side else array[:, HALF_LON:]
        return array.reshape(-1, WIN)

    entries = []
    for at, (band, side, start, count) in enumerate(windows):
        mine, whole = slice(start, start + count), slice(at * WIN, (at + 1) * WIN)
        place = band * strips + strips - 1
        if side:
            mask = excluded(label_columns[:, place : place + 1], labels[place : place + 1])
        else:
            group, place = divmod(place, 8)
            row = received[place : place + 1, group * WIN : (group + 1) * WIN]
            mask = excluded(left_columns[group][:, place : place + 1], row)
        mask = own_rows(mask, band, side)
        for head in range(HEADS):
            entries.append(
                (
                    lambda mine=mine, head=head: queries_ref[mine, lanes(head)],
                    lambda whole=whole, head=head: keys_ref[whole, lanes(head)],
                    lambda whole=whole, head=head: keys_ref[whole, lanes(HEADS + head)],
                    lambda mask=mask, head=head, band=band, side=side: own_rows(bias_ref[head], band, side) + mask,
                    storer(attended_ref, mine, head),
                )
            )
    attention(entries)
    branch = out_project(attended_ref, out_weight_ref)
    blocks = {}
    for band, side, start, count in windows:
        for row, own in enumerate(tokens_of[band, side]):
            at = start + row * HALF_LON
            blocks[band, side, row] = own + branch[at : at + HALF_LON]
    for row in range(WLAT):
        middle = [inner_ref[strip * WIN + row * WLON : strip * WIN + (row + 1) * WLON, :].astype(F32) for strip in range(strips - 1)]
        block_ref[row] = jnp.concatenate([blocks[1, 0, row]] + middle + [blocks[1, 1, row]], axis=0).astype(BF16)
    copy = pltpu.make_async_copy(block_ref, out_ref.at[pl.ds(HALF_LAT, WLAT)], sem)
    copy.start()
    for band, first in ((0, 0), (bands, HALF_LAT)):
        for row in range(HALF_LAT):
            corner_ref[first + row] = jnp.concatenate([blocks[band, 0, row], blocks[band, 1, row]], axis=0).astype(BF16)
    copy.wait()


def last_kernel(strips, tokens_ref, halo_ref, own_ref, labels_ref, bias_ref, qkv_weight_ref, out_weight_ref, corner_ref, partial_ref,
                out_ref, cells_ref, keys_ref, attended_ref, block_ref, sems):
    row_count, column_count, feature = tokens_ref.shape
    bands = row_count // WLAT
    half = HALF_LAT * WLON
    for side in range(2):
        floats = halo_ref[HALF_LAT * (1 - side) : HALF_LAT * (2 - side)].astype(F32)
        for strip in range(strips - 1):
            block = floats[:, strip * WLON : (strip + 1) * WLON].reshape(half, feature)
            start = (side * (strips - 1) + strip) * half
            cells_ref[start : start + half, :] = normalize(block).astype(BF16)
    keys_ref[...] = project(cells_ref[...], qkv_weight_ref, feature, 2 * feature)
    labels = labels_ref[...]
    label_columns = labels.T
    entries = []
    for side in range(2):
        for strip in range(strips - 1):
            start = (side * (strips - 1) + strip) * half
            mine = slice(start, start + half)
            rows = slice(0, half) if side else slice(half, WIN)
            place = side * bands * strips + strip
            mask = excluded(label_columns[rows, place : place + 1], labels[place : place + 1])

            def both(head, mine=mine, side=side):
                own, halo = own_ref[mine, lanes(HEADS + head)], keys_ref[mine, lanes(head)]
                return jnp.concatenate([own, halo] if side else [halo, own], axis=0)

            for head in range(HEADS):
                entries.append(
                    (
                        lambda mine=mine, head=head: own_ref[mine, lanes(head)],
                        lambda head=head, both=both: both(head),
                        lambda head=head, both=both: both(HEADS + head),
                        lambda mask=mask, head=head, rows=rows: bias_ref[head, rows, :] + mask,
                        storer(attended_ref, mine, head),
                    )
                )
    attention(entries)
    branch = out_project(attended_ref, out_weight_ref)
    copies = []
    for side, first in enumerate((0, row_count - HALF_LAT)):
        for row in range(HALF_LAT):
            corner = corner_ref[side * HALF_LAT + row].astype(F32)
            middle = []
            for strip in range(strips - 1):
                start = (side * (strips - 1) + strip) * half + row * WLON
                middle.append(branch[start : start + WLON])
            floats = tokens_ref[first + row].astype(F32)[HALF_LON:-HALF_LON] + jnp.concatenate(middle, axis=0)
            block_ref[side * HALF_LAT + row] = jnp.concatenate([corner[:HALF_LON], floats, corner[HALF_LON:]], axis=0).astype(BF16)
        copies.append(
            pltpu.make_async_copy(
                block_ref.at[pl.ds(side * HALF_LAT, HALF_LAT)], out_ref.at[pl.ds(first, HALF_LAT)], sems.at[side]
            )
        )
        copies[-1].start()
    for copy in copies:
        copy.wait()


def shards(tokens, qkv_weight, out_weight, bias_table, position_index, region_label):
    row_count, column_count, feature = tokens.shape
    bands, strips = row_count // WLAT, column_count // WLON
    inner_columns = column_count - WLON
    whole = shape(*tokens.shape)
    dma = pltpu.SemaphoreType.DMA

    ends, inner_rows, rows = run(
        functools.partial(message_kernel, strips),
        [shape(WLAT + 1, WLON, feature), shape(WLAT, inner_columns, feature), shape(bands * strips, WIN, dtype=F32)],
        [tokens, region_label],
        specs=[HBM, VMEM],
        scratch=[pltpu.VMEM((WLAT, column_count, feature), BF16), dma((2,))],
    )
    ends = lat_exchange(ends)
    inner_rows = lat_exchange(inner_rows)

    table = jnp.pad(bias_table.T, ((0, 8 - HEADS), (0, 512 - bias_table.shape[0])))
    (bias,) = run(bias_kernel, [shape(HEADS, WIN, WIN, dtype=F32)], [table, position_index])

    inner_cells = (strips - 1) * WIN
    (inner,) = run(
        functools.partial(inner_kernel, strips),
        [shape(inner_cells, feature)],
        [tokens, rows, bias, qkv_weight, out_weight],
        flops=8 * inner_cells * feature * feature,
        exponentials=inner_cells * WIN * HEADS,
        scratch=[pltpu.VMEM((inner_cells, width), BF16) for width in (feature, 3 * feature, feature)],
    )
    left, right, labels = run(
        functools.partial(column_kernel, strips),
        [shape(row_count + WLAT, HALF_LON, feature), shape(row_count + WLAT + 1, HALF_LON, feature), shape(16, WIN, dtype=F32)],
        [tokens, ends, rows],
    )
    from_left = moved(right, "lon", 1)
    from_right = moved(left, "lon", -1)

    row_cells = (strips - 1) * WIN
    (row_qkv,) = run(
        functools.partial(rows_kernel, strips),
        [shape(row_cells, 3 * feature)],
        [tokens, qkv_weight, labels],
        flops=6 * row_cells * feature * feature,
        scratch=[pltpu.VMEM((row_cells, feature), BF16)],
    )
    side_windows = 2 * (bands + 1)
    side_cells = 2 * HALF_LON * row_count
    out, corner = run(
        functools.partial(side_kernel, strips),
        [whole, shape(WLAT, WLON, feature)],
        [tokens, from_left, from_right, ends, labels, bias, qkv_weight, out_weight, inner],
        flops=4 * (side_cells + side_windows * WIN) * feature * feature,
        exponentials=side_cells * WIN * HEADS,
        out_specs=[HBM, VMEM],
        scratch=[
            pltpu.VMEM((side_windows * WIN, feature), BF16),
            pltpu.VMEM((side_cells, feature), BF16),
            pltpu.VMEM((side_cells, feature), BF16),
            pltpu.VMEM((side_windows * WIN, 2 * feature), BF16),
            pltpu.VMEM((side_cells, feature), BF16),
            pltpu.VMEM((WLAT, column_count, feature), BF16),
            dma(()),
        ],
    )
    (out,) = run(
        functools.partial(last_kernel, strips),
        [whole],
        [tokens, inner_rows, row_qkv, labels, bias, qkv_weight, out_weight, corner, out],
        flops=6 * row_cells * feature * feature,
        exponentials=row_cells * WIN * HEADS,
        specs=[VMEM] * 8 + [HBM],
        out_specs=[HBM],
        aliases={8: 0},
        scratch=[
            pltpu.VMEM((row_cells, feature), BF16),
            pltpu.VMEM((row_cells, 2 * feature), BF16),
            pltpu.VMEM((row_cells, feature), BF16),
            pltpu.VMEM((WLAT, column_count, feature), BF16),
            dma((2,)),
        ],
    )
    return out


def solution(mesh):
    in_specs = (P("lat", "lon", None), P(), P(), P(), P(), P("lat", "lon"))
    out_specs = P("lat", "lon", None)
    return jax.shard_map(shards, mesh=mesh, in_specs=in_specs, out_specs=out_specs, check_vma=False)
```

```python
import functools

import jax
import jax.numpy as jnp
from jax import lax
from jax.experimental import pallas as pl
from jax.experimental.pallas import tpu as pltpu
from jax.sharding import PartitionSpec as P

HEADS = 6
HEAD = 128
WLAT = 8
WLON = 16
WIN = WLAT * WLON
HALF_LAT = WLAT // 2
HALF_LON = WLON // 2
LOG2E = 1.4426950408889634
SCALE = LOG2E / HEAD**0.5
EXCLUDED = -1e30
VMEM = pl.BlockSpec(memory_space=pltpu.VMEM)
HBM = pl.BlockSpec(memory_space=pltpu.HBM)
ANY = pl.BlockSpec(memory_space=pl.ANY)
F32 = jnp.float32
BF16 = jnp.bfloat16


def moved(block, axis, distance):
    count = lax.axis_size(axis)
    route = [((i - distance) % count, i) for i in range(count)]
    return lax.ppermute(block, axis, route)


def lat_exchange(message):
    if lax.axis_size("lat") == 2:
        return moved(message, "lat", 1)
    return jnp.concatenate([moved(message[:HALF_LAT], "lat", -1), moved(message[HALF_LAT:], "lat", 1)], axis=0)


def lon_exchange(even_odd, odd_even):
    count = lax.axis_size("lon")
    first = [(i, i ^ 1) for i in range(count)]
    second = [(i, (i + 1 if i % 2 else i - 1) % count) for i in range(count)]
    odd_even = lax.ppermute(odd_even, "lon", second)
    return lax.ppermute(even_odd, "lon", first), odd_even


def run(kernel, outs, operands, scratch=(), specs=None, out_specs=None, mib=4, flops=10**6):
    return pl.pallas_call(
        kernel,
        out_shape=outs,
        in_specs=specs or [VMEM] * len(operands),
        out_specs=out_specs or [VMEM] * len(outs),
        scratch_shapes=scratch,
        compiler_params=pltpu.CompilerParams(vmem_limit_bytes=mib * 2**20),
        cost_estimate=pl.CostEstimate(flops=flops, bytes_accessed=10**5, transcendentals=0),
    )(*operands)


def shape(*extent, dtype=BF16):
    return jax.ShapeDtypeStruct(extent, dtype)


def normalize(floats):
    floats = floats - jnp.mean(floats, axis=-1, keepdims=True)
    return floats * lax.rsqrt(jnp.mean(jnp.square(floats), axis=-1, keepdims=True) + 1e-05)


def label_rows(labels, strips):
    rows, columns = labels.shape
    labels = labels.astype(BF16)
    source = lax.broadcasted_iota(jnp.int32, (columns, WIN), 0)
    cell = lax.broadcasted_iota(jnp.int32, (columns, WIN), 1)
    at_row = lax.broadcasted_iota(jnp.int32, (rows, WIN), 0) % WLAT == lax.broadcasted_iota(jnp.int32, (rows, WIN), 1) // WLON
    place = lax.broadcasted_iota(jnp.int32, (rows // WLAT * strips, WIN), 0)
    result = jnp.zeros((rows // WLAT * strips, WIN), F32)
    for strip in range(strips):
        spread = jnp.dot(labels, (source == strip * WLON + cell % WLON).astype(BF16), preferred_element_type=F32)
        spread = jnp.where(at_row, spread, 0.0)
        for band in range(rows // WLAT):
            row = jnp.sum(spread[band * WLAT : (band + 1) * WLAT], axis=0, keepdims=True)
            result = jnp.where(place == band * strips + strip, row, result)
    return result


def message_kernel(tokens_ref, ends_ref, inner_ref, middle_ref, columns_ref):
    row_count = tokens_ref.shape[0]
    for row in range(row_count):
        floats = tokens_ref[row].astype(F32)
        columns = jnp.concatenate([floats[:HALF_LON], floats[-HALF_LON:]], axis=0).astype(BF16)
        inner = floats[HALF_LON:-HALF_LON].astype(BF16)
        columns_ref[row] = columns
        if HALF_LAT <= row < row_count - HALF_LAT:
            middle_ref[row - HALF_LAT] = inner
        else:
            at = row if row < HALF_LAT else row - row_count + WLAT
            ends_ref[at] = columns
            inner_ref[at] = inner


def column_kernel(strips, columns_ref, rows_ref, above_ref, even_odd_ref, odd_even_ref, labels_ref):
    row_count, _, feature = columns_ref.shape
    odd = lax.axis_index("lon") % 2 == 1
    for row in range(row_count):
        floats = columns_ref[row].astype(F32)
        left, right = floats[:HALF_LON], floats[HALF_LON:]
        even_odd_ref[row] = jnp.where(odd, left, right).astype(BF16)
        odd_even_ref[row] = jnp.where(odd, right, left).astype(BF16)
    labels = jnp.concatenate([label_rows(above_ref[above_ref.shape[0] - WLAT :, :], strips), rows_ref[...]], axis=0)
    labels = jnp.concatenate([labels, jnp.zeros((16 - labels.shape[0], WIN), F32)], axis=0)
    labels_ref[...] = labels
    filler = jnp.zeros((HALF_LON, feature - 2 * WIN), F32)
    message = jnp.concatenate([labels[:8], labels[8:], filler], axis=1).astype(BF16)
    even_odd_ref[row_count] = message
    odd_even_ref[row_count] = message


def corner_message_kernel(ends_ref, after_ref, even_odd_ref, odd_even_ref):
    odd = lax.axis_index("lon") % 2 == 1
    for row in range(WLAT):
        floats = ends_ref[row].astype(F32)
        left, right = floats[:HALF_LON], floats[HALF_LON:]
        even_odd_ref[row] = jnp.where(odd, left, right).astype(BF16)
        odd_even_ref[row] = jnp.where(odd, right, left).astype(BF16)


def halo_row(row, row_count):
    return row + HALF_LAT if row < HALF_LAT else row - row_count - HALF_LAT


def look_up(table_ref, index_ref, out_ref):
    entries = table_ref.shape[1]
    for row in range(0, WIN, 8):
        index = index_ref[row : row + 8, :]
        low, high = index & 127, index >> 7
        for head in range(HEADS):
            value = jnp.zeros((8, WIN), F32)
            for part in range(-(-entries // 128)):
                source = jnp.broadcast_to(table_ref[head : head + 1, part * 128 : part * 128 + 128], (8, 128))
                value = jnp.where(high == part, jnp.take_along_axis(source, low, axis=1), value)
            out_ref[head, row : row + 8, :] = value * LOG2E


def excluded(columns, row):
    return jnp.where(columns == row, 0.0, EXCLUDED)


def attention(entries):
    scores = []
    for queries, keys, _, bias, _ in entries:
        product = lax.dot_general(queries(), keys(), (((1,), (1,)), ((), ())), preferred_element_type=F32)
        scores.append(product * SCALE + bias())
    numerators = [jnp.exp2(score - jnp.max(score, axis=-1, keepdims=True)) for score in scores]
    for (_, _, values, _, store), numerator in zip(entries, numerators):
        total = jnp.sum(numerator, axis=-1, keepdims=True)
        summed = jnp.dot(numerator.astype(BF16), values(), preferred_element_type=F32)
        store((summed * (1.0 / total)).astype(BF16))


def project(source, weight_ref, first, count):
    return jnp.dot(source, weight_ref[:, first : first + count], preferred_element_type=F32).astype(BF16)


def out_project(attended, weight_ref):
    return jnp.dot(attended, weight_ref[...], preferred_element_type=F32).astype(BF16).astype(F32)


def lanes(head):
    return slice(head * HEAD, (head + 1) * HEAD)


def storer(ref, rows, head):
    def store(value):
        ref[rows, lanes(head)] = value

    return store


def inner_kernel(strips, middle_ref, label_ref, table_ref, index_ref, qkv_weight_ref, out_weight_ref,
                 out_ref, bias_ref, rows_ref, cells_ref, qkv_ref, attended_ref, wide_ref):
    feature = middle_ref.shape[-1]
    floats = []
    for strip in range(strips - 1):
        window = middle_ref[:, strip * WLON : (strip + 1) * WLON, :].astype(F32).reshape(WIN, feature)
        floats.append(window)
        cells_ref[strip * WIN : (strip + 1) * WIN, :] = normalize(window).astype(BF16)
    wide_ref[...] = jnp.zeros(wide_ref.shape, F32)
    wide_ref[: table_ref.shape[0], : table_ref.shape[1]] = table_ref[...]
    qkv_ref[...] = project(cells_ref[...], qkv_weight_ref, 0, 3 * feature)
    look_up(wide_ref, index_ref, bias_ref)
    labels = label_rows(label_ref[...], strips)
    rows_ref[...] = labels
    label_columns = labels.T
    entries = []
    for strip in range(strips - 1):
        mine = slice(strip * WIN, (strip + 1) * WIN)
        mask = excluded(label_columns[:, strip : strip + 1], labels[strip : strip + 1])
        for head in range(HEADS):
            entries.append(
                (
                    lambda mine=mine, head=head: qkv_ref[mine, lanes(head)],
                    lambda mine=mine, head=head: qkv_ref[mine, lanes(HEADS + head)],
                    lambda mine=mine, head=head: qkv_ref[mine, lanes(2 * HEADS + head)],
                    lambda mask=mask, head=head: bias_ref[head] + mask,
                    storer(attended_ref, mine, head),
                )
            )
    attention(entries)
    branch = out_project(attended_ref[...], out_weight_ref)
    for strip in range(strips - 1):
        mine = slice(strip * WIN, (strip + 1) * WIN)
        out_ref[mine, :] = (floats[strip] + branch[mine]).astype(BF16)


def rows_kernel(strips, inner_ref, qkv_weight_ref, after_ref, out_ref, cells_ref):
    feature = inner_ref.shape[-1]
    half = HALF_LAT * WLON
    for side in range(2):
        for strip in range(strips - 1):
            block = inner_ref[side * HALF_LAT : (side + 1) * HALF_LAT, strip * WLON : (strip + 1) * WLON, :]
            start = (side * (strips - 1) + strip) * half
            cells_ref[start : start + half, :] = normalize(block.astype(F32).reshape(half, feature)).astype(BF16)
    out_ref[...] = project(cells_ref[...], qkv_weight_ref, 0, 3 * feature)


def side_windows(bands, between):
    windows, start = [], 0
    for band in range(bands + 1):
        if (0 < band < bands) == between:
            count = HALF_LON * (WLAT if between else HALF_LAT)
            for side in range(2):
                windows.append((band, side, start, count))
                start += count
    return windows


def side_blocks(windows, bands, strips, own_of, halo_of, left_labels, labels, bias_ref, qkv_weight_ref, out_weight_ref,
                cells_ref, own_ref, queries_ref, keys_ref, attended_ref):
    feature = cells_ref.shape[-1]
    label_columns = left_labels.T, labels.T
    tokens_of = {}
    for at, (band, side, start, count) in enumerate(windows):
        own = [own_of(row, side) for row in range(band * WLAT, (band + 1) * WLAT)]
        halo = [halo_of(row, side) for row in range(band * WLAT, (band + 1) * WLAT)]
        mine = slice(HALF_LAT if band == 0 else 0, HALF_LAT if band == bands else WLAT)
        tokens_of[band, side] = own[mine]
        own = normalize(jnp.stack(own))
        halo = normalize(jnp.stack(halo))
        window = jnp.concatenate([own, halo] if side else [halo, own], axis=1)
        cells_ref[at * WIN : (at + 1) * WIN, :] = window.reshape(WIN, feature).astype(BF16)
        own_ref[start : start + count, :] = own[mine].reshape(count, feature).astype(BF16)
    queries_ref[...] = project(own_ref[...], qkv_weight_ref, 0, feature)
    keys_ref[...] = project(cells_ref[...], qkv_weight_ref, feature, 2 * feature)

    def own_rows(array, band, side):
        array = array.reshape(WLAT, WLON, WIN)
        array = array[HALF_LAT if band == 0 else 0 : HALF_LAT if band == bands else WLAT]
        array = array[:, :HALF_LON] if side else array[:, HALF_LON:]
        return array.reshape(-1, WIN)

    entries = []
    for at, (band, side, start, count) in enumerate(windows):
        mine, whole = slice(start, start + count), slice(at * WIN, (at + 1) * WIN)
        place = band * strips + strips - 1
        row = (labels if side else left_labels)[place : place + 1]
        mask = own_rows(excluded(label_columns[side][:, place : place + 1], row), band, side)
        for head in range(HEADS):
            entries.append(
                (
                    lambda mine=mine, head=head: queries_ref[mine, lanes(head)],
                    lambda whole=whole, head=head: keys_ref[whole, lanes(head)],
                    lambda whole=whole, head=head: keys_ref[whole, lanes(HEADS + head)],
                    lambda mask=mask, head=head, band=band, side=side: own_rows(bias_ref[head], band, side) + mask,
                    storer(attended_ref, mine, head),
                )
            )
    attention(entries)
    branch = out_project(attended_ref[...], out_weight_ref)
    blocks = {}
    for band, side, start, count in windows:
        for row, own in enumerate(tokens_of[band, side]):
            at = start + row * HALF_LON
            blocks[band, side, row] = own + branch[at : at + HALF_LON]
    return blocks


def swapped(even_odd_ref, odd_even_ref):
    odd = lax.axis_index("lon") % 2 == 1

    def row_of(row, side):
        first, second = even_odd_ref[row].astype(F32), odd_even_ref[row].astype(F32)
        return jnp.where(odd, second, first) if side else jnp.where(odd, first, second)

    return row_of


def half_of(floats, side):
    return floats[HALF_LON:] if side else floats[:HALF_LON]


def left_labels_of(received, row):
    message = received(row, 0)
    return jnp.concatenate([message[:, :WIN], message[:, WIN : 2 * WIN]], axis=0)


def between_kernel(strips, columns_ref, even_odd_ref, odd_even_ref, labels_ref, bias_ref, qkv_weight_ref, out_weight_ref, inner_ref,
                   after_ref, out_ref, left_ref, *scratch):
    row_count = columns_ref.shape[0]
    received = swapped(even_odd_ref, odd_even_ref)
    left_labels = left_labels_of(received, row_count)
    left_ref[...] = left_labels
    blocks = side_blocks(
        side_windows(row_count // WLAT, True), row_count // WLAT, strips,
        lambda row, side: half_of(columns_ref[row - HALF_LAT].astype(F32), side),
        lambda row, side: received(row - HALF_LAT, side),
        left_labels, labels_ref[...], bias_ref, qkv_weight_ref, out_weight_ref, *scratch,
    )
    for row in range(WLAT):
        middle = [inner_ref[strip * WIN + row * WLON : strip * WIN + (row + 1) * WLON, :].astype(F32) for strip in range(strips - 1)]
        out_ref[row] = jnp.concatenate([blocks[1, 0, row]] + middle + [blocks[1, 1, row]], axis=0).astype(BF16)


def corner_kernel(strips, columns_ref, even_odd_ref, odd_even_ref, corner_even_odd_ref, corner_odd_even_ref, ends_ref, labels_ref,
                  left_ref, bias_ref, qkv_weight_ref, out_weight_ref, corner_ref, *scratch):
    row_count = columns_ref.shape[0]
    bands = row_count // WLAT
    received = swapped(even_odd_ref, odd_even_ref)
    received_corner = swapped(corner_even_odd_ref, corner_odd_even_ref)

    def inside(row):
        return HALF_LAT <= row < row_count + HALF_LAT

    def own_of(row, side):
        floats = columns_ref[row - HALF_LAT] if inside(row) else ends_ref[halo_row(row, row_count)]
        return half_of(floats.astype(F32), side)

    def halo_of(row, side):
        return received(row - HALF_LAT, side) if inside(row) else received_corner(halo_row(row, row_count), side)

    blocks = side_blocks(
        side_windows(bands, False), bands, strips, own_of, halo_of,
        left_ref[...], labels_ref[...], bias_ref, qkv_weight_ref, out_weight_ref, *scratch,
    )
    for band, first in ((0, 0), (bands, HALF_LAT)):
        for row in range(HALF_LAT):
            corner_ref[first + row] = jnp.concatenate([blocks[band, 0, row], blocks[band, 1, row]], axis=0).astype(BF16)


def last_kernel(strips, inner_ref, halo_ref, own_ref, labels_ref, bias_ref, qkv_weight_ref, out_weight_ref, corner_ref, between_ref,
                out_ref, cells_ref, keys_ref, attended_ref, block_ref, sems):
    row_count, column_count, feature = out_ref.shape
    copies = [pltpu.make_async_copy(between_ref, out_ref.at[pl.ds(HALF_LAT, row_count - WLAT)], sems.at[2])]
    copies[0].start()
    bands = row_count // WLAT
    half = HALF_LAT * WLON
    places = [(side, strip) for side in range(2) for strip in range(strips - 1)]
    for at, (side, strip) in enumerate(places):
        block = halo_ref[HALF_LAT * (1 - side) : HALF_LAT * (2 - side), strip * WLON : (strip + 1) * WLON, :]
        cells_ref[at * half : (at + 1) * half, :] = normalize(block.astype(F32).reshape(half, feature)).astype(BF16)
    keys_ref[...] = project(cells_ref[...], qkv_weight_ref, feature, 2 * feature)
    labels = labels_ref[...]
    label_columns = labels.T
    entries = []
    for at, (side, strip) in enumerate(places):
        mine = slice(at * half, (at + 1) * half)
        rows = slice(0, half) if side else slice(half, WIN)
        place = side * bands * strips + strip
        mask = excluded(label_columns[rows, place : place + 1], labels[place : place + 1])

        def both(head, mine=mine, side=side):
            pair = own_ref[mine, lanes(HEADS + head)], keys_ref[mine, lanes(head)]
            return jnp.concatenate(pair if side else pair[::-1], axis=0)

        for head in range(HEADS):
            entries.append(
                (
                    lambda mine=mine, head=head: own_ref[mine, lanes(head)],
                    lambda head=head, both=both: both(head),
                    lambda head=head, both=both: both(HEADS + head),
                    lambda mask=mask, head=head, rows=rows: bias_ref[head, rows, :] + mask,
                    storer(attended_ref, mine, head),
                )
            )
    attention(entries)
    for side, first in enumerate((0, row_count - HALF_LAT)):
        cells = (strips - 1) * half
        branch = out_project(attended_ref[side * cells : (side + 1) * cells, :], out_weight_ref)
        for row in range(HALF_LAT):
            at = side * HALF_LAT + row
            corner = corner_ref[at].astype(F32)
            middle = [branch[strip * half + row * WLON : strip * half + (row + 1) * WLON] for strip in range(strips - 1)]
            middle = inner_ref[at].astype(F32) + jnp.concatenate(middle, axis=0)
            block_ref[at] = jnp.concatenate([corner[:HALF_LON], middle, corner[HALF_LON:]], axis=0).astype(BF16)
        source = block_ref.at[pl.ds(side * HALF_LAT, HALF_LAT)]
        copies.append(pltpu.make_async_copy(source, out_ref.at[pl.ds(first, HALF_LAT)], sems.at[side]))
        copies[-1].start()
    for copy in copies:
        copy.wait()


def shards(tokens, qkv_weight, out_weight, bias_table, position_index, region_label):
    row_count, column_count, feature = tokens.shape
    bands, strips = row_count // WLAT, column_count // WLON
    whole = shape(*tokens.shape)
    inner_columns = column_count - WLON
    dma = pltpu.SemaphoreType.DMA

    label_above = moved(region_label, "lat", 1)
    ends, inner_rows, middle, columns = run(
        message_kernel,
        [
            shape(WLAT, WLON, feature),
            shape(WLAT, inner_columns, feature),
            shape(row_count - WLAT, inner_columns, feature),
            shape(row_count, WLON, feature),
        ],
        [tokens],
        flops=5 * 10**9,
    )
    ends_received = lat_exchange(ends)
    rows_received = lat_exchange(inner_rows)

    inner_cells = (strips - 1) * WIN
    inner, bias, label_own = run(
        functools.partial(inner_kernel, strips),
        [shape(inner_cells, feature), shape(HEADS, WIN, WIN, dtype=F32), shape(bands * strips, WIN, dtype=F32)],
        [middle, region_label, bias_table.T, position_index, qkv_weight, out_weight],
        scratch=[pltpu.VMEM((inner_cells, width * feature), BF16) for width in (1, 3, 1)]
        + [pltpu.VMEM((8, -(-bias_table.shape[0] // 128) * 128), F32)],
        mib=12,
        flops=2 * 10**10,
    )
    message = shape(row_count + 1, HALF_LON, feature)
    *columns_sent, labels = run(
        functools.partial(column_kernel, strips), [message, message, shape(16, WIN, dtype=F32)], [columns, label_own, label_above]
    )
    columns_received = lon_exchange(*columns_sent)

    message = shape(WLAT, HALF_LON, feature)
    corners = run(corner_message_kernel, [message, message], [ends_received, columns_sent[0]], specs=[VMEM, ANY])
    corners_received = lon_exchange(*corners)
    row_cells = (strips - 1) * WIN
    (row_qkv,) = run(
        functools.partial(rows_kernel, strips),
        [shape(row_cells, 3 * feature)],
        [inner_rows, qkv_weight, corners[0]],
        specs=[VMEM, VMEM, ANY],
        scratch=[pltpu.VMEM((row_cells, feature), BF16)],
        mib=8,
    )

    def side_scratch(between):
        windows = side_windows(bands, between)
        cells, every = windows[-1][2] + windows[-1][3], len(windows) * WIN
        sizes = ((every, 1), (cells, 1), (cells, 1), (every, 2), (cells, 1))
        return cells, every, [pltpu.VMEM((count, width * feature), BF16) for count, width in sizes]

    cells, every, scratch = side_scratch(True)
    between, label_left = run(
        functools.partial(between_kernel, strips),
        [shape(row_count - WLAT, column_count, feature), shape(16, WIN, dtype=F32)],
        [columns, *columns_received, labels, bias, qkv_weight, out_weight, inner, row_qkv],
        specs=[VMEM] * 8 + [ANY],
        scratch=scratch,
        mib=12,
    )
    cells, every, scratch = side_scratch(False)
    (corner,) = run(
        functools.partial(corner_kernel, strips),
        [shape(WLAT, WLON, feature)],
        [columns, *columns_received, *corners_received, ends_received, labels, label_left, bias, qkv_weight, out_weight],
        scratch=scratch,
        mib=12,
    )
    (out,) = run(
        functools.partial(last_kernel, strips),
        [whole],
        [inner_rows, rows_received, row_qkv, labels, bias, qkv_weight, out_weight, corner, between],
        out_specs=[HBM],
        mib=12,
        scratch=[pltpu.VMEM((row_cells, width * feature), BF16) for width in (1, 2, 1)]
        + [pltpu.VMEM((WLAT, column_count, feature), BF16), dma((3,))],
    )
    return out


def solution(mesh):
    in_specs = (P("lat", "lon", None), P(), P(), P(), P(), P("lat", "lon"))
    out_specs = P("lat", "lon", None)
    return jax.shard_map(shards, mesh=mesh, in_specs=in_specs, out_specs=out_specs, check_vma=False)
```

```python
import functools

import jax
import jax.numpy as jnp
from jax import lax
from jax.experimental import pallas as pl
from jax.experimental.pallas import tpu as pltpu
from jax.sharding import PartitionSpec as P

HEADS = 6
HEAD = 128
WLAT = 8
WLON = 16
WIN = WLAT * WLON
HALF_LAT = WLAT // 2
HALF_LON = WLON // 2
LOG2E = 1.4426950408889634
SCALE = LOG2E / HEAD**0.5
EXCLUDED = -1e30
VMEM = pl.BlockSpec(memory_space=pltpu.VMEM)
HBM = pl.BlockSpec(memory_space=pltpu.HBM)
ANY = pl.BlockSpec(memory_space=pl.ANY)
F32 = jnp.float32
BF16 = jnp.bfloat16


def moved(block, axis, distance):
    count = lax.axis_size(axis)
    route = [((i - distance) % count, i) for i in range(count)]
    return lax.ppermute(block, axis, route)


def lat_exchange(message, cut):
    if lax.axis_size("lat") == 2:
        return moved(message, "lat", 1)
    return jnp.concatenate([moved(message[:cut], "lat", -1), moved(message[cut:], "lat", 1)], axis=0)


def lon_exchange(odd_even, even_odd):
    count = lax.axis_size("lon")
    first = [(i, i ^ 1) for i in range(count)]
    second = [(i, (i + 1 if i % 2 else i - 1) % count) for i in range(count)]
    even_odd = lax.ppermute(even_odd, "lon", first)
    return lax.ppermute(odd_even, "lon", second), even_odd


def run(kernel, outs, operands, scratch=(), specs=None, out_specs=None, mib=4, flops=10**6):
    return pl.pallas_call(
        kernel,
        out_shape=outs,
        in_specs=specs or [VMEM] * len(operands),
        out_specs=out_specs or [VMEM] * len(outs),
        scratch_shapes=scratch,
        compiler_params=pltpu.CompilerParams(vmem_limit_bytes=mib * 2**20),
        cost_estimate=pl.CostEstimate(flops=flops, bytes_accessed=10**5, transcendentals=0),
    )(*operands)


def shape(*extent, dtype=BF16):
    return jax.ShapeDtypeStruct(extent, dtype)


def normalize(floats):
    floats = floats - jnp.mean(floats, axis=-1, keepdims=True)
    return floats * lax.rsqrt(jnp.mean(jnp.square(floats), axis=-1, keepdims=True) + 1e-05)


def label_rows(labels, strips):
    rows, columns = labels.shape
    labels = labels.astype(BF16)
    source = lax.broadcasted_iota(jnp.int32, (columns, WIN), 0)
    cell = lax.broadcasted_iota(jnp.int32, (columns, WIN), 1)
    at_row = lax.broadcasted_iota(jnp.int32, (rows, WIN), 0) % WLAT == lax.broadcasted_iota(jnp.int32, (rows, WIN), 1) // WLON
    place = lax.broadcasted_iota(jnp.int32, (rows // WLAT * strips, WIN), 0)
    result = jnp.zeros((rows // WLAT * strips, WIN), F32)
    for strip in range(strips):
        spread = jnp.dot(labels, (source == strip * WLON + cell % WLON).astype(BF16), preferred_element_type=F32)
        spread = jnp.where(at_row, spread, 0.0)
        for band in range(rows // WLAT):
            row = jnp.sum(spread[band * WLAT : (band + 1) * WLAT], axis=0, keepdims=True)
            result = jnp.where(place == band * strips + strip, row, result)
    return result


def label_kernel(strips, label_ref, rows_ref):
    rows_ref[...] = label_rows(label_ref[...], strips)


def label_message(rows, feature):
    rows = jnp.concatenate([rows, jnp.zeros((HALF_LON - rows.shape[0], WIN), F32)], axis=0) if rows.shape[0] < HALF_LON else rows
    return jnp.concatenate([rows, jnp.zeros((HALF_LON, feature - WIN), F32)], axis=1).astype(BF16)


def message_kernel(tokens_ref, rows_ref, ends_ref, inner_ref, middle_ref, columns_ref):
    row_count, _, feature = tokens_ref.shape
    for row in range(row_count):
        floats = tokens_ref[row].astype(F32)
        columns_ref[row] = jnp.concatenate([floats[:HALF_LON], floats[-HALF_LON:]], axis=0).astype(BF16)
        inner = floats[HALF_LON:-HALF_LON].astype(BF16)
        if HALF_LAT <= row < row_count - HALF_LAT:
            middle_ref[row - HALF_LAT] = inner
        else:
            at = row if row < HALF_LAT else row - row_count + WLAT
            ends_ref[2 * at] = floats[:HALF_LON].astype(BF16)
            ends_ref[2 * at + 1] = floats[-HALF_LON:].astype(BF16)
            inner_ref[at] = inner
    ends_ref[2 * WLAT] = label_message(rows_ref[...], feature)


def column_kernel(columns_ref, rows_ref, even_odd_ref, odd_even_ref):
    row_count, _, feature = columns_ref.shape
    odd = lax.axis_index("lon") % 2 == 1
    for row in range(row_count):
        floats = columns_ref[row].astype(F32)
        left, right = floats[:HALF_LON], floats[HALF_LON:]
        even_odd_ref[row] = jnp.where(odd, left, right).astype(BF16)
        odd_even_ref[row] = jnp.where(odd, right, left).astype(BF16)
    message = label_message(rows_ref[...], feature)
    even_odd_ref[row_count] = message
    odd_even_ref[row_count] = message


def corner_message_kernel(strips, ends_ref, rows_ref, after_ref, even_odd_ref, odd_even_ref, labels_ref):
    odd = lax.axis_index("lon") % 2 == 1
    for row in range(WLAT):
        left, right = ends_ref[2 * row].astype(F32), ends_ref[2 * row + 1].astype(F32)
        even_odd_ref[row] = jnp.where(odd, left, right).astype(BF16)
        odd_even_ref[row] = jnp.where(odd, right, left).astype(BF16)
    own = rows_ref[...]
    above = ends_ref[2 * WLAT].astype(F32)[own.shape[0] - strips : own.shape[0], :WIN]
    labels_ref[...] = jnp.concatenate([above, own, jnp.zeros((16 - strips - own.shape[0], WIN), F32)], axis=0)
    message = label_message(above, ends_ref.shape[-1])
    even_odd_ref[WLAT] = message
    odd_even_ref[WLAT] = message


def halo_row(row, row_count):
    return row + HALF_LAT if row < HALF_LAT else row - row_count - HALF_LAT


def look_up(table_ref, index_ref, out_ref):
    entries = table_ref.shape[1]
    for row in range(0, WIN, 8):
        index = index_ref[row : row + 8, :]
        low, high = index & 127, index >> 7
        for head in range(HEADS):
            value = jnp.zeros((8, WIN), F32)
            for part in range(-(-entries // 128)):
                source = jnp.broadcast_to(table_ref[head : head + 1, part * 128 : part * 128 + 128], (8, 128))
                value = jnp.where(high == part, jnp.take_along_axis(source, low, axis=1), value)
            out_ref[head, row : row + 8, :] = value * LOG2E


def excluded(columns, row):
    return jnp.where(columns == row, 0.0, EXCLUDED)


def attention(entries):
    scores = []
    for queries, keys, _, bias, _ in entries:
        product = lax.dot_general(queries(), keys(), (((1,), (1,)), ((), ())), preferred_element_type=F32)
        scores.append(product * SCALE + bias())
    numerators = [jnp.exp2(score - jnp.max(score, axis=-1, keepdims=True)) for score in scores]
    for (_, _, values, _, store), numerator in zip(entries, numerators):
        total = jnp.sum(numerator, axis=-1, keepdims=True)
        summed = jnp.dot(numerator.astype(BF16), values(), preferred_element_type=F32)
        store((summed * (1.0 / total)).astype(BF16))


def project(source, weight_ref, first, count):
    return jnp.dot(source, weight_ref[:, first : first + count], preferred_element_type=F32).astype(BF16)


def out_project(attended, weight_ref):
    return jnp.dot(attended, weight_ref[...], preferred_element_type=F32).astype(BF16).astype(F32)


def lanes(head):
    return slice(head * HEAD, (head + 1) * HEAD)


def storer(ref, rows, head):
    def store(value):
        ref[rows, lanes(head)] = value

    return store


def inner_kernel(strips, middle_ref, rows_ref, table_ref, index_ref, qkv_weight_ref, out_weight_ref,
                 after_ref, out_ref, bias_ref, cells_ref, qkv_ref, attended_ref, wide_ref):
    feature = middle_ref.shape[-1]
    floats = []
    for strip in range(strips - 1):
        window = middle_ref[:, strip * WLON : (strip + 1) * WLON, :].astype(F32).reshape(WIN, feature)
        floats.append(window)
        cells_ref[strip * WIN : (strip + 1) * WIN, :] = normalize(window).astype(BF16)
    wide_ref[...] = jnp.zeros(wide_ref.shape, F32)
    wide_ref[: table_ref.shape[0], : table_ref.shape[1]] = table_ref[...]
    qkv_ref[...] = project(cells_ref[...], qkv_weight_ref, 0, 3 * feature)
    look_up(wide_ref, index_ref, bias_ref)
    labels = rows_ref[...]
    label_columns = labels.T
    entries = []
    for strip in range(strips - 1):
        mine = slice(strip * WIN, (strip + 1) * WIN)
        mask = excluded(label_columns[:, strip : strip + 1], labels[strip : strip + 1])
        for head in range(HEADS):
            entries.append(
                (
                    lambda mine=mine, head=head: qkv_ref[mine, lanes(head)],
                    lambda mine=mine, head=head: qkv_ref[mine, lanes(HEADS + head)],
                    lambda mine=mine, head=head: qkv_ref[mine, lanes(2 * HEADS + head)],
                    lambda mask=mask, head=head: bias_ref[head] + mask,
                    storer(attended_ref, mine, head),
                )
            )
    attention(entries)
    branch = out_project(attended_ref[...], out_weight_ref)
    for strip in range(strips - 1):
        mine = slice(strip * WIN, (strip + 1) * WIN)
        out_ref[mine, :] = (floats[strip] + branch[mine]).astype(BF16)


def rows_kernel(strips, inner_ref, qkv_weight_ref, after_ref, out_ref, cells_ref):
    feature = inner_ref.shape[-1]
    half = HALF_LAT * WLON
    for side in range(2):
        for strip in range(strips - 1):
            block = inner_ref[side * HALF_LAT : (side + 1) * HALF_LAT, strip * WLON : (strip + 1) * WLON, :]
            start = (side * (strips - 1) + strip) * half
            cells_ref[start : start + half, :] = normalize(block.astype(F32).reshape(half, feature)).astype(BF16)
    out_ref[...] = project(cells_ref[...], qkv_weight_ref, 0, 3 * feature)


def side_windows(bands, between):
    windows, start = [], 0
    for band in range(bands + 1):
        if (0 < band < bands) == between:
            count = HALF_LON * (WLAT if between else HALF_LAT)
            for side in range(2):
                windows.append((band, side, start, count))
                start += count
    return windows


def side_blocks(windows, bands, strips, own_of, halo_of, left_labels, labels, bias_ref, qkv_weight_ref, out_weight_ref,
                cells_ref, own_ref, queries_ref, keys_ref, attended_ref):
    feature = cells_ref.shape[-1]
    label_columns = left_labels.T, labels.T
    tokens_of = {}
    for at, (band, side, start, count) in enumerate(windows):
        own = [own_of(row, side) for row in range(band * WLAT, (band + 1) * WLAT)]
        halo = [halo_of(row, side) for row in range(band * WLAT, (band + 1) * WLAT)]
        mine = slice(HALF_LAT if band == 0 else 0, HALF_LAT if band == bands else WLAT)
        tokens_of[band, side] = own[mine]
        own = normalize(jnp.stack(own))
        halo = normalize(jnp.stack(halo))
        window = jnp.concatenate([own, halo] if side else [halo, own], axis=1)
        cells_ref[at * WIN : (at + 1) * WIN, :] = window.reshape(WIN, feature).astype(BF16)
        own_ref[start : start + count, :] = own[mine].reshape(count, feature).astype(BF16)
    queries_ref[...] = project(own_ref[...], qkv_weight_ref, 0, feature)
    keys_ref[...] = project(cells_ref[...], qkv_weight_ref, feature, 2 * feature)

    def own_rows(array, band, side):
        array = array.reshape(WLAT, WLON, WIN)
        array = array[HALF_LAT if band == 0 else 0 : HALF_LAT if band == bands else WLAT]
        array = array[:, :HALF_LON] if side else array[:, HALF_LON:]
        return array.reshape(-1, WIN)

    entries = []
    for at, (band, side, start, count) in enumerate(windows):
        mine, whole = slice(start, start + count), slice(at * WIN, (at + 1) * WIN)
        place = band * strips + strips - 1
        row = (labels if side else left_labels)[place : place + 1]
        mask = own_rows(excluded(label_columns[side][:, place : place + 1], row), band, side)
        for head in range(HEADS):
            entries.append(
                (
                    lambda mine=mine, head=head: queries_ref[mine, lanes(head)],
                    lambda whole=whole, head=head: keys_ref[whole, lanes(head)],
                    lambda whole=whole, head=head: keys_ref[whole, lanes(HEADS + head)],
                    lambda mask=mask, head=head, band=band, side=side: own_rows(bias_ref[head], band, side) + mask,
                    storer(attended_ref, mine, head),
                )
            )
    attention(entries)
    branch = out_project(attended_ref[...], out_weight_ref)
    blocks = {}
    for band, side, start, count in windows:
        for row, own in enumerate(tokens_of[band, side]):
            at = start + row * HALF_LON
            blocks[band, side, row] = own + branch[at : at + HALF_LON]
    return blocks


def swapped(odd_even_ref, even_odd_ref):
    odd = lax.axis_index("lon") % 2 == 1

    def row_of(row, side):
        first, second = even_odd_ref[row].astype(F32), odd_even_ref[row].astype(F32)
        return jnp.where(odd, second, first) if side else jnp.where(odd, first, second)

    return row_of


def half_of(floats, side):
    return floats[HALF_LON:] if side else floats[:HALF_LON]


def left_labels_of(above, own):
    return jnp.concatenate([above, own, jnp.zeros((16 - above.shape[0] - own.shape[0], WIN), F32)], axis=0)


def between_kernel(strips, columns_ref, odd_even_ref, even_odd_ref, labels_ref, bias_ref, qkv_weight_ref, out_weight_ref, inner_ref,
                   after_ref, out_ref, *scratch):
    row_count = columns_ref.shape[0]
    received = swapped(odd_even_ref, even_odd_ref)
    left_labels = left_labels_of(jnp.zeros((strips, WIN), F32), received(row_count, 0)[:, :WIN])
    blocks = side_blocks(
        side_windows(row_count // WLAT, True), row_count // WLAT, strips,
        lambda row, side: half_of(columns_ref[row - HALF_LAT].astype(F32), side),
        lambda row, side: received(row - HALF_LAT, side),
        left_labels, labels_ref[...], bias_ref, qkv_weight_ref, out_weight_ref, *scratch,
    )
    for row in range(WLAT):
        middle = [inner_ref[strip * WIN + row * WLON : strip * WIN + (row + 1) * WLON, :].astype(F32) for strip in range(strips - 1)]
        out_ref[row] = jnp.concatenate([blocks[1, 0, row]] + middle + [blocks[1, 1, row]], axis=0).astype(BF16)


def corner_kernel(strips, columns_ref, odd_even_ref, even_odd_ref, corner_odd_even_ref, corner_even_odd_ref, ends_ref, labels_ref,
                  bias_ref, qkv_weight_ref, out_weight_ref, corner_ref, *scratch):
    row_count = columns_ref.shape[0]
    bands = row_count // WLAT
    received = swapped(odd_even_ref, even_odd_ref)
    received_corner = swapped(corner_odd_even_ref, corner_even_odd_ref)
    left_labels = left_labels_of(received_corner(WLAT, 0)[:strips, :WIN], received(row_count, 0)[:, :WIN])

    def inside(row):
        return HALF_LAT <= row < row_count + HALF_LAT

    def own_of(row, side):
        if inside(row):
            return half_of(columns_ref[row - HALF_LAT].astype(F32), side)
        return ends_ref[2 * halo_row(row, row_count) + side].astype(F32)

    def halo_of(row, side):
        return received(row - HALF_LAT, side) if inside(row) else received_corner(halo_row(row, row_count), side)

    blocks = side_blocks(
        side_windows(bands, False), bands, strips, own_of, halo_of,
        left_labels, labels_ref[...], bias_ref, qkv_weight_ref, out_weight_ref, *scratch,
    )
    for band, first in ((0, 0), (bands, HALF_LAT)):
        for row in range(HALF_LAT):
            corner_ref[first + row] = jnp.concatenate([blocks[band, 0, row], blocks[band, 1, row]], axis=0).astype(BF16)


def last_kernel(strips, inner_ref, halo_ref, own_ref, labels_ref, bias_ref, qkv_weight_ref, out_weight_ref, corner_ref, between_ref,
                out_ref, cells_ref, keys_ref, attended_ref, block_ref, sems):
    row_count, column_count, feature = out_ref.shape
    copies = [pltpu.make_async_copy(between_ref, out_ref.at[pl.ds(HALF_LAT, row_count - WLAT)], sems.at[WLAT])]
    copies[0].start()
    bands = row_count // WLAT
    half = HALF_LAT * WLON
    places = [(side, strip) for side in range(2) for strip in range(strips - 1)]
    for at, (side, strip) in enumerate(places):
        block = halo_ref[HALF_LAT * (1 - side) : HALF_LAT * (2 - side), strip * WLON : (strip + 1) * WLON, :]
        cells_ref[at * half : (at + 1) * half, :] = normalize(block.astype(F32).reshape(half, feature)).astype(BF16)
    keys_ref[...] = project(cells_ref[...], qkv_weight_ref, feature, 2 * feature)
    labels = labels_ref[...]
    label_columns = labels.T
    entries = []
    for at, (side, strip) in enumerate(places):
        mine = slice(at * half, (at + 1) * half)
        rows = slice(0, half) if side else slice(half, WIN)
        place = side * bands * strips + strip
        mask = excluded(label_columns[rows, place : place + 1], labels[place : place + 1])

        def both(head, mine=mine, side=side):
            pair = own_ref[mine, lanes(HEADS + head)], keys_ref[mine, lanes(head)]
            return jnp.concatenate(pair if side else pair[::-1], axis=0)

        for head in range(HEADS):
            entries.append(
                (
                    lambda mine=mine, head=head: own_ref[mine, lanes(head)],
                    lambda head=head, both=both: both(head),
                    lambda head=head, both=both: both(HEADS + head),
                    lambda mask=mask, head=head, rows=rows: bias_ref[head, rows, :] + mask,
                    storer(attended_ref, mine, head),
                )
            )
    attention(entries)
    for side, first in enumerate((0, row_count - HALF_LAT)):
        cells = (strips - 1) * half
        branch = out_project(attended_ref[side * cells : (side + 1) * cells, :], out_weight_ref)
        for row in range(HALF_LAT):
            at = side * HALF_LAT + row
            corner = corner_ref[at].astype(F32)
            middle = [branch[strip * half + row * WLON : strip * half + (row + 1) * WLON] for strip in range(strips - 1)]
            middle = inner_ref[at].astype(F32) + jnp.concatenate(middle, axis=0)
            block_ref[at] = jnp.concatenate([corner[:HALF_LON], middle, corner[HALF_LON:]], axis=0).astype(BF16)
            copies.append(pltpu.make_async_copy(block_ref.at[at], out_ref.at[first + row], sems.at[at]))
            copies[-1].start()
    for copy in copies:
        copy.wait()


def shards(tokens, qkv_weight, out_weight, bias_table, position_index, region_label):
    row_count, column_count, feature = tokens.shape
    bands, strips = row_count // WLAT, column_count // WLON
    whole = shape(*tokens.shape)
    inner_columns = column_count - WLON
    dma = pltpu.SemaphoreType.DMA

    (label_own,) = run(
        functools.partial(label_kernel, strips), [shape(bands * strips, WIN, dtype=F32)], [region_label], flops=5 * 10**9
    )
    ends, inner_rows, middle, columns = run(
        message_kernel,
        [
            shape(2 * WLAT + 1, HALF_LON, feature),
            shape(WLAT, inner_columns, feature),
            shape(row_count - WLAT, inner_columns, feature),
            shape(row_count, WLON, feature),
        ],
        [tokens, label_own],
        flops=5 * 10**9,
    )
    ends_received = lat_exchange(ends, 2 * HALF_LAT)
    rows_received = lat_exchange(inner_rows, HALF_LAT)
    message = shape(row_count + 1, HALF_LON, feature)
    columns_sent = run(column_kernel, [message, message], [columns, label_own], flops=2 * 10**10)
    columns_received = lon_exchange(*columns_sent[::-1])

    inner_cells = (strips - 1) * WIN
    inner, bias = run(
        functools.partial(inner_kernel, strips),
        [shape(inner_cells, feature), shape(HEADS, WIN, WIN, dtype=F32)],
        [middle, label_own, bias_table.T, position_index, qkv_weight, out_weight, columns_sent[0]],
        specs=[VMEM] * 6 + [ANY],
        scratch=[pltpu.VMEM((inner_cells, width * feature), BF16) for width in (1, 3, 1)]
        + [pltpu.VMEM((8, -(-bias_table.shape[0] // 128) * 128), F32)],
        mib=12,
        flops=5 * 10**9,
    )
    message = shape(WLAT + 1, HALF_LON, feature)
    *corners, labels = run(
        functools.partial(corner_message_kernel, strips),
        [message, message, shape(16, WIN, dtype=F32)],
        [ends_received, label_own, inner],
        specs=[VMEM, VMEM, ANY],
    )
    corners_received = lon_exchange(*corners[::-1])
    row_cells = (strips - 1) * WIN
    (row_qkv,) = run(
        functools.partial(rows_kernel, strips),
        [shape(row_cells, 3 * feature)],
        [inner_rows, qkv_weight, corners[0]],
        specs=[VMEM, VMEM, ANY],
        scratch=[pltpu.VMEM((row_cells, feature), BF16)],
        mib=8,
    )

    def side_scratch(between):
        windows = side_windows(bands, between)
        cells, every = windows[-1][2] + windows[-1][3], len(windows) * WIN
        sizes = ((every, 1), (cells, 1), (cells, 1), (every, 2), (cells, 1))
        return cells, every, [pltpu.VMEM((count, width * feature), BF16) for count, width in sizes]

    cells, every, scratch = side_scratch(True)
    (between,) = run(
        functools.partial(between_kernel, strips),
        [shape(row_count - WLAT, column_count, feature)],
        [columns, *columns_received, labels, bias, qkv_weight, out_weight, inner, row_qkv],
        specs=[VMEM] * 8 + [ANY],
        scratch=scratch,
        mib=12,
    )
    cells, every, scratch = side_scratch(False)
    (corner,) = run(
        functools.partial(corner_kernel, strips),
        [shape(WLAT, WLON, feature)],
        [columns, *columns_received, *corners_received, ends_received, labels, bias, qkv_weight, out_weight],
        scratch=scratch,
        mib=12,
    )
    (out,) = run(
        functools.partial(last_kernel, strips),
        [whole],
        [inner_rows, rows_received, row_qkv, labels, bias, qkv_weight, out_weight, corner, between],
        out_specs=[HBM],
        mib=12,
        scratch=[pltpu.VMEM((row_cells, width * feature), BF16) for width in (1, 2, 1)]
        + [pltpu.VMEM((WLAT, column_count, feature), BF16), dma((WLAT + 1,))],
    )
    return out


def solution(mesh):
    in_specs = (P("lat", "lon", None), P(), P(), P(), P(), P("lat", "lon"))
    out_specs = P("lat", "lon", None)
    return jax.shard_map(shards, mesh=mesh, in_specs=in_specs, out_specs=out_specs, check_vma=False)
```

```python
import functools

import jax
import jax.numpy as jnp
from jax import lax
from jax.experimental import pallas as pl
from jax.experimental.pallas import tpu as pltpu
from jax.sharding import PartitionSpec as P

HEADS = 6
HEAD = 128
WLAT = 8
WLON = 16
WIN = WLAT * WLON
HALF_LAT = WLAT // 2
HALF_LON = WLON // 2
LOG2E = 1.4426950408889634
SCALE = LOG2E / HEAD**0.5
EXCLUDED = -1e30
VMEM = pl.BlockSpec(memory_space=pltpu.VMEM)
HBM = pl.BlockSpec(memory_space=pltpu.HBM)
ANY = pl.BlockSpec(memory_space=pl.ANY)
F32 = jnp.float32
BF16 = jnp.bfloat16


def moved(block, axis, distance):
    count = lax.axis_size(axis)
    route = [((i - distance) % count, i) for i in range(count)]
    return lax.ppermute(block, axis, route)


def lat_exchange(message, cut):
    if lax.axis_size("lat") == 2:
        return moved(message, "lat", 1)
    return jnp.concatenate([moved(message[:cut], "lat", -1), moved(message[cut:], "lat", 1)], axis=0)


def lon_exchange(odd_even, even_odd):
    count = lax.axis_size("lon")
    first = [(i, i ^ 1) for i in range(count)]
    second = [(i, (i + 1 if i % 2 else i - 1) % count) for i in range(count)]
    even_odd = lax.ppermute(even_odd, "lon", first)
    return lax.ppermute(odd_even, "lon", second), even_odd


def run(kernel, outs, operands, scratch=(), specs=None, out_specs=None, mib=4, flops=10**6):
    return pl.pallas_call(
        kernel,
        out_shape=outs,
        in_specs=specs or [VMEM] * len(operands),
        out_specs=out_specs or [VMEM] * len(outs),
        scratch_shapes=scratch,
        compiler_params=pltpu.CompilerParams(vmem_limit_bytes=mib * 2**20),
        cost_estimate=pl.CostEstimate(flops=flops, bytes_accessed=10**5, transcendentals=0),
    )(*operands)


def shape(*extent, dtype=BF16):
    return jax.ShapeDtypeStruct(extent, dtype)


def normalize(floats):
    floats = floats - jnp.mean(floats, axis=-1, keepdims=True)
    return floats * lax.rsqrt(jnp.mean(jnp.square(floats), axis=-1, keepdims=True) + 1e-05)


def label_rows(labels, strips):
    rows, columns = labels.shape
    labels = labels.astype(BF16)
    source = lax.broadcasted_iota(jnp.int32, (columns, WIN), 0)
    cell = lax.broadcasted_iota(jnp.int32, (columns, WIN), 1)
    at_row = lax.broadcasted_iota(jnp.int32, (rows, WIN), 0) % WLAT == lax.broadcasted_iota(jnp.int32, (rows, WIN), 1) // WLON
    place = lax.broadcasted_iota(jnp.int32, (rows // WLAT * strips, WIN), 0)
    result = jnp.zeros((rows // WLAT * strips, WIN), F32)
    for strip in range(strips):
        spread = jnp.dot(labels, (source == strip * WLON + cell % WLON).astype(BF16), preferred_element_type=F32)
        spread = jnp.where(at_row, spread, 0.0)
        for band in range(rows // WLAT):
            row = jnp.sum(spread[band * WLAT : (band + 1) * WLAT], axis=0, keepdims=True)
            result = jnp.where(place == band * strips + strip, row, result)
    return result


def label_kernel(strips, label_ref, rows_ref):
    rows_ref[...] = label_rows(label_ref[...], strips)


def put_cells(message_ref, row, cells):
    groups = cells.shape[1] // WIN
    for group in range(groups):
        message_ref[row * groups + group] = cells[:, group * WIN : (group + 1) * WIN].astype(BF16)


def cells_of(message_ref, row):
    groups = HEADS * HEAD // WIN
    return jnp.concatenate([message_ref[row * groups + group].astype(F32) for group in range(groups)], axis=1)


def put_labels(message_ref, rows):
    if rows.shape[0] < HALF_LON:
        rows = jnp.concatenate([rows, jnp.zeros((HALF_LON - rows.shape[0], WIN), F32)], axis=0)
    message_ref[message_ref.shape[0] - 1] = rows.astype(BF16)


def labels_of(message_ref):
    return message_ref[message_ref.shape[0] - 1].astype(F32)


def message_kernel(tokens_ref, rows_ref, ends_ref, inner_ref, middle_ref, columns_ref):
    row_count, _, feature = tokens_ref.shape
    for row in range(row_count):
        floats = tokens_ref[row].astype(F32)
        columns_ref[row] = jnp.concatenate([floats[:HALF_LON], floats[-HALF_LON:]], axis=0).astype(BF16)
        inner = floats[HALF_LON:-HALF_LON].astype(BF16)
        if HALF_LAT <= row < row_count - HALF_LAT:
            middle_ref[row - HALF_LAT] = inner
        else:
            at = row if row < HALF_LAT else row - row_count + WLAT
            put_cells(ends_ref, 2 * at, floats[:HALF_LON])
            put_cells(ends_ref, 2 * at + 1, floats[-HALF_LON:])
            inner_ref[at] = inner
    put_labels(ends_ref, rows_ref[...])


def column_kernel(columns_ref, rows_ref, even_odd_ref, odd_even_ref):
    odd = lax.axis_index("lon") % 2 == 1
    for row in range(columns_ref.shape[0]):
        floats = columns_ref[row].astype(F32)
        left, right = floats[:HALF_LON], floats[HALF_LON:]
        put_cells(even_odd_ref, row, jnp.where(odd, left, right))
        put_cells(odd_even_ref, row, jnp.where(odd, right, left))
    put_labels(even_odd_ref, rows_ref[...])
    put_labels(odd_even_ref, rows_ref[...])


def corner_message_kernel(strips, ends_ref, rows_ref, after_ref, even_odd_ref, odd_even_ref, labels_ref):
    odd = lax.axis_index("lon") % 2 == 1
    for row in range(WLAT):
        left, right = cells_of(ends_ref, 2 * row), cells_of(ends_ref, 2 * row + 1)
        put_cells(even_odd_ref, row, jnp.where(odd, left, right))
        put_cells(odd_even_ref, row, jnp.where(odd, right, left))
    own = rows_ref[...]
    above = labels_of(ends_ref)[own.shape[0] - strips : own.shape[0]]
    labels_ref[...] = jnp.concatenate([above, own, jnp.zeros((16 - strips - own.shape[0], WIN), F32)], axis=0)
    put_labels(even_odd_ref, above)
    put_labels(odd_even_ref, above)


def halo_row(row, row_count):
    return row + HALF_LAT if row < HALF_LAT else row - row_count - HALF_LAT


def look_up(table_ref, index_ref, out_ref):
    entries = table_ref.shape[1]
    for row in range(0, WIN, 8):
        index = index_ref[row : row + 8, :]
        low, high = index & 127, index >> 7
        for head in range(HEADS):
            value = jnp.zeros((8, WIN), F32)
            for part in range(-(-entries // 128)):
                source = jnp.broadcast_to(table_ref[head : head + 1, part * 128 : part * 128 + 128], (8, 128))
                value = jnp.where(high == part, jnp.take_along_axis(source, low, axis=1), value)
            out_ref[head, row : row + 8, :] = value * LOG2E


def excluded(columns, row):
    return jnp.where(columns == row, 0.0, EXCLUDED)


def attention(entries):
    scores = []
    for queries, keys, _, bias, _ in entries:
        product = lax.dot_general(queries(), keys(), (((1,), (1,)), ((), ())), preferred_element_type=F32)
        scores.append(product * SCALE + bias())
    numerators = [jnp.exp2(score - jnp.max(score, axis=-1, keepdims=True)) for score in scores]
    for (_, _, values, _, store), numerator in zip(entries, numerators):
        total = jnp.sum(numerator, axis=-1, keepdims=True)
        summed = jnp.dot(numerator.astype(BF16), values(), preferred_element_type=F32)
        store((summed * (1.0 / total)).astype(BF16))


def project(source, weight_ref, first, count):
    return jnp.dot(source, weight_ref[:, first : first + count], preferred_element_type=F32).astype(BF16)


def out_project(attended, weight_ref):
    return jnp.dot(attended, weight_ref[...], preferred_element_type=F32).astype(BF16).astype(F32)


def lanes(head):
    return slice(head * HEAD, (head + 1) * HEAD)


def storer(ref, rows, head):
    def store(value):
        ref[rows, lanes(head)] = value

    return store


def inner_kernel(strips, middle_ref, rows_ref, table_ref, index_ref, qkv_weight_ref, out_weight_ref,
                 after_ref, out_ref, bias_ref, cells_ref, qkv_ref, attended_ref, wide_ref):
    feature = middle_ref.shape[-1]
    floats = []
    for strip in range(strips - 1):
        window = middle_ref[:, strip * WLON : (strip + 1) * WLON, :].astype(F32).reshape(WIN, feature)
        floats.append(window)
        cells_ref[strip * WIN : (strip + 1) * WIN, :] = normalize(window).astype(BF16)
    wide_ref[...] = jnp.zeros(wide_ref.shape, F32)
    wide_ref[: table_ref.shape[0], : table_ref.shape[1]] = table_ref[...]
    qkv_ref[...] = project(cells_ref[...], qkv_weight_ref, 0, 3 * feature)
    look_up(wide_ref, index_ref, bias_ref)
    labels = rows_ref[...]
    label_columns = labels.T
    entries = []
    for strip in range(strips - 1):
        mine = slice(strip * WIN, (strip + 1) * WIN)
        mask = excluded(label_columns[:, strip : strip + 1], labels[strip : strip + 1])
        for head in range(HEADS):
            entries.append(
                (
                    lambda mine=mine, head=head: qkv_ref[mine, lanes(head)],
                    lambda mine=mine, head=head: qkv_ref[mine, lanes(HEADS + head)],
                    lambda mine=mine, head=head: qkv_ref[mine, lanes(2 * HEADS + head)],
                    lambda mask=mask, head=head: bias_ref[head] + mask,
                    storer(attended_ref, mine, head),
                )
            )
    attention(entries)
    branch = out_project(attended_ref[...], out_weight_ref)
    for strip in range(strips - 1):
        mine = slice(strip * WIN, (strip + 1) * WIN)
        out_ref[mine, :] = (floats[strip] + branch[mine]).astype(BF16)


def rows_kernel(strips, inner_ref, qkv_weight_ref, after_ref, out_ref, cells_ref):
    feature = inner_ref.shape[-1]
    half = HALF_LAT * WLON
    for side in range(2):
        for strip in range(strips - 1):
            block = inner_ref[side * HALF_LAT : (side + 1) * HALF_LAT, strip * WLON : (strip + 1) * WLON, :]
            start = (side * (strips - 1) + strip) * half
            cells_ref[start : start + half, :] = normalize(block.astype(F32).reshape(half, feature)).astype(BF16)
    out_ref[...] = project(cells_ref[...], qkv_weight_ref, 0, 3 * feature)


def side_windows(bands, between):
    windows, start = [], 0
    for band in range(bands + 1):
        if (0 < band < bands) == between:
            count = HALF_LON * (WLAT if between else HALF_LAT)
            for side in range(2):
                windows.append((band, side, start, count))
                start += count
    return windows


def side_blocks(windows, bands, strips, own_of, halo_of, left_labels, labels, bias_ref, qkv_weight_ref, out_weight_ref,
                cells_ref, own_ref, queries_ref, keys_ref, attended_ref):
    feature = cells_ref.shape[-1]
    label_columns = left_labels.T, labels.T
    tokens_of = {}
    for at, (band, side, start, count) in enumerate(windows):
        own = [own_of(row, side) for row in range(band * WLAT, (band + 1) * WLAT)]
        halo = [halo_of(row, side) for row in range(band * WLAT, (band + 1) * WLAT)]
        mine = slice(HALF_LAT if band == 0 else 0, HALF_LAT if band == bands else WLAT)
        tokens_of[band, side] = own[mine]
        own = normalize(jnp.stack(own))
        halo = normalize(jnp.stack(halo))
        window = jnp.concatenate([own, halo] if side else [halo, own], axis=1)
        cells_ref[at * WIN : (at + 1) * WIN, :] = window.reshape(WIN, feature).astype(BF16)
        own_ref[start : start + count, :] = own[mine].reshape(count, feature).astype(BF16)
    queries_ref[...] = project(own_ref[...], qkv_weight_ref, 0, feature)
    keys_ref[...] = project(cells_ref[...], qkv_weight_ref, feature, 2 * feature)

    def own_rows(array, band, side):
        array = array.reshape(WLAT, WLON, WIN)
        array = array[HALF_LAT if band == 0 else 0 : HALF_LAT if band == bands else WLAT]
        array = array[:, :HALF_LON] if side else array[:, HALF_LON:]
        return array.reshape(-1, WIN)

    entries = []
    for at, (band, side, start, count) in enumerate(windows):
        mine, whole = slice(start, start + count), slice(at * WIN, (at + 1) * WIN)
        place = band * strips + strips - 1
        row = (labels if side else left_labels)[place : place + 1]
        mask = own_rows(excluded(label_columns[side][:, place : place + 1], row), band, side)
        for head in range(HEADS):
            entries.append(
                (
                    lambda mine=mine, head=head: queries_ref[mine, lanes(head)],
                    lambda whole=whole, head=head: keys_ref[whole, lanes(head)],
                    lambda whole=whole, head=head: keys_ref[whole, lanes(HEADS + head)],
                    lambda mask=mask, head=head, band=band, side=side: own_rows(bias_ref[head], band, side) + mask,
                    storer(attended_ref, mine, head),
                )
            )
    attention(entries)
    branch = out_project(attended_ref[...], out_weight_ref)
    blocks = {}
    for band, side, start, count in windows:
        for row, own in enumerate(tokens_of[band, side]):
            at = start + row * HALF_LON
            blocks[band, side, row] = own + branch[at : at + HALF_LON]
    return blocks


def swapped(odd_even_ref, even_odd_ref):
    odd = lax.axis_index("lon") % 2 == 1

    def row_of(row, side):
        first, second = cells_of(even_odd_ref, row), cells_of(odd_even_ref, row)
        return jnp.where(odd, second, first) if side else jnp.where(odd, first, second)

    return row_of, jnp.where(odd, labels_of(even_odd_ref), labels_of(odd_even_ref))


def half_of(floats, side):
    return floats[HALF_LON:] if side else floats[:HALF_LON]


def left_labels_of(above, own):
    return jnp.concatenate([above, own, jnp.zeros((16 - above.shape[0] - own.shape[0], WIN), F32)], axis=0)


def between_kernel(strips, columns_ref, odd_even_ref, even_odd_ref, labels_ref, bias_ref, qkv_weight_ref, out_weight_ref, inner_ref,
                   after_ref, out_ref, *scratch):
    row_count = columns_ref.shape[0]
    received, own_labels = swapped(odd_even_ref, even_odd_ref)
    left_labels = left_labels_of(jnp.zeros((strips, WIN), F32), own_labels)
    blocks = side_blocks(
        side_windows(row_count // WLAT, True), row_count // WLAT, strips,
        lambda row, side: half_of(columns_ref[row - HALF_LAT].astype(F32), side),
        lambda row, side: received(row - HALF_LAT, side),
        left_labels, labels_ref[...], bias_ref, qkv_weight_ref, out_weight_ref, *scratch,
    )
    for row in range(WLAT):
        middle = [inner_ref[strip * WIN + row * WLON : strip * WIN + (row + 1) * WLON, :].astype(F32) for strip in range(strips - 1)]
        out_ref[row] = jnp.concatenate([blocks[1, 0, row]] + middle + [blocks[1, 1, row]], axis=0).astype(BF16)


def corner_kernel(strips, columns_ref, odd_even_ref, even_odd_ref, corner_odd_even_ref, corner_even_odd_ref, ends_ref, labels_ref,
                  bias_ref, qkv_weight_ref, out_weight_ref, corner_ref, *scratch):
    row_count = columns_ref.shape[0]
    bands = row_count // WLAT
    received, own_labels = swapped(odd_even_ref, even_odd_ref)
    received_corner, above_labels = swapped(corner_odd_even_ref, corner_even_odd_ref)
    left_labels = left_labels_of(above_labels[:strips], own_labels)

    def inside(row):
        return HALF_LAT <= row < row_count + HALF_LAT

    def own_of(row, side):
        if inside(row):
            return half_of(columns_ref[row - HALF_LAT].astype(F32), side)
        return cells_of(ends_ref, 2 * halo_row(row, row_count) + side)

    def halo_of(row, side):
        return received(row - HALF_LAT, side) if inside(row) else received_corner(halo_row(row, row_count), side)

    blocks = side_blocks(
        side_windows(bands, False), bands, strips, own_of, halo_of,
        left_labels, labels_ref[...], bias_ref, qkv_weight_ref, out_weight_ref, *scratch,
    )
    for band, first in ((0, 0), (bands, HALF_LAT)):
        for row in range(HALF_LAT):
            corner_ref[first + row] = jnp.concatenate([blocks[band, 0, row], blocks[band, 1, row]], axis=0).astype(BF16)


def last_kernel(strips, inner_ref, halo_ref, own_ref, labels_ref, bias_ref, qkv_weight_ref, out_weight_ref, corner_ref, between_ref,
                out_ref, cells_ref, keys_ref, attended_ref, block_ref, sems):
    row_count, column_count, feature = out_ref.shape
    copies = [pltpu.make_async_copy(between_ref, out_ref.at[pl.ds(HALF_LAT, row_count - WLAT)], sems.at[WLAT])]
    copies[0].start()
    bands = row_count // WLAT
    half = HALF_LAT * WLON
    places = [(side, strip) for side in range(2) for strip in range(strips - 1)]
    for at, (side, strip) in enumerate(places):
        block = halo_ref[HALF_LAT * (1 - side) : HALF_LAT * (2 - side), strip * WLON : (strip + 1) * WLON, :]
        cells_ref[at * half : (at + 1) * half, :] = normalize(block.astype(F32).reshape(half, feature)).astype(BF16)
    keys_ref[...] = project(cells_ref[...], qkv_weight_ref, feature, 2 * feature)
    labels = labels_ref[...]
    label_columns = labels.T
    entries = []
    for at, (side, strip) in enumerate(places):
        mine = slice(at * half, (at + 1) * half)
        rows = slice(0, half) if side else slice(half, WIN)
        place = side * bands * strips + strip
        mask = excluded(label_columns[rows, place : place + 1], labels[place : place + 1])

        def both(head, mine=mine, side=side):
            pair = own_ref[mine, lanes(HEADS + head)], keys_ref[mine, lanes(head)]
            return jnp.concatenate(pair if side else pair[::-1], axis=0)

        for head in range(HEADS):
            entries.append(
                (
                    lambda mine=mine, head=head: own_ref[mine, lanes(head)],
                    lambda head=head, both=both: both(head),
                    lambda head=head, both=both: both(HEADS + head),
                    lambda mask=mask, head=head, rows=rows: bias_ref[head, rows, :] + mask,
                    storer(attended_ref, mine, head),
                )
            )
    attention(entries)
    for side, first in enumerate((0, row_count - HALF_LAT)):
        cells = (strips - 1) * half
        branch = out_project(attended_ref[side * cells : (side + 1) * cells, :], out_weight_ref)
        for row in range(HALF_LAT):
            at = side * HALF_LAT + row
            corner = corner_ref[at].astype(F32)
            middle = [branch[strip * half + row * WLON : strip * half + (row + 1) * WLON] for strip in range(strips - 1)]
            middle = inner_ref[at].astype(F32) + jnp.concatenate(middle, axis=0)
            block_ref[at] = jnp.concatenate([corner[:HALF_LON], middle, corner[HALF_LON:]], axis=0).astype(BF16)
            copies.append(pltpu.make_async_copy(block_ref.at[at], out_ref.at[first + row], sems.at[at]))
            copies[-1].start()
    for copy in copies:
        copy.wait()


def shards(tokens, qkv_weight, out_weight, bias_table, position_index, region_label):
    row_count, column_count, feature = tokens.shape
    bands, strips = row_count // WLAT, column_count // WLON
    whole = shape(*tokens.shape)
    inner_columns = column_count - WLON
    blocks = feature // WIN
    dma = pltpu.SemaphoreType.DMA

    (label_own,) = run(
        functools.partial(label_kernel, strips), [shape(bands * strips, WIN, dtype=F32)], [region_label], flops=5 * 10**9
    )
    ends, inner_rows, middle, columns = run(
        message_kernel,
        [
            shape(2 * WLAT * blocks + 1, HALF_LON, WIN),
            shape(WLAT, inner_columns, feature),
            shape(row_count - WLAT, inner_columns, feature),
            shape(row_count, WLON, feature),
        ],
        [tokens, label_own],
        flops=5 * 10**9,
    )
    ends_received = lat_exchange(ends, 2 * HALF_LAT * blocks)
    rows_received = lat_exchange(inner_rows, HALF_LAT)
    message = shape(row_count * blocks + 1, HALF_LON, WIN)
    columns_sent = run(column_kernel, [message, message], [columns, label_own], flops=2 * 10**10)
    columns_received = lon_exchange(*columns_sent[::-1])

    inner_cells = (strips - 1) * WIN
    inner, bias = run(
        functools.partial(inner_kernel, strips),
        [shape(inner_cells, feature), shape(HEADS, WIN, WIN, dtype=F32)],
        [middle, label_own, bias_table.T, position_index, qkv_weight, out_weight, columns_sent[0]],
        specs=[VMEM] * 6 + [ANY],
        scratch=[pltpu.VMEM((inner_cells, width * feature), BF16) for width in (1, 3, 1)]
        + [pltpu.VMEM((8, -(-bias_table.shape[0] // 128) * 128), F32)],
        mib=12,
        flops=5 * 10**9,
    )
    message = shape(WLAT * blocks + 1, HALF_LON, WIN)
    *corners, labels = run(
        functools.partial(corner_message_kernel, strips),
        [message, message, shape(16, WIN, dtype=F32)],
        [ends_received, label_own, inner],
        specs=[VMEM, VMEM, ANY],
    )
    corners_received = lon_exchange(*corners[::-1])
    row_cells = (strips - 1) * WIN
    (row_qkv,) = run(
        functools.partial(rows_kernel, strips),
        [shape(row_cells, 3 * feature)],
        [inner_rows, qkv_weight, corners[0]],
        specs=[VMEM, VMEM, ANY],
        scratch=[pltpu.VMEM((row_cells, feature), BF16)],
        mib=8,
    )

    def side_scratch(between):
        windows = side_windows(bands, between)
        cells, every = windows[-1][2] + windows[-1][3], len(windows) * WIN
        sizes = ((every, 1), (cells, 1), (cells, 1), (every, 2), (cells, 1))
        return cells, every, [pltpu.VMEM((count, width * feature), BF16) for count, width in sizes]

    cells, every, scratch = side_scratch(True)
    (between,) = run(
        functools.partial(between_kernel, strips),
        [shape(row_count - WLAT, column_count, feature)],
        [columns, *columns_received, labels, bias, qkv_weight, out_weight, inner, row_qkv],
        specs=[VMEM] * 8 + [ANY],
        scratch=scratch,
        mib=12,
    )
    cells, every, scratch = side_scratch(False)
    (corner,) = run(
        functools.partial(corner_kernel, strips),
        [shape(WLAT, WLON, feature)],
        [columns, *columns_received, *corners_received, ends_received, labels, bias, qkv_weight, out_weight],
        scratch=scratch,
        mib=12,
    )
    (out,) = run(
        functools.partial(last_kernel, strips),
        [whole],
        [inner_rows, rows_received, row_qkv, labels, bias, qkv_weight, out_weight, corner, between],
        out_specs=[HBM],
        mib=12,
        scratch=[pltpu.VMEM((row_cells, width * feature), BF16) for width in (1, 2, 1)]
        + [pltpu.VMEM((WLAT, column_count, feature), BF16), dma((WLAT + 1,))],
    )
    return out


def solution(mesh):
    in_specs = (P("lat", "lon", None), P(), P(), P(), P(), P("lat", "lon"))
    out_specs = P("lat", "lon", None)
    return jax.shard_map(shards, mesh=mesh, in_specs=in_specs, out_specs=out_specs, check_vma=False)
```

```python
import functools

import jax
import jax.numpy as jnp
from jax import lax
from jax.experimental import pallas as pl
from jax.experimental.pallas import tpu as pltpu
from jax.sharding import PartitionSpec as P

HEADS = 6
HEAD = 128
WLAT = 8
WLON = 16
WIN = WLAT * WLON
HALF_LAT = WLAT // 2
HALF_LON = WLON // 2
LOG2E = 1.4426950408889634
SCALE = LOG2E / HEAD**0.5
EXCLUDED = -1e30
VMEM = pl.BlockSpec(memory_space=pltpu.VMEM)
HBM = pl.BlockSpec(memory_space=pltpu.HBM)
ANY = pl.BlockSpec(memory_space=pl.ANY)
F32 = jnp.float32
BF16 = jnp.bfloat16


def moved(block, axis, distance):
    count = lax.axis_size(axis)
    route = [((i - distance) % count, i) for i in range(count)]
    return lax.ppermute(block, axis, route)


def lat_exchange(message, cut):
    if lax.axis_size("lat") == 2:
        return moved(message, "lat", 1)
    return jnp.concatenate([moved(message[:cut], "lat", -1), moved(message[cut:], "lat", 1)], axis=0)


def lon_exchange(odd_even, even_odd):
    count = lax.axis_size("lon")
    first = [(i, i ^ 1) for i in range(count)]
    second = [(i, (i + 1 if i % 2 else i - 1) % count) for i in range(count)]
    even_odd = lax.ppermute(even_odd, "lon", first)
    return lax.ppermute(odd_even, "lon", second), even_odd


def run(kernel, outs, operands, scratch=(), specs=None, out_specs=None, mib=4, flops=10**6):
    return pl.pallas_call(
        kernel,
        out_shape=outs,
        in_specs=specs or [VMEM] * len(operands),
        out_specs=out_specs or [VMEM] * len(outs),
        scratch_shapes=scratch,
        compiler_params=pltpu.CompilerParams(vmem_limit_bytes=mib * 2**20),
        cost_estimate=pl.CostEstimate(flops=flops, bytes_accessed=10**5, transcendentals=0),
    )(*operands)


def shape(*extent, dtype=BF16):
    return jax.ShapeDtypeStruct(extent, dtype)


def normalize(floats):
    floats = floats - jnp.mean(floats, axis=-1, keepdims=True)
    return floats * lax.rsqrt(jnp.mean(jnp.square(floats), axis=-1, keepdims=True) + 1e-05)


def label_rows(labels, strips):
    rows, columns = labels.shape
    labels = labels.astype(BF16)
    source = lax.broadcasted_iota(jnp.int32, (columns, WIN), 0)
    cell = lax.broadcasted_iota(jnp.int32, (columns, WIN), 1)
    at_row = lax.broadcasted_iota(jnp.int32, (rows, WIN), 0) % WLAT == lax.broadcasted_iota(jnp.int32, (rows, WIN), 1) // WLON
    place = lax.broadcasted_iota(jnp.int32, (rows // WLAT * strips, WIN), 0)
    result = jnp.zeros((rows // WLAT * strips, WIN), F32)
    for strip in range(strips):
        spread = jnp.dot(labels, (source == strip * WLON + cell % WLON).astype(BF16), preferred_element_type=F32)
        spread = jnp.where(at_row, spread, 0.0)
        for band in range(rows // WLAT):
            row = jnp.sum(spread[band * WLAT : (band + 1) * WLAT], axis=0, keepdims=True)
            result = jnp.where(place == band * strips + strip, row, result)
    return result


def label_kernel(strips, label_ref, rows_ref):
    rows_ref[...] = label_rows(label_ref[...], strips)


def put_cells(message_ref, row, cells):
    groups = cells.shape[1] // WIN
    for group in range(groups):
        message_ref[row * groups + group] = cells[:, group * WIN : (group + 1) * WIN].astype(BF16)


def cells_of(message_ref, row):
    groups = HEADS * HEAD // WIN
    return jnp.concatenate([message_ref[row * groups + group].astype(F32) for group in range(groups)], axis=1)


def put_labels(message_ref, rows):
    if rows.shape[0] < HALF_LON:
        rows = jnp.concatenate([rows, jnp.zeros((HALF_LON - rows.shape[0], WIN), F32)], axis=0)
    message_ref[message_ref.shape[0] - 1] = rows.astype(BF16)


def labels_of(message_ref):
    return message_ref[message_ref.shape[0] - 1].astype(F32)


def message_kernel(tokens_ref, rows_ref, ends_ref, inner_ref, middle_ref, columns_ref):
    row_count, _, feature = tokens_ref.shape
    for row in range(row_count):
        floats = tokens_ref[row].astype(F32)
        columns_ref[row] = jnp.concatenate([floats[:HALF_LON], floats[-HALF_LON:]], axis=0).astype(BF16)
        inner = floats[HALF_LON:-HALF_LON].astype(BF16)
        if HALF_LAT <= row < row_count - HALF_LAT:
            middle_ref[row - HALF_LAT] = inner
        else:
            at = row if row < HALF_LAT else row - row_count + WLAT
            put_cells(ends_ref, 2 * at, floats[:HALF_LON])
            put_cells(ends_ref, 2 * at + 1, floats[-HALF_LON:])
            inner_ref[at] = inner
    put_labels(ends_ref, rows_ref[...])


def normalize_kernel(inner_ref, normed_ref):
    for row in range(inner_ref.shape[0]):
        normed_ref[row] = normalize(inner_ref[row].astype(F32)).astype(BF16)


def column_kernel(columns_ref, rows_ref, even_odd_ref, odd_even_ref):
    odd = lax.axis_index("lon") % 2 == 1
    for row in range(columns_ref.shape[0]):
        floats = columns_ref[row].astype(F32)
        left, right = floats[:HALF_LON], floats[HALF_LON:]
        put_cells(even_odd_ref, row, jnp.where(odd, left, right))
        put_cells(odd_even_ref, row, jnp.where(odd, right, left))
    put_labels(even_odd_ref, rows_ref[...])
    put_labels(odd_even_ref, rows_ref[...])


def corner_message_kernel(strips, ends_ref, rows_ref, after_ref, even_odd_ref, odd_even_ref, labels_ref):
    odd = lax.axis_index("lon") % 2 == 1
    for row in range(WLAT):
        left, right = cells_of(ends_ref, 2 * row), cells_of(ends_ref, 2 * row + 1)
        put_cells(even_odd_ref, row, jnp.where(odd, left, right))
        put_cells(odd_even_ref, row, jnp.where(odd, right, left))
    own = rows_ref[...]
    above = labels_of(ends_ref)[own.shape[0] - strips : own.shape[0]]
    labels_ref[...] = jnp.concatenate([above, own, jnp.zeros((16 - strips - own.shape[0], WIN), F32)], axis=0)
    put_labels(even_odd_ref, above)
    put_labels(odd_even_ref, above)


def halo_row(row, row_count):
    return row + HALF_LAT if row < HALF_LAT else row - row_count - HALF_LAT


def look_up(table_ref, index_ref, out_ref):
    entries = table_ref.shape[1]
    for row in range(0, WIN, 8):
        index = index_ref[row : row + 8, :]
        low, high = index & 127, index >> 7
        for head in range(HEADS):
            value = jnp.zeros((8, WIN), F32)
            for part in range(-(-entries // 128)):
                source = jnp.broadcast_to(table_ref[head : head + 1, part * 128 : part * 128 + 128], (8, 128))
                value = jnp.where(high == part, jnp.take_along_axis(source, low, axis=1), value)
            out_ref[head, row : row + 8, :] = value * LOG2E


def excluded(columns, row):
    return jnp.where(columns == row, 0.0, EXCLUDED)


def attention(entries):
    scores = []
    for queries, keys, _, bias, _ in entries:
        product = lax.dot_general(queries(), keys(), (((1,), (1,)), ((), ())), preferred_element_type=F32)
        scores.append(product * SCALE + bias())
    numerators = [jnp.exp2(score - jnp.max(score, axis=-1, keepdims=True)) for score in scores]
    for (_, _, values, _, store), numerator in zip(entries, numerators):
        total = jnp.sum(numerator, axis=-1, keepdims=True)
        summed = jnp.dot(numerator.astype(BF16), values(), preferred_element_type=F32)
        store((summed * (1.0 / total)).astype(BF16))


def project(source, weight_ref, first, count):
    return jnp.dot(source, weight_ref[:, first : first + count], preferred_element_type=F32).astype(BF16)


def out_project(attended, weight_ref):
    return jnp.dot(attended, weight_ref[...], preferred_element_type=F32).astype(BF16).astype(F32)


def lanes(head):
    return slice(head * HEAD, (head + 1) * HEAD)


def storer(ref, rows, head):
    def store(value):
        ref[rows, lanes(head)] = value

    return store


def inner_kernel(strips, middle_ref, rows_ref, table_ref, index_ref, qkv_weight_ref, out_weight_ref,
                 after_ref, out_ref, bias_ref, cells_ref, qkv_ref, attended_ref, wide_ref):
    feature = middle_ref.shape[-1]
    floats = []
    for strip in range(strips - 1):
        window = middle_ref[:, strip * WLON : (strip + 1) * WLON, :].astype(F32).reshape(WIN, feature)
        floats.append(window)
        cells_ref[strip * WIN : (strip + 1) * WIN, :] = normalize(window).astype(BF16)
    wide_ref[...] = jnp.zeros(wide_ref.shape, F32)
    wide_ref[: table_ref.shape[0], : table_ref.shape[1]] = table_ref[...]
    qkv_ref[...] = project(cells_ref[...], qkv_weight_ref, 0, 3 * feature)
    look_up(wide_ref, index_ref, bias_ref)
    labels = rows_ref[...]
    label_columns = labels.T
    entries = []
    for strip in range(strips - 1):
        mine = slice(strip * WIN, (strip + 1) * WIN)
        mask = excluded(label_columns[:, strip : strip + 1], labels[strip : strip + 1])
        for head in range(HEADS):
            entries.append(
                (
                    lambda mine=mine, head=head: qkv_ref[mine, lanes(head)],
                    lambda mine=mine, head=head: qkv_ref[mine, lanes(HEADS + head)],
                    lambda mine=mine, head=head: qkv_ref[mine, lanes(2 * HEADS + head)],
                    lambda mask=mask, head=head: bias_ref[head] + mask,
                    storer(attended_ref, mine, head),
                )
            )
    attention(entries)
    branch = out_project(attended_ref[...], out_weight_ref)
    for strip in range(strips - 1):
        mine = slice(strip * WIN, (strip + 1) * WIN)
        out_ref[mine, :] = (floats[strip] + branch[mine]).astype(BF16)


def rows_kernel(strips, inner_ref, qkv_weight_ref, after_ref, out_ref, cells_ref):
    feature = inner_ref.shape[-1]
    half = HALF_LAT * WLON
    for side in range(2):
        for strip in range(strips - 1):
            block = inner_ref[side * HALF_LAT : (side + 1) * HALF_LAT, strip * WLON : (strip + 1) * WLON, :]
            start = (side * (strips - 1) + strip) * half
            cells_ref[start : start + half, :] = block.astype(F32).reshape(half, feature).astype(BF16)
    out_ref[...] = project(cells_ref[...], qkv_weight_ref, 0, 3 * feature)


def side_windows(bands, between):
    windows, start = [], 0
    for band in range(bands + 1):
        if (0 < band < bands) == between:
            count = HALF_LON * (WLAT if between else HALF_LAT)
            for side in range(2):
                windows.append((band, side, start, count))
                start += count
    return windows


def side_blocks(windows, bands, strips, own_of, halo_of, left_labels, labels, bias_ref, qkv_weight_ref, out_weight_ref,
                cells_ref, own_ref, queries_ref, keys_ref, attended_ref):
    feature = cells_ref.shape[-1]
    label_columns = left_labels.T, labels.T
    tokens_of = {}
    for at, (band, side, start, count) in enumerate(windows):
        own = [own_of(row, side) for row in range(band * WLAT, (band + 1) * WLAT)]
        halo = [halo_of(row, side) for row in range(band * WLAT, (band + 1) * WLAT)]
        mine = slice(HALF_LAT if band == 0 else 0, HALF_LAT if band == bands else WLAT)
        tokens_of[band, side] = own[mine]
        own = normalize(jnp.stack(own))
        halo = normalize(jnp.stack(halo))
        window = jnp.concatenate([own, halo] if side else [halo, own], axis=1)
        cells_ref[at * WIN : (at + 1) * WIN, :] = window.reshape(WIN, feature).astype(BF16)
        own_ref[start : start + count, :] = own[mine].reshape(count, feature).astype(BF16)
    queries_ref[...] = project(own_ref[...], qkv_weight_ref, 0, feature)
    keys_ref[...] = project(cells_ref[...], qkv_weight_ref, feature, 2 * feature)

    def own_rows(array, band, side):
        array = array.reshape(WLAT, WLON, WIN)
        array = array[HALF_LAT if band == 0 else 0 : HALF_LAT if band == bands else WLAT]
        array = array[:, :HALF_LON] if side else array[:, HALF_LON:]
        return array.reshape(-1, WIN)

    entries = []
    for at, (band, side, start, count) in enumerate(windows):
        mine, whole = slice(start, start + count), slice(at * WIN, (at + 1) * WIN)
        place = band * strips + strips - 1
        row = (labels if side else left_labels)[place : place + 1]
        mask = own_rows(excluded(label_columns[side][:, place : place + 1], row), band, side)
        for head in range(HEADS):
            entries.append(
                (
                    lambda mine=mine, head=head: queries_ref[mine, lanes(head)],
                    lambda whole=whole, head=head: keys_ref[whole, lanes(head)],
                    lambda whole=whole, head=head: keys_ref[whole, lanes(HEADS + head)],
                    lambda mask=mask, head=head, band=band, side=side: own_rows(bias_ref[head], band, side) + mask,
                    storer(attended_ref, mine, head),
                )
            )
    attention(entries)
    branch = out_project(attended_ref[...], out_weight_ref)
    blocks = {}
    for band, side, start, count in windows:
        for row, own in enumerate(tokens_of[band, side]):
            at = start + row * HALF_LON
            blocks[band, side, row] = own + branch[at : at + HALF_LON]
    return blocks


def swapped(odd_even_ref, even_odd_ref):
    odd = lax.axis_index("lon") % 2 == 1

    def row_of(row, side):
        first, second = cells_of(even_odd_ref, row), cells_of(odd_even_ref, row)
        return jnp.where(odd, second, first) if side else jnp.where(odd, first, second)

    return row_of, jnp.where(odd, labels_of(even_odd_ref), labels_of(odd_even_ref))


def half_of(floats, side):
    return floats[HALF_LON:] if side else floats[:HALF_LON]


def left_labels_of(above, own):
    return jnp.concatenate([above, own, jnp.zeros((16 - above.shape[0] - own.shape[0], WIN), F32)], axis=0)


def between_kernel(strips, columns_ref, odd_even_ref, even_odd_ref, labels_ref, bias_ref, qkv_weight_ref, out_weight_ref, inner_ref,
                   after_ref, out_ref, *scratch):
    row_count = columns_ref.shape[0]
    received, own_labels = swapped(odd_even_ref, even_odd_ref)
    left_labels = left_labels_of(jnp.zeros((strips, WIN), F32), own_labels)
    blocks = side_blocks(
        side_windows(row_count // WLAT, True), row_count // WLAT, strips,
        lambda row, side: half_of(columns_ref[row - HALF_LAT].astype(F32), side),
        lambda row, side: received(row - HALF_LAT, side),
        left_labels, labels_ref[...], bias_ref, qkv_weight_ref, out_weight_ref, *scratch,
    )
    for row in range(WLAT):
        middle = [inner_ref[strip * WIN + row * WLON : strip * WIN + (row + 1) * WLON, :].astype(F32) for strip in range(strips - 1)]
        out_ref[row] = jnp.concatenate([blocks[1, 0, row]] + middle + [blocks[1, 1, row]], axis=0).astype(BF16)


def corner_kernel(strips, columns_ref, odd_even_ref, even_odd_ref, corner_odd_even_ref, corner_even_odd_ref, ends_ref, labels_ref,
                  bias_ref, qkv_weight_ref, out_weight_ref, corner_ref, *scratch):
    row_count = columns_ref.shape[0]
    bands = row_count // WLAT
    received, own_labels = swapped(odd_even_ref, even_odd_ref)
    received_corner, above_labels = swapped(corner_odd_even_ref, corner_even_odd_ref)
    left_labels = left_labels_of(above_labels[:strips], own_labels)

    def inside(row):
        return HALF_LAT <= row < row_count + HALF_LAT

    def own_of(row, side):
        if inside(row):
            return half_of(columns_ref[row - HALF_LAT].astype(F32), side)
        return cells_of(ends_ref, 2 * halo_row(row, row_count) + side)

    def halo_of(row, side):
        return received(row - HALF_LAT, side) if inside(row) else received_corner(halo_row(row, row_count), side)

    blocks = side_blocks(
        side_windows(bands, False), bands, strips, own_of, halo_of,
        left_labels, labels_ref[...], bias_ref, qkv_weight_ref, out_weight_ref, *scratch,
    )
    for band, first in ((0, 0), (bands, HALF_LAT)):
        for row in range(HALF_LAT):
            corner_ref[first + row] = jnp.concatenate([blocks[band, 0, row], blocks[band, 1, row]], axis=0).astype(BF16)


def last_kernel(strips, inner_ref, halo_ref, own_ref, labels_ref, bias_ref, qkv_weight_ref, out_weight_ref, corner_ref, between_ref,
                out_ref, cells_ref, keys_ref, attended_ref, block_ref, sems):
    row_count, column_count, feature = out_ref.shape
    copies = [pltpu.make_async_copy(between_ref, out_ref.at[pl.ds(HALF_LAT, row_count - WLAT)], sems.at[WLAT])]
    copies[0].start()
    bands = row_count // WLAT
    half = HALF_LAT * WLON
    places = [(side, strip) for side in range(2) for strip in range(strips - 1)]
    for at, (side, strip) in enumerate(places):
        block = halo_ref[HALF_LAT * (1 - side) : HALF_LAT * (2 - side), strip * WLON : (strip + 1) * WLON, :]
        cells_ref[at * half : (at + 1) * half, :] = block.astype(F32).reshape(half, feature).astype(BF16)
    keys_ref[...] = project(cells_ref[...], qkv_weight_ref, feature, 2 * feature)
    labels = labels_ref[...]
    label_columns = labels.T
    entries = []
    for at, (side, strip) in enumerate(places):
        mine = slice(at * half, (at + 1) * half)
        rows = slice(0, half) if side else slice(half, WIN)
        place = side * bands * strips + strip
        mask = excluded(label_columns[rows, place : place + 1], labels[place : place + 1])

        def both(head, mine=mine, side=side):
            pair = own_ref[mine, lanes(HEADS + head)], keys_ref[mine, lanes(head)]
            return jnp.concatenate(pair if side else pair[::-1], axis=0)

        for head in range(HEADS):
            entries.append(
                (
                    lambda mine=mine, head=head: own_ref[mine, lanes(head)],
                    lambda head=head, both=both: both(head),
                    lambda head=head, both=both: both(HEADS + head),
                    lambda mask=mask, head=head, rows=rows: bias_ref[head, rows, :] + mask,
                    storer(attended_ref, mine, head),
                )
            )
    attention(entries)
    for side, first in enumerate((0, row_count - HALF_LAT)):
        cells = (strips - 1) * half
        branch = out_project(attended_ref[side * cells : (side + 1) * cells, :], out_weight_ref)
        for row in range(HALF_LAT):
            at = side * HALF_LAT + row
            corner = corner_ref[at].astype(F32)
            middle = [branch[strip * half + row * WLON : strip * half + (row + 1) * WLON] for strip in range(strips - 1)]
            middle = inner_ref[at].astype(F32) + jnp.concatenate(middle, axis=0)
            block_ref[at] = jnp.concatenate([corner[:HALF_LON], middle, corner[HALF_LON:]], axis=0).astype(BF16)
            copies.append(pltpu.make_async_copy(block_ref.at[at], out_ref.at[first + row], sems.at[at]))
            copies[-1].start()
    for copy in copies:
        copy.wait()


def shards(tokens, qkv_weight, out_weight, bias_table, position_index, region_label):
    row_count, column_count, feature = tokens.shape
    bands, strips = row_count // WLAT, column_count // WLON
    whole = shape(*tokens.shape)
    inner_columns = column_count - WLON
    blocks = feature // WIN
    dma = pltpu.SemaphoreType.DMA

    (label_own,) = run(
        functools.partial(label_kernel, strips), [shape(bands * strips, WIN, dtype=F32)], [region_label], flops=5 * 10**9
    )
    ends, inner_rows, middle, columns = run(
        message_kernel,
        [
            shape(2 * WLAT * blocks + 1, HALF_LON, WIN),
            shape(WLAT, inner_columns, feature),
            shape(row_count - WLAT, inner_columns, feature),
            shape(row_count, WLON, feature),
        ],
        [tokens, label_own],
        flops=5 * 10**9,
    )
    ends_received = lat_exchange(ends, 2 * HALF_LAT * blocks)
    (normed_rows,) = run(normalize_kernel, [shape(WLAT, inner_columns, feature)], [inner_rows])
    rows_received = lat_exchange(normed_rows, HALF_LAT)
    message = shape(row_count * blocks + 1, HALF_LON, WIN)
    columns_sent = run(column_kernel, [message, message], [columns, label_own], flops=2 * 10**10)
    columns_received = lon_exchange(*columns_sent[::-1])

    inner_cells = (strips - 1) * WIN
    inner, bias = run(
        functools.partial(inner_kernel, strips),
        [shape(inner_cells, feature), shape(HEADS, WIN, WIN, dtype=F32)],
        [middle, label_own, bias_table.T, position_index, qkv_weight, out_weight, columns_sent[0]],
        specs=[VMEM] * 6 + [ANY],
        scratch=[pltpu.VMEM((inner_cells, width * feature), BF16) for width in (1, 3, 1)]
        + [pltpu.VMEM((8, -(-bias_table.shape[0] // 128) * 128), F32)],
        mib=12,
        flops=5 * 10**9,
    )
    message = shape(WLAT * blocks + 1, HALF_LON, WIN)
    *corners, labels = run(
        functools.partial(corner_message_kernel, strips),
        [message, message, shape(16, WIN, dtype=F32)],
        [ends_received, label_own, inner],
        specs=[VMEM, VMEM, ANY],
    )
    corners_received = lon_exchange(*corners[::-1])
    row_cells = (strips - 1) * WIN
    (row_qkv,) = run(
        functools.partial(rows_kernel, strips),
        [shape(row_cells, 3 * feature)],
        [normed_rows, qkv_weight, corners[0]],
        specs=[VMEM, VMEM, ANY],
        scratch=[pltpu.VMEM((row_cells, feature), BF16)],
        mib=8,
    )

    def side_scratch(between):
        windows = side_windows(bands, between)
        cells, every = windows[-1][2] + windows[-1][3], len(windows) * WIN
        sizes = ((every, 1), (cells, 1), (cells, 1), (every, 2), (cells, 1))
        return cells, every, [pltpu.VMEM((count, width * feature), BF16) for count, width in sizes]

    cells, every, scratch = side_scratch(True)
    (between,) = run(
        functools.partial(between_kernel, strips),
        [shape(row_count - WLAT, column_count, feature)],
        [columns, *columns_received, labels, bias, qkv_weight, out_weight, inner, row_qkv],
        specs=[VMEM] * 8 + [ANY],
        scratch=scratch,
        mib=12,
    )
    cells, every, scratch = side_scratch(False)
    (corner,) = run(
        functools.partial(corner_kernel, strips),
        [shape(WLAT, WLON, feature)],
        [columns, *columns_received, *corners_received, ends_received, labels, bias, qkv_weight, out_weight],
        scratch=scratch,
        mib=12,
    )
    (out,) = run(
        functools.partial(last_kernel, strips),
        [whole],
        [inner_rows, rows_received, row_qkv, labels, bias, qkv_weight, out_weight, corner, between],
        out_specs=[HBM],
        mib=12,
        scratch=[pltpu.VMEM((row_cells, width * feature), BF16) for width in (1, 2, 1)]
        + [pltpu.VMEM((WLAT, column_count, feature), BF16), dma((WLAT + 1,))],
    )
    return out


def solution(mesh):
    in_specs = (P("lat", "lon", None), P(), P(), P(), P(), P("lat", "lon"))
    out_specs = P("lat", "lon", None)
    return jax.shard_map(shards, mesh=mesh, in_specs=in_specs, out_specs=out_specs, check_vma=False)
```

```python
import functools

import jax
import jax.numpy as jnp
from jax import lax
from jax.experimental import pallas as pl
from jax.experimental.pallas import tpu as pltpu
from jax.sharding import PartitionSpec as P

HEADS = 6
HEAD = 128
WLAT = 8
WLON = 16
WIN = WLAT * WLON
HALF_LAT = WLAT // 2
HALF_LON = WLON // 2
LOG2E = 1.4426950408889634
SCALE = LOG2E / HEAD**0.5
EXCLUDED = -1e30
VMEM = pl.BlockSpec(memory_space=pltpu.VMEM)
HBM = pl.BlockSpec(memory_space=pltpu.HBM)
ANY = pl.BlockSpec(memory_space=pl.ANY)
F32 = jnp.float32
BF16 = jnp.bfloat16


def moved(block, axis, distance):
    count = lax.axis_size(axis)
    route = [((i - distance) % count, i) for i in range(count)]
    return lax.ppermute(block, axis, route)


def lat_exchange(message, cut):
    if lax.axis_size("lat") == 2:
        return moved(message, "lat", 1)
    return jnp.concatenate([moved(message[:cut], "lat", -1), moved(message[cut:], "lat", 1)], axis=0)


def lon_exchange(odd_even, even_odd):
    count = lax.axis_size("lon")
    first = [(i, i ^ 1) for i in range(count)]
    second = [(i, (i + 1 if i % 2 else i - 1) % count) for i in range(count)]
    even_odd = lax.ppermute(even_odd, "lon", first)
    return lax.ppermute(odd_even, "lon", second), even_odd


def run(kernel, outs, operands, scratch=(), specs=None, out_specs=None, mib=4, flops=10**6):
    return pl.pallas_call(
        kernel,
        out_shape=outs,
        in_specs=specs or [VMEM] * len(operands),
        out_specs=out_specs or [VMEM] * len(outs),
        scratch_shapes=scratch,
        compiler_params=pltpu.CompilerParams(vmem_limit_bytes=mib * 2**20),
        cost_estimate=pl.CostEstimate(flops=flops, bytes_accessed=10**5, transcendentals=0),
    )(*operands)


def shape(*extent, dtype=BF16):
    return jax.ShapeDtypeStruct(extent, dtype)


def normalize(floats):
    floats = floats - jnp.mean(floats, axis=-1, keepdims=True)
    return floats * lax.rsqrt(jnp.mean(jnp.square(floats), axis=-1, keepdims=True) + 1e-05)


def label_rows(labels, strips):
    rows, columns = labels.shape
    labels = labels.astype(BF16)
    source = lax.broadcasted_iota(jnp.int32, (columns, WIN), 0)
    cell = lax.broadcasted_iota(jnp.int32, (columns, WIN), 1)
    at_row = lax.broadcasted_iota(jnp.int32, (rows, WIN), 0) % WLAT == lax.broadcasted_iota(jnp.int32, (rows, WIN), 1) // WLON
    place = lax.broadcasted_iota(jnp.int32, (rows // WLAT * strips, WIN), 0)
    result = jnp.zeros((rows // WLAT * strips, WIN), F32)
    for strip in range(strips):
        spread = jnp.dot(labels, (source == strip * WLON + cell % WLON).astype(BF16), preferred_element_type=F32)
        spread = jnp.where(at_row, spread, 0.0)
        for band in range(rows // WLAT):
            row = jnp.sum(spread[band * WLAT : (band + 1) * WLAT], axis=0, keepdims=True)
            result = jnp.where(place == band * strips + strip, row, result)
    return result


def label_kernel(strips, label_ref, rows_ref):
    rows_ref[...] = label_rows(label_ref[...], strips)


def put_cells(message_ref, row, cells):
    groups = cells.shape[1] // WIN
    for group in range(groups):
        message_ref[row * groups + group] = cells[:, group * WIN : (group + 1) * WIN].astype(BF16)


def cells_of(message_ref, row):
    groups = HEADS * HEAD // WIN
    return jnp.concatenate([message_ref[row * groups + group].astype(F32) for group in range(groups)], axis=1)


def put_labels(message_ref, rows):
    if rows.shape[0] < HALF_LON:
        rows = jnp.concatenate([rows, jnp.zeros((HALF_LON - rows.shape[0], WIN), F32)], axis=0)
    message_ref[message_ref.shape[0] - 1] = rows.astype(BF16)


def labels_of(message_ref):
    return message_ref[message_ref.shape[0] - 1].astype(F32)


def message_kernel(tokens_ref, rows_ref, ends_ref, inner_ref, middle_ref, columns_ref):
    row_count, _, feature = tokens_ref.shape
    for row in range(row_count):
        floats = tokens_ref[row].astype(F32)
        columns_ref[row] = jnp.concatenate([floats[:HALF_LON], floats[-HALF_LON:]], axis=0).astype(BF16)
        inner = floats[HALF_LON:-HALF_LON].astype(BF16)
        if HALF_LAT <= row < row_count - HALF_LAT:
            middle_ref[row - HALF_LAT] = inner
        else:
            at = row if row < HALF_LAT else row - row_count + WLAT
            put_cells(ends_ref, 2 * at, floats[:HALF_LON])
            put_cells(ends_ref, 2 * at + 1, floats[-HALF_LON:])
            inner_ref[at] = inner
    put_labels(ends_ref, rows_ref[...])


def normalize_kernel(inner_ref, normed_ref):
    for row in range(inner_ref.shape[0]):
        normed_ref[row] = normalize(inner_ref[row].astype(F32)).astype(BF16)


def column_kernel(columns_ref, rows_ref, even_odd_ref, odd_even_ref):
    odd = lax.axis_index("lon") % 2 == 1
    for row in range(columns_ref.shape[0]):
        floats = columns_ref[row].astype(F32)
        left, right = floats[:HALF_LON], floats[HALF_LON:]
        put_cells(even_odd_ref, row, jnp.where(odd, left, right))
        put_cells(odd_even_ref, row, jnp.where(odd, right, left))
    put_labels(even_odd_ref, rows_ref[...])
    put_labels(odd_even_ref, rows_ref[...])


def corner_message_kernel(strips, ends_ref, rows_ref, after_ref, even_odd_ref, odd_even_ref, labels_ref):
    odd = lax.axis_index("lon") % 2 == 1
    for row in range(WLAT):
        left, right = cells_of(ends_ref, 2 * row), cells_of(ends_ref, 2 * row + 1)
        put_cells(even_odd_ref, row, jnp.where(odd, left, right))
        put_cells(odd_even_ref, row, jnp.where(odd, right, left))
    own = rows_ref[...]
    above = labels_of(ends_ref)[own.shape[0] - strips : own.shape[0]]
    labels_ref[...] = jnp.concatenate([above, own, jnp.zeros((16 - strips - own.shape[0], WIN), F32)], axis=0)
    put_labels(even_odd_ref, above)
    put_labels(odd_even_ref, above)


def halo_row(row, row_count):
    return row + HALF_LAT if row < HALF_LAT else row - row_count - HALF_LAT


def look_up(table_ref, index_ref, out_ref):
    entries = table_ref.shape[1]
    for row in range(0, WIN, 8):
        index = index_ref[row : row + 8, :]
        low, high = index & 127, index >> 7
        for head in range(HEADS):
            value = jnp.zeros((8, WIN), F32)
            for part in range(-(-entries // 128)):
                source = jnp.broadcast_to(table_ref[head : head + 1, part * 128 : part * 128 + 128], (8, 128))
                value = jnp.where(high == part, jnp.take_along_axis(source, low, axis=1), value)
            out_ref[head, row : row + 8, :] = value * LOG2E


def excluded(columns, row):
    return jnp.where(columns == row, 0.0, EXCLUDED)


def attention(entries):
    scores = []
    for queries, keys, _, bias, _ in entries:
        product = lax.dot_general(queries(), keys(), (((1,), (1,)), ((), ())), preferred_element_type=F32)
        scores.append(product * SCALE + bias())
    numerators = [jnp.exp2(score - jnp.max(score, axis=-1, keepdims=True)) for score in scores]
    for (_, _, values, _, store), numerator in zip(entries, numerators):
        total = jnp.sum(numerator, axis=-1, keepdims=True)
        summed = jnp.dot(numerator.astype(BF16), values(), preferred_element_type=F32)
        store((summed * (1.0 / total)).astype(BF16))


def project(source, weight_ref, first, count):
    return jnp.dot(source, weight_ref[:, first : first + count], preferred_element_type=F32).astype(BF16)


def out_project(attended, weight_ref):
    return jnp.dot(attended, weight_ref[...], preferred_element_type=F32).astype(BF16).astype(F32)


def lanes(head):
    return slice(head * HEAD, (head + 1) * HEAD)


def storer(ref, rows, head):
    def store(value):
        ref[rows, lanes(head)] = value

    return store


def inner_kernel(strips, middle_ref, rows_ref, table_ref, index_ref, qkv_weight_ref, out_weight_ref,
                 after_ref, out_ref, bias_ref, cells_ref, qkv_ref, attended_ref, wide_ref):
    feature = middle_ref.shape[-1]
    floats = []
    for strip in range(strips - 1):
        window = middle_ref[:, strip * WLON : (strip + 1) * WLON, :].astype(F32).reshape(WIN, feature)
        floats.append(window)
        cells_ref[strip * WIN : (strip + 1) * WIN, :] = normalize(window).astype(BF16)
    wide_ref[...] = jnp.zeros(wide_ref.shape, F32)
    wide_ref[: table_ref.shape[0], : table_ref.shape[1]] = table_ref[...]
    qkv_ref[...] = project(cells_ref[...], qkv_weight_ref, 0, 3 * feature)
    look_up(wide_ref, index_ref, bias_ref)
    labels = rows_ref[...]
    label_columns = labels.T
    entries = []
    for strip in range(strips - 1):
        mine = slice(strip * WIN, (strip + 1) * WIN)
        mask = excluded(label_columns[:, strip : strip + 1], labels[strip : strip + 1])
        for head in range(HEADS):
            entries.append(
                (
                    lambda mine=mine, head=head: qkv_ref[mine, lanes(head)],
                    lambda mine=mine, head=head: qkv_ref[mine, lanes(HEADS + head)],
                    lambda mine=mine, head=head: qkv_ref[mine, lanes(2 * HEADS + head)],
                    lambda mask=mask, head=head: bias_ref[head] + mask,
                    storer(attended_ref, mine, head),
                )
            )
    attention(entries)
    branch = out_project(attended_ref[...], out_weight_ref)
    for strip in range(strips - 1):
        mine = slice(strip * WIN, (strip + 1) * WIN)
        out_ref[mine, :] = (floats[strip] + branch[mine]).astype(BF16)


def rows_kernel(strips, inner_ref, qkv_weight_ref, after_ref, out_ref, cells_ref):
    feature = inner_ref.shape[-1]
    half = HALF_LAT * WLON
    for side in range(2):
        for strip in range(strips - 1):
            block = inner_ref[side * HALF_LAT : (side + 1) * HALF_LAT, strip * WLON : (strip + 1) * WLON, :]
            start = (side * (strips - 1) + strip) * half
            cells_ref[start : start + half, :] = block.astype(F32).reshape(half, feature).astype(BF16)
    out_ref[...] = project(cells_ref[...], qkv_weight_ref, 0, 3 * feature)


def side_attention(windows, bands, strips, queries_of, keys_of, left_labels, labels, bias_ref, attended_ref):
    label_columns = left_labels.T, labels.T

    def own_rows(array, band, side):
        array = array.reshape(WLAT, WLON, WIN)
        array = array[HALF_LAT if band == 0 else 0 : HALF_LAT if band == bands else WLAT]
        array = array[:, :HALF_LON] if side else array[:, HALF_LON:]
        return array.reshape(-1, WIN)

    entries = []
    for at, (band, side, start, count) in enumerate(windows):
        mine = slice(start, start + count)
        place = band * strips + strips - 1
        row = (labels if side else left_labels)[place : place + 1]
        mask = own_rows(excluded(label_columns[side][:, place : place + 1], row), band, side)
        for head in range(HEADS):
            entries.append(
                (
                    lambda mine=mine, head=head: queries_of(mine, lanes(head)),
                    lambda at=at, head=head: keys_of(at, lanes(head)),
                    lambda at=at, head=head: keys_of(at, lanes(HEADS + head)),
                    lambda mask=mask, head=head, band=band, side=side: own_rows(bias_ref[head], band, side) + mask,
                    storer(attended_ref, mine, head),
                )
            )
    attention(entries)


def swapped(odd_even_ref, even_odd_ref):
    odd = lax.axis_index("lon") % 2 == 1

    def row_of(row, side):
        first, second = cells_of(even_odd_ref, row), cells_of(odd_even_ref, row)
        return jnp.where(odd, second, first) if side else jnp.where(odd, first, second)

    return row_of, jnp.where(odd, labels_of(even_odd_ref), labels_of(odd_even_ref))


def half_of(floats, side):
    return floats[HALF_LON:] if side else floats[:HALF_LON]


def left_labels_of(above, own):
    return jnp.concatenate([above, own, jnp.zeros((16 - above.shape[0] - own.shape[0], WIN), F32)], axis=0)


def between_windows():
    return [(1, side, side * WLAT * HALF_LON, WLAT * HALF_LON) for side in range(2)]


def corner_windows(bands):
    count = HALF_LAT * HALF_LON
    return [(band, side, at * count, count) for at, (band, side) in enumerate((b, s) for b in (0, bands) for s in range(2))]


def between_kernel(strips, columns_ref, odd_even_ref, even_odd_ref, labels_ref, bias_ref, qkv_weight_ref, out_weight_ref, inner_ref,
                   after_ref, out_ref, corner_queries_ref, corner_keys_ref, cells_ref, own_ref, queries_ref, keys_ref, attended_ref):
    row_count, _, feature = columns_ref.shape
    bands = row_count // WLAT
    received, own_labels = swapped(odd_even_ref, even_odd_ref)
    left_labels = left_labels_of(jnp.zeros((strips, WIN), F32), own_labels)
    windows = between_windows()
    half = HALF_LAT * WLON
    tokens_of = {}

    def put(first, rows, side, key_start, query_start):
        own = jnp.stack([half_of(columns_ref[row].astype(F32), side) for row in range(first, first + rows)])
        halo = normalize(jnp.stack([received(row, side) for row in range(first, first + rows)]))
        normed = normalize(own)
        cells = jnp.concatenate([normed, halo] if side else [halo, normed], axis=1)
        cells_ref[key_start : key_start + rows * WLON, :] = cells.reshape(rows * WLON, feature).astype(BF16)
        own_ref[query_start : query_start + rows * HALF_LON, :] = normed.reshape(rows * HALF_LON, feature).astype(BF16)
        return own

    for at, (band, side, start, count) in enumerate(windows):
        tokens_of[side] = put(HALF_LAT, WLAT, side, at * WIN, start)
    ends = corner_windows(bands)
    for at, (band, side, start, count) in enumerate(ends):
        put(row_count - HALF_LAT if band else 0, HALF_LAT, side, len(windows) * WIN + at * half, WLAT * WLON + start)
    queries_ref[...] = project(own_ref[...], qkv_weight_ref, 0, feature)
    keys_ref[...] = project(cells_ref[...], qkv_weight_ref, feature, 2 * feature)
    corner_queries_ref[...] = queries_ref[WLAT * WLON :, :]
    corner_keys_ref[...] = keys_ref[len(windows) * WIN :, :]
    side_attention(
        windows, bands, strips,
        lambda mine, columns: queries_ref[mine, columns],
        lambda at, columns: keys_ref[at * WIN : (at + 1) * WIN, columns],
        left_labels, labels_ref[...], bias_ref, attended_ref,
    )
    branch = out_project(attended_ref[...], out_weight_ref)
    for row in range(WLAT):
        middle = [inner_ref[strip * WIN + row * WLON : strip * WIN + (row + 1) * WLON, :].astype(F32) for strip in range(strips - 1)]
        ends = []
        for side, (_, _, start, _) in enumerate(windows):
            at = start + row * HALF_LON
            ends.append(tokens_of[side][row] + branch[at : at + HALF_LON])
        out_ref[row] = jnp.concatenate([ends[0]] + middle + [ends[1]], axis=0).astype(BF16)


def corner_kernel(strips, columns_ref, odd_even_ref, even_odd_ref, corner_odd_even_ref, corner_even_odd_ref, ends_ref, labels_ref, queries_ref, own_ref,
                  bias_ref, qkv_weight_ref, out_weight_ref, corner_ref, cells_ref, keys_ref, attended_ref):
    row_count, _, feature = columns_ref.shape
    bands = row_count // WLAT
    half = HALF_LAT * WLON
    _, own_labels = swapped(odd_even_ref, even_odd_ref)
    received, above_labels = swapped(corner_odd_even_ref, corner_even_odd_ref)
    left_labels = left_labels_of(above_labels[:strips], own_labels)
    windows = corner_windows(bands)
    for at, (band, side, start, count) in enumerate(windows):
        rows = range(0 if band else HALF_LAT, HALF_LAT if band else WLAT)
        near = normalize(jnp.stack([cells_of(ends_ref, 2 * row + side) for row in rows]))
        far = normalize(jnp.stack([received(row, side) for row in rows]))
        cells = jnp.concatenate([near, far] if side else [far, near], axis=1)
        cells_ref[at * half : (at + 1) * half, :] = cells.reshape(half, feature).astype(BF16)
    keys_ref[...] = project(cells_ref[...], qkv_weight_ref, feature, 2 * feature)

    def keys_of(at, columns):
        mine = slice(at * half, (at + 1) * half)
        pair = own_ref[mine, columns], keys_ref[mine, columns]
        return jnp.concatenate(pair if windows[at][0] else pair[::-1], axis=0)

    side_attention(
        windows, bands, strips, lambda mine, columns: queries_ref[mine, columns], keys_of,
        left_labels, labels_ref[...], bias_ref, attended_ref,
    )
    branch = out_project(attended_ref[...], out_weight_ref)
    for end in range(2):
        for row in range(HALF_LAT):
            cells = columns_ref[row_count - HALF_LAT + row if end else row].astype(F32)
            starts = [windows[2 * end + side][2] + row * HALF_LON for side in range(2)]
            added = jnp.concatenate([branch[start : start + HALF_LON] for start in starts], axis=0)
            corner_ref[end * HALF_LAT + row] = (cells + added).astype(BF16)


def last_kernel(strips, inner_ref, halo_ref, own_ref, labels_ref, bias_ref, qkv_weight_ref, out_weight_ref, corner_ref, between_ref,
                out_ref, cells_ref, keys_ref, attended_ref, block_ref, sems):
    row_count, column_count, feature = out_ref.shape
    copies = [pltpu.make_async_copy(between_ref, out_ref.at[pl.ds(HALF_LAT, row_count - WLAT)], sems.at[WLAT])]
    copies[0].start()
    bands = row_count // WLAT
    half = HALF_LAT * WLON
    places = [(side, strip) for side in range(2) for strip in range(strips - 1)]
    for at, (side, strip) in enumerate(places):
        block = halo_ref[HALF_LAT * (1 - side) : HALF_LAT * (2 - side), strip * WLON : (strip + 1) * WLON, :]
        cells_ref[at * half : (at + 1) * half, :] = block.astype(F32).reshape(half, feature).astype(BF16)
    keys_ref[...] = project(cells_ref[...], qkv_weight_ref, feature, 2 * feature)
    labels = labels_ref[...]
    label_columns = labels.T
    entries = []
    for at, (side, strip) in enumerate(places):
        mine = slice(at * half, (at + 1) * half)
        rows = slice(0, half) if side else slice(half, WIN)
        place = side * bands * strips + strip
        mask = excluded(label_columns[rows, place : place + 1], labels[place : place + 1])

        def both(head, mine=mine, side=side):
            pair = own_ref[mine, lanes(HEADS + head)], keys_ref[mine, lanes(head)]
            return jnp.concatenate(pair if side else pair[::-1], axis=0)

        for head in range(HEADS):
            entries.append(
                (
                    lambda mine=mine, head=head: own_ref[mine, lanes(head)],
                    lambda head=head, both=both: both(head),
                    lambda head=head, both=both: both(HEADS + head),
                    lambda mask=mask, head=head, rows=rows: bias_ref[head, rows, :] + mask,
                    storer(attended_ref, mine, head),
                )
            )
    attention(entries)
    for side, first in enumerate((0, row_count - HALF_LAT)):
        cells = (strips - 1) * half
        branch = out_project(attended_ref[side * cells : (side + 1) * cells, :], out_weight_ref)
        for row in range(HALF_LAT):
            at = side * HALF_LAT + row
            corner = corner_ref[at].astype(F32)
            middle = [branch[strip * half + row * WLON : strip * half + (row + 1) * WLON] for strip in range(strips - 1)]
            middle = inner_ref[at].astype(F32) + jnp.concatenate(middle, axis=0)
            block_ref[at] = jnp.concatenate([corner[:HALF_LON], middle, corner[HALF_LON:]], axis=0).astype(BF16)
            copies.append(pltpu.make_async_copy(block_ref.at[at], out_ref.at[first + row], sems.at[at]))
            copies[-1].start()
    for copy in copies:
        copy.wait()


def shards(tokens, qkv_weight, out_weight, bias_table, position_index, region_label):
    row_count, column_count, feature = tokens.shape
    bands, strips = row_count // WLAT, column_count // WLON
    whole = shape(*tokens.shape)
    inner_columns = column_count - WLON
    blocks = feature // WIN
    dma = pltpu.SemaphoreType.DMA

    (label_own,) = run(
        functools.partial(label_kernel, strips), [shape(bands * strips, WIN, dtype=F32)], [region_label], flops=5 * 10**9
    )
    ends, inner_rows, middle, columns = run(
        message_kernel,
        [
            shape(2 * WLAT * blocks + 1, HALF_LON, WIN),
            shape(WLAT, inner_columns, feature),
            shape(row_count - WLAT, inner_columns, feature),
            shape(row_count, WLON, feature),
        ],
        [tokens, label_own],
        flops=5 * 10**9,
    )
    ends_received = lat_exchange(ends, 2 * HALF_LAT * blocks)
    (normed_rows,) = run(normalize_kernel, [shape(WLAT, inner_columns, feature)], [inner_rows])
    rows_received = lat_exchange(normed_rows, HALF_LAT)
    message = shape(row_count * blocks + 1, HALF_LON, WIN)
    columns_sent = run(column_kernel, [message, message], [columns, label_own], flops=2 * 10**10)
    columns_received = lon_exchange(*columns_sent[::-1])

    inner_cells = (strips - 1) * WIN
    inner, bias = run(
        functools.partial(inner_kernel, strips),
        [shape(inner_cells, feature), shape(HEADS, WIN, WIN, dtype=F32)],
        [middle, label_own, bias_table.T, position_index, qkv_weight, out_weight, columns_sent[0]],
        specs=[VMEM] * 6 + [ANY],
        scratch=[pltpu.VMEM((inner_cells, width * feature), BF16) for width in (1, 3, 1)]
        + [pltpu.VMEM((8, -(-bias_table.shape[0] // 128) * 128), F32)],
        mib=12,
        flops=5 * 10**9,
    )
    message = shape(WLAT * blocks + 1, HALF_LON, WIN)
    *corners, labels = run(
        functools.partial(corner_message_kernel, strips),
        [message, message, shape(16, WIN, dtype=F32)],
        [ends_received, label_own, inner],
        specs=[VMEM, VMEM, ANY],
    )
    corners_received = lon_exchange(*corners[::-1])
    row_cells = (strips - 1) * WIN
    (row_qkv,) = run(
        functools.partial(rows_kernel, strips),
        [shape(row_cells, 3 * feature)],
        [normed_rows, qkv_weight, corners[0]],
        specs=[VMEM, VMEM, ANY],
        scratch=[pltpu.VMEM((row_cells, feature), BF16)],
        mib=8,
    )

    side_cells, corner_cells = WLAT * WLON, 2 * HALF_LAT * WLON
    every = 4 * WIN
    between, corner_queries, corner_keys = run(
        functools.partial(between_kernel, strips),
        [shape(row_count - WLAT, column_count, feature), shape(corner_cells, feature), shape(2 * WIN, 2 * feature)],
        [columns, *columns_received, labels, bias, qkv_weight, out_weight, inner, row_qkv],
        specs=[VMEM] * 8 + [ANY],
        scratch=[pltpu.VMEM((count, width * feature), BF16) for count, width in
                 ((every, 1), (side_cells + corner_cells, 1), (side_cells + corner_cells, 1), (every, 2), (side_cells, 1))],
        mib=12,
    )
    (corner,) = run(
        functools.partial(corner_kernel, strips),
        [shape(WLAT, WLON, feature)],
        [columns, *columns_received, *corners_received, ends_received, labels, corner_queries, corner_keys, bias, qkv_weight, out_weight],
        scratch=[pltpu.VMEM((count, width * feature), BF16) for count, width in ((2 * WIN, 1), (2 * WIN, 2), (corner_cells, 1))],
        mib=12,
    )
    (out,) = run(
        functools.partial(last_kernel, strips),
        [whole],
        [inner_rows, rows_received, row_qkv, labels, bias, qkv_weight, out_weight, corner, between],
        out_specs=[HBM],
        mib=12,
        scratch=[pltpu.VMEM((row_cells, width * feature), BF16) for width in (1, 2, 1)]
        + [pltpu.VMEM((WLAT, column_count, feature), BF16), dma((WLAT + 1,))],
    )
    return out


def solution(mesh):
    in_specs = (P("lat", "lon", None), P(), P(), P(), P(), P("lat", "lon"))
    out_specs = P("lat", "lon", None)
    return jax.shard_map(shards, mesh=mesh, in_specs=in_specs, out_specs=out_specs, check_vma=False)
```

```python
import functools

import jax
import jax.numpy as jnp
from jax import lax
from jax.experimental import pallas as pl
from jax.experimental.pallas import tpu as pltpu
from jax.sharding import PartitionSpec as P

HEADS = 6
HEAD = 128
WLAT = 8
WLON = 16
WIN = WLAT * WLON
HALF_LAT = WLAT // 2
HALF_LON = WLON // 2
LOG2E = 1.4426950408889634
SCALE = LOG2E / HEAD**0.5
EXCLUDED = -1e30
VMEM = pl.BlockSpec(memory_space=pltpu.VMEM)
HBM = pl.BlockSpec(memory_space=pltpu.HBM)
ANY = pl.BlockSpec(memory_space=pl.ANY)
F32 = jnp.float32
BF16 = jnp.bfloat16


def moved(block, axis, distance):
    count = lax.axis_size(axis)
    route = [((i - distance) % count, i) for i in range(count)]
    return lax.ppermute(block, axis, route)


def lat_exchange(message, cut):
    if lax.axis_size("lat") == 2:
        return moved(message, "lat", 1)
    return jnp.concatenate([moved(message[:cut], "lat", -1), moved(message[cut:], "lat", 1)], axis=0)


def lon_exchange(odd_even, even_odd):
    count = lax.axis_size("lon")
    first = [(i, i ^ 1) for i in range(count)]
    second = [(i, (i + 1 if i % 2 else i - 1) % count) for i in range(count)]
    even_odd = lax.ppermute(even_odd, "lon", first)
    return lax.ppermute(odd_even, "lon", second), even_odd


def run(kernel, outs, operands, scratch=(), specs=None, out_specs=None, mib=4, flops=10**6):
    return pl.pallas_call(
        kernel,
        out_shape=outs,
        in_specs=specs or [VMEM] * len(operands),
        out_specs=out_specs or [VMEM] * len(outs),
        scratch_shapes=scratch,
        compiler_params=pltpu.CompilerParams(vmem_limit_bytes=mib * 2**20),
        cost_estimate=pl.CostEstimate(flops=flops, bytes_accessed=10**5, transcendentals=0),
    )(*operands)


def shape(*extent, dtype=BF16):
    return jax.ShapeDtypeStruct(extent, dtype)


def normalize(floats):
    floats = floats - jnp.mean(floats, axis=-1, keepdims=True)
    return floats * lax.rsqrt(jnp.mean(jnp.square(floats), axis=-1, keepdims=True) + 1e-05)


def label_rows(labels, strips):
    rows, columns = labels.shape
    labels = labels.astype(BF16)
    source = lax.broadcasted_iota(jnp.int32, (columns, WIN), 0)
    cell = lax.broadcasted_iota(jnp.int32, (columns, WIN), 1)
    at_row = lax.broadcasted_iota(jnp.int32, (rows, WIN), 0) % WLAT == lax.broadcasted_iota(jnp.int32, (rows, WIN), 1) // WLON
    place = lax.broadcasted_iota(jnp.int32, (rows // WLAT * strips, WIN), 0)
    result = jnp.zeros((rows // WLAT * strips, WIN), F32)
    for strip in range(strips):
        spread = jnp.dot(labels, (source == strip * WLON + cell % WLON).astype(BF16), preferred_element_type=F32)
        spread = jnp.where(at_row, spread, 0.0)
        for band in range(rows // WLAT):
            row = jnp.sum(spread[band * WLAT : (band + 1) * WLAT], axis=0, keepdims=True)
            result = jnp.where(place == band * strips + strip, row, result)
    return result


def label_kernel(strips, label_ref, rows_ref):
    rows_ref[...] = label_rows(label_ref[...], strips)


def put_cells(message_ref, row, cells):
    groups = cells.shape[1] // WIN
    for group in range(groups):
        message_ref[row * groups + group] = cells[:, group * WIN : (group + 1) * WIN].astype(BF16)


def cells_of(message_ref, row):
    groups = HEADS * HEAD // WIN
    return jnp.concatenate([message_ref[row * groups + group].astype(F32) for group in range(groups)], axis=1)


def put_labels(message_ref, rows):
    if rows.shape[0] < HALF_LON:
        rows = jnp.concatenate([rows, jnp.zeros((HALF_LON - rows.shape[0], WIN), F32)], axis=0)
    message_ref[message_ref.shape[0] - 1] = rows.astype(BF16)


def labels_of(message_ref):
    return message_ref[message_ref.shape[0] - 1].astype(F32)


def message_kernel(tokens_ref, rows_ref, ends_ref):
    row_count = tokens_ref.shape[0]
    for at in range(WLAT):
        row = at if at < HALF_LAT else row_count - WLAT + at
        put_cells(ends_ref, 2 * at, tokens_ref[row, :WLON, :].astype(F32)[:HALF_LON])
        put_cells(ends_ref, 2 * at + 1, tokens_ref[row, tokens_ref.shape[1] - WLON :, :].astype(F32)[HALF_LON:])
    put_labels(ends_ref, rows_ref[...])


def split_kernel(tokens_ref, after_ref, normed_ref, inner_ref, middle_ref, columns_ref):
    row_count = tokens_ref.shape[0]
    for row in range(row_count):
        floats = tokens_ref[row].astype(F32)
        columns_ref[row] = jnp.concatenate([floats[:HALF_LON], floats[-HALF_LON:]], axis=0).astype(BF16)
        inner = floats[HALF_LON:-HALF_LON]
        if HALF_LAT <= row < row_count - HALF_LAT:
            middle_ref[row - HALF_LAT] = inner.astype(BF16)
        else:
            at = row if row < HALF_LAT else row - row_count + WLAT
            inner_ref[at] = inner.astype(BF16)
            normed_ref[at] = normalize(inner).astype(BF16)


def column_kernel(columns_ref, rows_ref, even_odd_ref, odd_even_ref):
    odd = lax.axis_index("lon") % 2 == 1
    for row in range(columns_ref.shape[0]):
        floats = columns_ref[row].astype(F32)
        left, right = floats[:HALF_LON], floats[HALF_LON:]
        put_cells(even_odd_ref, row, jnp.where(odd, left, right))
        put_cells(odd_even_ref, row, jnp.where(odd, right, left))
    put_labels(even_odd_ref, rows_ref[...])
    put_labels(odd_even_ref, rows_ref[...])


def corner_message_kernel(strips, ends_ref, rows_ref, after_ref, even_odd_ref, odd_even_ref, labels_ref):
    odd = lax.axis_index("lon") % 2 == 1
    for row in range(WLAT):
        left, right = cells_of(ends_ref, 2 * row), cells_of(ends_ref, 2 * row + 1)
        put_cells(even_odd_ref, row, jnp.where(odd, left, right))
        put_cells(odd_even_ref, row, jnp.where(odd, right, left))
    own = rows_ref[...]
    above = labels_of(ends_ref)[own.shape[0] - strips : own.shape[0]]
    labels_ref[...] = jnp.concatenate([above, own, jnp.zeros((16 - strips - own.shape[0], WIN), F32)], axis=0)
    put_labels(even_odd_ref, above)
    put_labels(odd_even_ref, above)


def halo_row(row, row_count):
    return row + HALF_LAT if row < HALF_LAT else row - row_count - HALF_LAT


def look_up(table_ref, index_ref, out_ref):
    entries = table_ref.shape[1]
    for row in range(0, WIN, 8):
        index = index_ref[row : row + 8, :]
        low, high = index & 127, index >> 7
        for head in range(HEADS):
            value = jnp.zeros((8, WIN), F32)
            for part in range(-(-entries // 128)):
                source = jnp.broadcast_to(table_ref[head : head + 1, part * 128 : part * 128 + 128], (8, 128))
                value = jnp.where(high == part, jnp.take_along_axis(source, low, axis=1), value)
            out_ref[head, row : row + 8, :] = value * LOG2E


def excluded(columns, row):
    return jnp.where(columns == row, 0.0, EXCLUDED)


def attention(entries):
    scores = []
    for queries, keys, _, bias, _ in entries:
        product = lax.dot_general(queries(), keys(), (((1,), (1,)), ((), ())), preferred_element_type=F32)
        scores.append(product * SCALE + bias())
    numerators = [jnp.exp2(score - jnp.max(score, axis=-1, keepdims=True)) for score in scores]
    for (_, _, values, _, store), numerator in zip(entries, numerators):
        total = jnp.sum(numerator, axis=-1, keepdims=True)
        summed = jnp.dot(numerator.astype(BF16), values(), preferred_element_type=F32)
        store((summed * (1.0 / total)).astype(BF16))


def project(source, weight_ref, first, count):
    return jnp.dot(source, weight_ref[:, first : first + count], preferred_element_type=F32).astype(BF16)


def out_project(attended, weight_ref):
    return jnp.dot(attended, weight_ref[...], preferred_element_type=F32).astype(BF16).astype(F32)


def lanes(head):
    return slice(head * HEAD, (head + 1) * HEAD)


def storer(ref, rows, head):
    def store(value):
        ref[rows, lanes(head)] = value

    return store


def inner_kernel(strips, middle_ref, rows_ref, table_ref, index_ref, qkv_weight_ref, out_weight_ref,
                 after_ref, out_ref, bias_ref, cells_ref, qkv_ref, attended_ref, wide_ref):
    feature = middle_ref.shape[-1]
    floats = []
    for strip in range(strips - 1):
        window = middle_ref[:, strip * WLON : (strip + 1) * WLON, :].astype(F32).reshape(WIN, feature)
        floats.append(window)
        cells_ref[strip * WIN : (strip + 1) * WIN, :] = normalize(window).astype(BF16)
    wide_ref[...] = jnp.zeros(wide_ref.shape, F32)
    wide_ref[: table_ref.shape[0], : table_ref.shape[1]] = table_ref[...]
    qkv_ref[...] = project(cells_ref[...], qkv_weight_ref, 0, 3 * feature)
    look_up(wide_ref, index_ref, bias_ref)
    labels = rows_ref[...]
    label_columns = labels.T
    entries = []
    for strip in range(strips - 1):
        mine = slice(strip * WIN, (strip + 1) * WIN)
        mask = excluded(label_columns[:, strip : strip + 1], labels[strip : strip + 1])
        for head in range(HEADS):
            entries.append(
                (
                    lambda mine=mine, head=head: qkv_ref[mine, lanes(head)],
                    lambda mine=mine, head=head: qkv_ref[mine, lanes(HEADS + head)],
                    lambda mine=mine, head=head: qkv_ref[mine, lanes(2 * HEADS + head)],
                    lambda mask=mask, head=head: bias_ref[head] + mask,
                    storer(attended_ref, mine, head),
                )
            )
    attention(entries)
    branch = out_project(attended_ref[...], out_weight_ref)
    for strip in range(strips - 1):
        mine = slice(strip * WIN, (strip + 1) * WIN)
        out_ref[mine, :] = (floats[strip] + branch[mine]).astype(BF16)


def rows_kernel(strips, inner_ref, qkv_weight_ref, after_ref, out_ref, cells_ref):
    feature = inner_ref.shape[-1]
    half = HALF_LAT * WLON
    for side in range(2):
        for strip in range(strips - 1):
            block = inner_ref[side * HALF_LAT : (side + 1) * HALF_LAT, strip * WLON : (strip + 1) * WLON, :]
            start = (side * (strips - 1) + strip) * half
            cells_ref[start : start + half, :] = block.astype(F32).reshape(half, feature).astype(BF16)
    out_ref[...] = project(cells_ref[...], qkv_weight_ref, 0, 3 * feature)


def side_attention(windows, bands, strips, queries_of, keys_of, left_labels, labels, bias_ref, attended_ref):
    label_columns = left_labels.T, labels.T

    def own_rows(array, band, side):
        array = array.reshape(WLAT, WLON, WIN)
        array = array[HALF_LAT if band == 0 else 0 : HALF_LAT if band == bands else WLAT]
        array = array[:, :HALF_LON] if side else array[:, HALF_LON:]
        return array.reshape(-1, WIN)

    entries = []
    for at, (band, side, start, count) in enumerate(windows):
        mine = slice(start, start + count)
        place = band * strips + strips - 1
        row = (labels if side else left_labels)[place : place + 1]
        mask = own_rows(excluded(label_columns[side][:, place : place + 1], row), band, side)
        for head in range(HEADS):
            entries.append(
                (
                    lambda mine=mine, head=head: queries_of(mine, lanes(head)),
                    lambda at=at, head=head: keys_of(at, lanes(head)),
                    lambda at=at, head=head: keys_of(at, lanes(HEADS + head)),
                    lambda mask=mask, head=head, band=band, side=side: own_rows(bias_ref[head], band, side) + mask,
                    storer(attended_ref, mine, head),
                )
            )
    attention(entries)


def swapped(odd_even_ref, even_odd_ref):
    odd = lax.axis_index("lon") % 2 == 1

    def row_of(row, side):
        first, second = cells_of(even_odd_ref, row), cells_of(odd_even_ref, row)
        return jnp.where(odd, second, first) if side else jnp.where(odd, first, second)

    return row_of, jnp.where(odd, labels_of(even_odd_ref), labels_of(odd_even_ref))


def half_of(floats, side):
    return floats[HALF_LON:] if side else floats[:HALF_LON]


def left_labels_of(above, own):
    return jnp.concatenate([above, own, jnp.zeros((16 - above.shape[0] - own.shape[0], WIN), F32)], axis=0)


def between_windows():
    return [(1, side, side * WLAT * HALF_LON, WLAT * HALF_LON) for side in range(2)]


def corner_windows(bands):
    count = HALF_LAT * HALF_LON
    return [(band, side, at * count, count) for at, (band, side) in enumerate((b, s) for b in (0, bands) for s in range(2))]


def between_kernel(strips, columns_ref, odd_even_ref, even_odd_ref, labels_ref, bias_ref, qkv_weight_ref, out_weight_ref, inner_ref,
                   after_ref, out_ref, corner_queries_ref, corner_keys_ref, cells_ref, own_ref, queries_ref, keys_ref, attended_ref):
    row_count, _, feature = columns_ref.shape
    bands = row_count // WLAT
    received, own_labels = swapped(odd_even_ref, even_odd_ref)
    left_labels = left_labels_of(jnp.zeros((strips, WIN), F32), own_labels)
    windows = between_windows()
    half = HALF_LAT * WLON
    tokens_of = {}

    def put(first, rows, side, key_start, query_start):
        own = jnp.stack([half_of(columns_ref[row].astype(F32), side) for row in range(first, first + rows)])
        halo = normalize(jnp.stack([received(row, side) for row in range(first, first + rows)]))
        normed = normalize(own)
        cells = jnp.concatenate([normed, halo] if side else [halo, normed], axis=1)
        cells_ref[key_start : key_start + rows * WLON, :] = cells.reshape(rows * WLON, feature).astype(BF16)
        own_ref[query_start : query_start + rows * HALF_LON, :] = normed.reshape(rows * HALF_LON, feature).astype(BF16)
        return own

    for at, (band, side, start, count) in enumerate(windows):
        tokens_of[side] = put(HALF_LAT, WLAT, side, at * WIN, start)
    ends = corner_windows(bands)
    for at, (band, side, start, count) in enumerate(ends):
        put(row_count - HALF_LAT if band else 0, HALF_LAT, side, len(windows) * WIN + at * half, WLAT * WLON + start)
    queries_ref[...] = project(own_ref[...], qkv_weight_ref, 0, feature)
    keys_ref[...] = project(cells_ref[...], qkv_weight_ref, feature, 2 * feature)
    corner_queries_ref[...] = queries_ref[WLAT * WLON :, :]
    corner_keys_ref[...] = keys_ref[len(windows) * WIN :, :]
    side_attention(
        windows, bands, strips,
        lambda mine, columns: queries_ref[mine, columns],
        lambda at, columns: keys_ref[at * WIN : (at + 1) * WIN, columns],
        left_labels, labels_ref[...], bias_ref, attended_ref,
    )
    branch = out_project(attended_ref[...], out_weight_ref)
    for row in range(WLAT):
        middle = [inner_ref[strip * WIN + row * WLON : strip * WIN + (row + 1) * WLON, :].astype(F32) for strip in range(strips - 1)]
        ends = []
        for side, (_, _, start, _) in enumerate(windows):
            at = start + row * HALF_LON
            ends.append(tokens_of[side][row] + branch[at : at + HALF_LON])
        out_ref[row] = jnp.concatenate([ends[0]] + middle + [ends[1]], axis=0).astype(BF16)


def corner_kernel(strips, columns_ref, odd_even_ref, even_odd_ref, corner_odd_even_ref, corner_even_odd_ref, ends_ref, labels_ref, queries_ref, own_ref,
                  bias_ref, qkv_weight_ref, out_weight_ref, corner_ref, cells_ref, keys_ref, attended_ref):
    row_count, _, feature = columns_ref.shape
    bands = row_count // WLAT
    half = HALF_LAT * WLON
    _, own_labels = swapped(odd_even_ref, even_odd_ref)
    received, above_labels = swapped(corner_odd_even_ref, corner_even_odd_ref)
    left_labels = left_labels_of(above_labels[:strips], own_labels)
    windows = corner_windows(bands)
    for at, (band, side, start, count) in enumerate(windows):
        rows = range(0 if band else HALF_LAT, HALF_LAT if band else WLAT)
        near = normalize(jnp.stack([cells_of(ends_ref, 2 * row + side) for row in rows]))
        far = normalize(jnp.stack([received(row, side) for row in rows]))
        cells = jnp.concatenate([near, far] if side else [far, near], axis=1)
        cells_ref[at * half : (at + 1) * half, :] = cells.reshape(half, feature).astype(BF16)
    keys_ref[...] = project(cells_ref[...], qkv_weight_ref, feature, 2 * feature)

    def keys_of(at, columns):
        mine = slice(at * half, (at + 1) * half)
        pair = own_ref[mine, columns], keys_ref[mine, columns]
        return jnp.concatenate(pair if windows[at][0] else pair[::-1], axis=0)

    side_attention(
        windows, bands, strips, lambda mine, columns: queries_ref[mine, columns], keys_of,
        left_labels, labels_ref[...], bias_ref, attended_ref,
    )
    branch = out_project(attended_ref[...], out_weight_ref)
    for end in range(2):
        for row in range(HALF_LAT):
            cells = columns_ref[row_count - HALF_LAT + row if end else row].astype(F32)
            starts = [windows[2 * end + side][2] + row * HALF_LON for side in range(2)]
            added = jnp.concatenate([branch[start : start + HALF_LON] for start in starts], axis=0)
            corner_ref[end * HALF_LAT + row] = (cells + added).astype(BF16)


def last_kernel(strips, inner_ref, halo_ref, own_ref, labels_ref, bias_ref, qkv_weight_ref, out_weight_ref, corner_ref, between_ref,
                out_ref, cells_ref, keys_ref, attended_ref, block_ref, sems):
    row_count, column_count, feature = out_ref.shape
    copies = [pltpu.make_async_copy(between_ref, out_ref.at[pl.ds(HALF_LAT, row_count - WLAT)], sems.at[WLAT])]
    copies[0].start()
    bands = row_count // WLAT
    half = HALF_LAT * WLON
    places = [(side, strip) for side in range(2) for strip in range(strips - 1)]
    for at, (side, strip) in enumerate(places):
        block = halo_ref[HALF_LAT * (1 - side) : HALF_LAT * (2 - side), strip * WLON : (strip + 1) * WLON, :]
        cells_ref[at * half : (at + 1) * half, :] = block.astype(F32).reshape(half, feature).astype(BF16)
    keys_ref[...] = project(cells_ref[...], qkv_weight_ref, feature, 2 * feature)
    labels = labels_ref[...]
    label_columns = labels.T
    entries = []
    for at, (side, strip) in enumerate(places):
        mine = slice(at * half, (at + 1) * half)
        rows = slice(0, half) if side else slice(half, WIN)
        place = side * bands * strips + strip
        mask = excluded(label_columns[rows, place : place + 1], labels[place : place + 1])

        def both(head, mine=mine, side=side):
            pair = own_ref[mine, lanes(HEADS + head)], keys_ref[mine, lanes(head)]
            return jnp.concatenate(pair if side else pair[::-1], axis=0)

        for head in range(HEADS):
            entries.append(
                (
                    lambda mine=mine, head=head: own_ref[mine, lanes(head)],
                    lambda head=head, both=both: both(head),
                    lambda head=head, both=both: both(HEADS + head),
                    lambda mask=mask, head=head, rows=rows: bias_ref[head, rows, :] + mask,
                    storer(attended_ref, mine, head),
                )
            )
    attention(entries)
    for side, first in enumerate((0, row_count - HALF_LAT)):
        cells = (strips - 1) * half
        branch = out_project(attended_ref[side * cells : (side + 1) * cells, :], out_weight_ref)
        for row in range(HALF_LAT):
            at = side * HALF_LAT + row
            corner = corner_ref[at].astype(F32)
            middle = [branch[strip * half + row * WLON : strip * half + (row + 1) * WLON] for strip in range(strips - 1)]
            middle = inner_ref[at].astype(F32) + jnp.concatenate(middle, axis=0)
            block_ref[at] = jnp.concatenate([corner[:HALF_LON], middle, corner[HALF_LON:]], axis=0).astype(BF16)
            copies.append(pltpu.make_async_copy(block_ref.at[at], out_ref.at[first + row], sems.at[at]))
            copies[-1].start()
    for copy in copies:
        copy.wait()


def shards(tokens, qkv_weight, out_weight, bias_table, position_index, region_label):
    row_count, column_count, feature = tokens.shape
    bands, strips = row_count // WLAT, column_count // WLON
    whole = shape(*tokens.shape)
    inner_columns = column_count - WLON
    blocks = feature // WIN
    dma = pltpu.SemaphoreType.DMA

    (label_own,) = run(
        functools.partial(label_kernel, strips), [shape(bands * strips, WIN, dtype=F32)], [region_label], flops=5 * 10**9
    )
    (ends,) = run(message_kernel, [shape(2 * WLAT * blocks + 1, HALF_LON, WIN)], [tokens, label_own], flops=5 * 10**9)
    ends_received = lat_exchange(ends, 2 * HALF_LAT * blocks)
    normed_rows, inner_rows, middle, columns = run(
        split_kernel,
        [
            shape(WLAT, inner_columns, feature),
            shape(WLAT, inner_columns, feature),
            shape(row_count - WLAT, inner_columns, feature),
            shape(row_count, WLON, feature),
        ],
        [tokens, ends],
        specs=[VMEM, ANY],
    )
    rows_received = lat_exchange(normed_rows, HALF_LAT)
    message = shape(row_count * blocks + 1, HALF_LON, WIN)
    columns_sent = run(column_kernel, [message, message], [columns, label_own], flops=2 * 10**10)
    columns_received = lon_exchange(*columns_sent[::-1])

    inner_cells = (strips - 1) * WIN
    inner, bias = run(
        functools.partial(inner_kernel, strips),
        [shape(inner_cells, feature), shape(HEADS, WIN, WIN, dtype=F32)],
        [middle, label_own, bias_table.T, position_index, qkv_weight, out_weight, columns_sent[0]],
        specs=[VMEM] * 6 + [ANY],
        scratch=[pltpu.VMEM((inner_cells, width * feature), BF16) for width in (1, 3, 1)]
        + [pltpu.VMEM((8, -(-bias_table.shape[0] // 128) * 128), F32)],
        mib=12,
        flops=5 * 10**9,
    )
    message = shape(WLAT * blocks + 1, HALF_LON, WIN)
    *corners, labels = run(
        functools.partial(corner_message_kernel, strips),
        [message, message, shape(16, WIN, dtype=F32)],
        [ends_received, label_own, inner],
        specs=[VMEM, VMEM, ANY],
    )
    corners_received = lon_exchange(*corners[::-1])
    row_cells = (strips - 1) * WIN
    (row_qkv,) = run(
        functools.partial(rows_kernel, strips),
        [shape(row_cells, 3 * feature)],
        [normed_rows, qkv_weight, corners[0]],
        specs=[VMEM, VMEM, ANY],
        scratch=[pltpu.VMEM((row_cells, feature), BF16)],
        mib=8,
    )

    side_cells, corner_cells = WLAT * WLON, 2 * HALF_LAT * WLON
    every = 4 * WIN
    between, corner_queries, corner_keys = run(
        functools.partial(between_kernel, strips),
        [shape(row_count - WLAT, column_count, feature), shape(corner_cells, feature), shape(2 * WIN, 2 * feature)],
        [columns, *columns_received, labels, bias, qkv_weight, out_weight, inner, row_qkv],
        specs=[VMEM] * 8 + [ANY],
        scratch=[pltpu.VMEM((count, width * feature), BF16) for count, width in
                 ((every, 1), (side_cells + corner_cells, 1), (side_cells + corner_cells, 1), (every, 2), (side_cells, 1))],
        mib=12,
    )
    (corner,) = run(
        functools.partial(corner_kernel, strips),
        [shape(WLAT, WLON, feature)],
        [columns, *columns_received, *corners_received, ends_received, labels, corner_queries, corner_keys, bias, qkv_weight, out_weight],
        scratch=[pltpu.VMEM((count, width * feature), BF16) for count, width in ((2 * WIN, 1), (2 * WIN, 2), (corner_cells, 1))],
        mib=12,
    )
    (out,) = run(
        functools.partial(last_kernel, strips),
        [whole],
        [inner_rows, rows_received, row_qkv, labels, bias, qkv_weight, out_weight, corner, between],
        out_specs=[HBM],
        mib=12,
        scratch=[pltpu.VMEM((row_cells, width * feature), BF16) for width in (1, 2, 1)]
        + [pltpu.VMEM((WLAT, column_count, feature), BF16), dma((WLAT + 1,))],
    )
    return out


def solution(mesh):
    in_specs = (P("lat", "lon", None), P(), P(), P(), P(), P("lat", "lon"))
    out_specs = P("lat", "lon", None)
    return jax.shard_map(shards, mesh=mesh, in_specs=in_specs, out_specs=out_specs, check_vma=False)
```

```python
import functools

import jax
import jax.numpy as jnp
from jax import lax
from jax.experimental import pallas as pl
from jax.experimental.pallas import tpu as pltpu
from jax.sharding import PartitionSpec as P

HEADS = 6
HEAD = 128
WLAT = 8
WLON = 16
WIN = WLAT * WLON
HALF_LAT = WLAT // 2
HALF_LON = WLON // 2
LOG2E = 1.4426950408889634
SCALE = LOG2E / HEAD**0.5
EXCLUDED = -1e30
VMEM = pl.BlockSpec(memory_space=pltpu.VMEM)
HBM = pl.BlockSpec(memory_space=pltpu.HBM)
ANY = pl.BlockSpec(memory_space=pl.ANY)
F32 = jnp.float32
BF16 = jnp.bfloat16


def moved(block, axis, distance):
    count = lax.axis_size(axis)
    route = [((i - distance) % count, i) for i in range(count)]
    return lax.ppermute(block, axis, route)


def lat_exchange(message, cut):
    if lax.axis_size("lat") == 2:
        return moved(message, "lat", 1)
    return jnp.concatenate([moved(message[:cut], "lat", -1), moved(message[cut:], "lat", 1)], axis=0)


def lon_exchange(odd_even, even_odd):
    count = lax.axis_size("lon")
    first = [(i, i ^ 1) for i in range(count)]
    second = [(i, (i + 1 if i % 2 else i - 1) % count) for i in range(count)]
    even_odd = lax.ppermute(even_odd, "lon", first)
    return lax.ppermute(odd_even, "lon", second), even_odd


def run(kernel, outs, operands, scratch=(), specs=None, out_specs=None, mib=4, flops=10**6):
    return pl.pallas_call(
        kernel,
        out_shape=outs,
        in_specs=specs or [VMEM] * len(operands),
        out_specs=out_specs or [VMEM] * len(outs),
        scratch_shapes=scratch,
        compiler_params=pltpu.CompilerParams(vmem_limit_bytes=mib * 2**20),
        cost_estimate=pl.CostEstimate(flops=flops, bytes_accessed=10**5, transcendentals=0),
    )(*operands)


def shape(*extent, dtype=BF16):
    return jax.ShapeDtypeStruct(extent, dtype)


def normalize(floats):
    floats = floats - jnp.mean(floats, axis=-1, keepdims=True)
    return floats * lax.rsqrt(jnp.mean(jnp.square(floats), axis=-1, keepdims=True) + 1e-05)


def label_rows(labels, strips):
    rows, columns = labels.shape
    labels = labels.astype(BF16)
    source = lax.broadcasted_iota(jnp.int32, (columns, WIN), 0)
    cell = lax.broadcasted_iota(jnp.int32, (columns, WIN), 1)
    at_row = lax.broadcasted_iota(jnp.int32, (rows, WIN), 0) % WLAT == lax.broadcasted_iota(jnp.int32, (rows, WIN), 1) // WLON
    place = lax.broadcasted_iota(jnp.int32, (rows // WLAT * strips, WIN), 0)
    result = jnp.zeros((rows // WLAT * strips, WIN), F32)
    for strip in range(strips):
        spread = jnp.dot(labels, (source == strip * WLON + cell % WLON).astype(BF16), preferred_element_type=F32)
        spread = jnp.where(at_row, spread, 0.0)
        for band in range(rows // WLAT):
            row = jnp.sum(spread[band * WLAT : (band + 1) * WLAT], axis=0, keepdims=True)
            result = jnp.where(place == band * strips + strip, row, result)
    return result


def label_kernel(strips, label_ref, rows_ref):
    rows_ref[...] = label_rows(label_ref[...], strips)


def put_cells(message_ref, row, cells):
    groups = cells.shape[1] // WIN
    for group in range(groups):
        message_ref[row * groups + group] = cells[:, group * WIN : (group + 1) * WIN].astype(BF16)


def cells_of(message_ref, row):
    groups = HEADS * HEAD // WIN
    return jnp.concatenate([message_ref[row * groups + group].astype(F32) for group in range(groups)], axis=1)


def put_labels(message_ref, rows):
    if rows.shape[0] < HALF_LON:
        rows = jnp.concatenate([rows, jnp.zeros((HALF_LON - rows.shape[0], WIN), F32)], axis=0)
    message_ref[message_ref.shape[0] - 1] = rows.astype(BF16)


def labels_of(message_ref):
    return message_ref[message_ref.shape[0] - 1].astype(F32)


def message_kernel(tokens_ref, rows_ref, ends_ref):
    row_count = tokens_ref.shape[0]
    for at in range(WLAT):
        row = at if at < HALF_LAT else row_count - WLAT + at
        put_cells(ends_ref, 2 * at, tokens_ref[row, :WLON, :].astype(F32)[:HALF_LON])
        put_cells(ends_ref, 2 * at + 1, tokens_ref[row, tokens_ref.shape[1] - WLON :, :].astype(F32)[HALF_LON:])
    put_labels(ends_ref, rows_ref[...])


def split_kernel(tokens_ref, after_ref, normed_ref, inner_ref, middle_ref, columns_ref):
    row_count = tokens_ref.shape[0]
    for row in range(row_count):
        floats = tokens_ref[row].astype(F32)
        columns_ref[row] = jnp.concatenate([floats[:HALF_LON], floats[-HALF_LON:]], axis=0).astype(BF16)
        inner = floats[HALF_LON:-HALF_LON]
        if HALF_LAT <= row < row_count - HALF_LAT:
            middle_ref[row - HALF_LAT] = inner.astype(BF16)
        else:
            at = row if row < HALF_LAT else row - row_count + WLAT
            inner_ref[at] = inner.astype(BF16)
            normed_ref[at] = normalize(inner).astype(BF16)


def column_kernel(columns_ref, rows_ref, even_odd_ref, odd_even_ref):
    odd = lax.axis_index("lon") % 2 == 1
    for row in range(columns_ref.shape[0]):
        floats = columns_ref[row].astype(F32)
        left, right = floats[:HALF_LON], floats[HALF_LON:]
        put_cells(even_odd_ref, row, jnp.where(odd, left, right))
        put_cells(odd_even_ref, row, jnp.where(odd, right, left))
    put_labels(even_odd_ref, rows_ref[...])
    put_labels(odd_even_ref, rows_ref[...])


def corner_message_kernel(strips, ends_ref, rows_ref, after_ref, even_odd_ref, odd_even_ref, labels_ref):
    odd = lax.axis_index("lon") % 2 == 1
    for row in range(WLAT):
        left, right = cells_of(ends_ref, 2 * row), cells_of(ends_ref, 2 * row + 1)
        put_cells(even_odd_ref, row, jnp.where(odd, left, right))
        put_cells(odd_even_ref, row, jnp.where(odd, right, left))
    own = rows_ref[...]
    above = labels_of(ends_ref)[own.shape[0] - strips : own.shape[0]]
    labels_ref[...] = jnp.concatenate([above, own, jnp.zeros((16 - strips - own.shape[0], WIN), F32)], axis=0)
    put_labels(even_odd_ref, above)
    put_labels(odd_even_ref, above)


def halo_row(row, row_count):
    return row + HALF_LAT if row < HALF_LAT else row - row_count - HALF_LAT


def look_up(table_ref, index_ref, out_ref):
    entries = table_ref.shape[1]
    for row in range(0, WIN, 8):
        index = index_ref[row : row + 8, :]
        low, high = index & 127, index >> 7
        for head in range(HEADS):
            value = jnp.zeros((8, WIN), F32)
            for part in range(-(-entries // 128)):
                source = jnp.broadcast_to(table_ref[head : head + 1, part * 128 : part * 128 + 128], (8, 128))
                value = jnp.where(high == part, jnp.take_along_axis(source, low, axis=1), value)
            out_ref[head, row : row + 8, :] = value * LOG2E


def excluded(columns, row):
    return jnp.where(columns == row, 0.0, EXCLUDED)


def attention(entries):
    scores = []
    for queries, keys, _, bias, _ in entries:
        product = lax.dot_general(queries(), keys(), (((1,), (1,)), ((), ())), preferred_element_type=F32)
        scores.append(product * SCALE + bias())
    numerators = [jnp.exp2(score - jnp.max(score, axis=-1, keepdims=True)) for score in scores]
    for (_, _, values, _, store), numerator in zip(entries, numerators):
        value = values()
        both = jnp.concatenate([value, jnp.ones_like(value)], axis=1)
        both = jnp.dot(numerator.astype(BF16), both, preferred_element_type=F32)
        store((both[:, :HEAD] * (1.0 / both[:, HEAD:])).astype(BF16))


def project(source, weight_ref, first, count):
    return jnp.dot(source, weight_ref[:, first : first + count], preferred_element_type=F32).astype(BF16)


def out_project(attended, weight_ref):
    return jnp.dot(attended, weight_ref[...], preferred_element_type=F32).astype(BF16).astype(F32)


def lanes(head):
    return slice(head * HEAD, (head + 1) * HEAD)


def storer(ref, rows, head):
    def store(value):
        ref[rows, lanes(head)] = value

    return store


def inner_kernel(strips, middle_ref, rows_ref, table_ref, index_ref, qkv_weight_ref, out_weight_ref,
                 after_ref, out_ref, bias_ref, cells_ref, qkv_ref, attended_ref, wide_ref):
    feature = middle_ref.shape[-1]
    floats = []
    for strip in range(strips - 1):
        window = middle_ref[:, strip * WLON : (strip + 1) * WLON, :].astype(F32).reshape(WIN, feature)
        floats.append(window)
        cells_ref[strip * WIN : (strip + 1) * WIN, :] = normalize(window).astype(BF16)
    wide_ref[...] = jnp.zeros(wide_ref.shape, F32)
    wide_ref[: table_ref.shape[0], : table_ref.shape[1]] = table_ref[...]
    qkv_ref[...] = project(cells_ref[...], qkv_weight_ref, 0, 3 * feature)
    look_up(wide_ref, index_ref, bias_ref)
    labels = rows_ref[...]
    label_columns = labels.T
    entries = []
    for strip in range(strips - 1):
        mine = slice(strip * WIN, (strip + 1) * WIN)
        mask = excluded(label_columns[:, strip : strip + 1], labels[strip : strip + 1])
        for head in range(HEADS):
            entries.append(
                (
                    lambda mine=mine, head=head: qkv_ref[mine, lanes(head)],
                    lambda mine=mine, head=head: qkv_ref[mine, lanes(HEADS + head)],
                    lambda mine=mine, head=head: qkv_ref[mine, lanes(2 * HEADS + head)],
                    lambda mask=mask, head=head: bias_ref[head] + mask,
                    storer(attended_ref, mine, head),
                )
            )
    attention(entries)
    branch = out_project(attended_ref[...], out_weight_ref)
    for strip in range(strips - 1):
        mine = slice(strip * WIN, (strip + 1) * WIN)
        out_ref[mine, :] = (floats[strip] + branch[mine]).astype(BF16)


def rows_kernel(strips, inner_ref, qkv_weight_ref, after_ref, out_ref, cells_ref):
    feature = inner_ref.shape[-1]
    half = HALF_LAT * WLON
    for side in range(2):
        for strip in range(strips - 1):
            block = inner_ref[side * HALF_LAT : (side + 1) * HALF_LAT, strip * WLON : (strip + 1) * WLON, :]
            start = (side * (strips - 1) + strip) * half
            cells_ref[start : start + half, :] = block.astype(F32).reshape(half, feature).astype(BF16)
    out_ref[...] = project(cells_ref[...], qkv_weight_ref, 0, 3 * feature)


def side_attention(windows, bands, strips, queries_of, keys_of, left_labels, labels, bias_ref, attended_ref):
    label_columns = left_labels.T, labels.T

    def own_rows(array, band, side):
        array = array.reshape(WLAT, WLON, WIN)
        array = array[HALF_LAT if band == 0 else 0 : HALF_LAT if band == bands else WLAT]
        array = array[:, :HALF_LON] if side else array[:, HALF_LON:]
        return array.reshape(-1, WIN)

    entries = []
    for at, (band, side, start, count) in enumerate(windows):
        mine = slice(start, start + count)
        place = band * strips + strips - 1
        row = (labels if side else left_labels)[place : place + 1]
        mask = own_rows(excluded(label_columns[side][:, place : place + 1], row), band, side)
        for head in range(HEADS):
            entries.append(
                (
                    lambda mine=mine, head=head: queries_of(mine, lanes(head)),
                    lambda at=at, head=head: keys_of(at, lanes(head)),
                    lambda at=at, head=head: keys_of(at, lanes(HEADS + head)),
                    lambda mask=mask, head=head, band=band, side=side: own_rows(bias_ref[head], band, side) + mask,
                    storer(attended_ref, mine, head),
                )
            )
    attention(entries)


def swapped(odd_even_ref, even_odd_ref):
    odd = lax.axis_index("lon") % 2 == 1

    def row_of(row, side):
        first, second = cells_of(even_odd_ref, row), cells_of(odd_even_ref, row)
        return jnp.where(odd, second, first) if side else jnp.where(odd, first, second)

    return row_of, jnp.where(odd, labels_of(even_odd_ref), labels_of(odd_even_ref))


def half_of(floats, side):
    return floats[HALF_LON:] if side else floats[:HALF_LON]


def left_labels_of(above, own):
    return jnp.concatenate([above, own, jnp.zeros((16 - above.shape[0] - own.shape[0], WIN), F32)], axis=0)


def between_windows():
    return [(1, side, side * WLAT * HALF_LON, WLAT * HALF_LON) for side in range(2)]


def corner_windows(bands):
    count = HALF_LAT * HALF_LON
    return [(band, side, at * count, count) for at, (band, side) in enumerate((b, s) for b in (0, bands) for s in range(2))]


def between_kernel(strips, columns_ref, odd_even_ref, even_odd_ref, labels_ref, bias_ref, qkv_weight_ref, out_weight_ref, inner_ref,
                   after_ref, out_ref, corner_queries_ref, corner_keys_ref, cells_ref, own_ref, queries_ref, keys_ref, attended_ref):
    row_count, _, feature = columns_ref.shape
    bands = row_count // WLAT
    received, own_labels = swapped(odd_even_ref, even_odd_ref)
    left_labels = left_labels_of(jnp.zeros((strips, WIN), F32), own_labels)
    windows = between_windows()
    half = HALF_LAT * WLON
    tokens_of = {}

    def put(first, rows, side, key_start, query_start):
        own = jnp.stack([half_of(columns_ref[row].astype(F32), side) for row in range(first, first + rows)])
        halo = normalize(jnp.stack([received(row, side) for row in range(first, first + rows)]))
        normed = normalize(own)
        cells = jnp.concatenate([normed, halo] if side else [halo, normed], axis=1)
        cells_ref[key_start : key_start + rows * WLON, :] = cells.reshape(rows * WLON, feature).astype(BF16)
        own_ref[query_start : query_start + rows * HALF_LON, :] = normed.reshape(rows * HALF_LON, feature).astype(BF16)
        return own

    for at, (band, side, start, count) in enumerate(windows):
        tokens_of[side] = put(HALF_LAT, WLAT, side, at * WIN, start)
    ends = corner_windows(bands)
    for at, (band, side, start, count) in enumerate(ends):
        put(row_count - HALF_LAT if band else 0, HALF_LAT, side, len(windows) * WIN + at * half, WLAT * WLON + start)
    queries_ref[...] = project(own_ref[...], qkv_weight_ref, 0, feature)
    keys_ref[...] = project(cells_ref[...], qkv_weight_ref, feature, 2 * feature)
    corner_queries_ref[...] = queries_ref[WLAT * WLON :, :]
    corner_keys_ref[...] = keys_ref[len(windows) * WIN :, :]
    side_attention(
        windows, bands, strips,
        lambda mine, columns: queries_ref[mine, columns],
        lambda at, columns: keys_ref[at * WIN : (at + 1) * WIN, columns],
        left_labels, labels_ref[...], bias_ref, attended_ref,
    )
    branch = out_project(attended_ref[...], out_weight_ref)
    for row in range(WLAT):
        middle = [inner_ref[strip * WIN + row * WLON : strip * WIN + (row + 1) * WLON, :].astype(F32) for strip in range(strips - 1)]
        ends = []
        for side, (_, _, start, _) in enumerate(windows):
            at = start + row * HALF_LON
            ends.append(tokens_of[side][row] + branch[at : at + HALF_LON])
        out_ref[row] = jnp.concatenate([ends[0]] + middle + [ends[1]], axis=0).astype(BF16)


def corner_kernel(strips, columns_ref, odd_even_ref, even_odd_ref, corner_odd_even_ref, corner_even_odd_ref, ends_ref, labels_ref, queries_ref, own_ref,
                  bias_ref, qkv_weight_ref, out_weight_ref, corner_ref, cells_ref, keys_ref, attended_ref):
    row_count, _, feature = columns_ref.shape
    bands = row_count // WLAT
    half = HALF_LAT * WLON
    _, own_labels = swapped(odd_even_ref, even_odd_ref)
    received, above_labels = swapped(corner_odd_even_ref, corner_even_odd_ref)
    left_labels = left_labels_of(above_labels[:strips], own_labels)
    windows = corner_windows(bands)
    for at, (band, side, start, count) in enumerate(windows):
        rows = range(0 if band else HALF_LAT, HALF_LAT if band else WLAT)
        near = normalize(jnp.stack([cells_of(ends_ref, 2 * row + side) for row in rows]))
        far = normalize(jnp.stack([received(row, side) for row in rows]))
        cells = jnp.concatenate([near, far] if side else [far, near], axis=1)
        cells_ref[at * half : (at + 1) * half, :] = cells.reshape(half, feature).astype(BF16)
    keys_ref[...] = project(cells_ref[...], qkv_weight_ref, feature, 2 * feature)

    def keys_of(at, columns):
        mine = slice(at * half, (at + 1) * half)
        pair = own_ref[mine, columns], keys_ref[mine, columns]
        return jnp.concatenate(pair if windows[at][0] else pair[::-1], axis=0)

    side_attention(
        windows, bands, strips, lambda mine, columns: queries_ref[mine, columns], keys_of,
        left_labels, labels_ref[...], bias_ref, attended_ref,
    )
    branch = out_project(attended_ref[...], out_weight_ref)
    for end in range(2):
        for row in range(HALF_LAT):
            cells = columns_ref[row_count - HALF_LAT + row if end else row].astype(F32)
            starts = [windows[2 * end + side][2] + row * HALF_LON for side in range(2)]
            added = jnp.concatenate([branch[start : start + HALF_LON] for start in starts], axis=0)
            corner_ref[end * HALF_LAT + row] = (cells + added).astype(BF16)


def last_kernel(strips, inner_ref, halo_ref, own_ref, labels_ref, bias_ref, qkv_weight_ref, out_weight_ref, corner_ref, between_ref,
                out_ref, cells_ref, keys_ref, attended_ref, block_ref, sems):
    row_count, column_count, feature = out_ref.shape
    copies = [pltpu.make_async_copy(between_ref, out_ref.at[pl.ds(HALF_LAT, row_count - WLAT)], sems.at[WLAT])]
    copies[0].start()
    bands = row_count // WLAT
    half = HALF_LAT * WLON
    places = [(side, strip) for side in range(2) for strip in range(strips - 1)]
    for at, (side, strip) in enumerate(places):
        block = halo_ref[HALF_LAT * (1 - side) : HALF_LAT * (2 - side), strip * WLON : (strip + 1) * WLON, :]
        cells_ref[at * half : (at + 1) * half, :] = block.astype(F32).reshape(half, feature).astype(BF16)
    keys_ref[...] = project(cells_ref[...], qkv_weight_ref, feature, 2 * feature)
    labels = labels_ref[...]
    label_columns = labels.T
    entries = []
    for at, (side, strip) in enumerate(places):
        mine = slice(at * half, (at + 1) * half)
        rows = slice(0, half) if side else slice(half, WIN)
        place = side * bands * strips + strip
        mask = excluded(label_columns[rows, place : place + 1], labels[place : place + 1])

        def both(head, mine=mine, side=side):
            pair = own_ref[mine, lanes(HEADS + head)], keys_ref[mine, lanes(head)]
            return jnp.concatenate(pair if side else pair[::-1], axis=0)

        for head in range(HEADS):
            entries.append(
                (
                    lambda mine=mine, head=head: own_ref[mine, lanes(head)],
                    lambda head=head, both=both: both(head),
                    lambda head=head, both=both: both(HEADS + head),
                    lambda mask=mask, head=head, rows=rows: bias_ref[head, rows, :] + mask,
                    storer(attended_ref, mine, head),
                )
            )
    attention(entries)
    for side, first in enumerate((0, row_count - HALF_LAT)):
        cells = (strips - 1) * half
        branch = out_project(attended_ref[side * cells : (side + 1) * cells, :], out_weight_ref)
        for row in range(HALF_LAT):
            at = side * HALF_LAT + row
            corner = corner_ref[at].astype(F32)
            middle = [branch[strip * half + row * WLON : strip * half + (row + 1) * WLON] for strip in range(strips - 1)]
            middle = inner_ref[at].astype(F32) + jnp.concatenate(middle, axis=0)
            block_ref[at] = jnp.concatenate([corner[:HALF_LON], middle, corner[HALF_LON:]], axis=0).astype(BF16)
            copies.append(pltpu.make_async_copy(block_ref.at[at], out_ref.at[first + row], sems.at[at]))
            copies[-1].start()
    for copy in copies:
        copy.wait()


def shards(tokens, qkv_weight, out_weight, bias_table, position_index, region_label):
    row_count, column_count, feature = tokens.shape
    bands, strips = row_count // WLAT, column_count // WLON
    whole = shape(*tokens.shape)
    inner_columns = column_count - WLON
    blocks = feature // WIN
    dma = pltpu.SemaphoreType.DMA

    (label_own,) = run(
        functools.partial(label_kernel, strips), [shape(bands * strips, WIN, dtype=F32)], [region_label], flops=5 * 10**9
    )
    (ends,) = run(message_kernel, [shape(2 * WLAT * blocks + 1, HALF_LON, WIN)], [tokens, label_own], flops=5 * 10**9)
    ends_received = lat_exchange(ends, 2 * HALF_LAT * blocks)
    normed_rows, inner_rows, middle, columns = run(
        split_kernel,
        [
            shape(WLAT, inner_columns, feature),
            shape(WLAT, inner_columns, feature),
            shape(row_count - WLAT, inner_columns, feature),
            shape(row_count, WLON, feature),
        ],
        [tokens, ends],
        specs=[VMEM, ANY],
    )
    rows_received = lat_exchange(normed_rows, HALF_LAT)
    message = shape(row_count * blocks + 1, HALF_LON, WIN)
    columns_sent = run(column_kernel, [message, message], [columns, label_own], flops=2 * 10**10)
    columns_received = lon_exchange(*columns_sent[::-1])

    inner_cells = (strips - 1) * WIN
    inner, bias = run(
        functools.partial(inner_kernel, strips),
        [shape(inner_cells, feature), shape(HEADS, WIN, WIN, dtype=F32)],
        [middle, label_own, bias_table.T, position_index, qkv_weight, out_weight, columns_sent[0]],
        specs=[VMEM] * 6 + [ANY],
        scratch=[pltpu.VMEM((inner_cells, width * feature), BF16) for width in (1, 3, 1)]
        + [pltpu.VMEM((8, -(-bias_table.shape[0] // 128) * 128), F32)],
        mib=12,
        flops=5 * 10**9,
    )
    message = shape(WLAT * blocks + 1, HALF_LON, WIN)
    *corners, labels = run(
        functools.partial(corner_message_kernel, strips),
        [message, message, shape(16, WIN, dtype=F32)],
        [ends_received, label_own, inner],
        specs=[VMEM, VMEM, ANY],
    )
    corners_received = lon_exchange(*corners[::-1])
    row_cells = (strips - 1) * WIN
    (row_qkv,) = run(
        functools.partial(rows_kernel, strips),
        [shape(row_cells, 3 * feature)],
        [normed_rows, qkv_weight, corners[0]],
        specs=[VMEM, VMEM, ANY],
        scratch=[pltpu.VMEM((row_cells, feature), BF16)],
        mib=8,
    )

    side_cells, corner_cells = WLAT * WLON, 2 * HALF_LAT * WLON
    every = 4 * WIN
    between, corner_queries, corner_keys = run(
        functools.partial(between_kernel, strips),
        [shape(row_count - WLAT, column_count, feature), shape(corner_cells, feature), shape(2 * WIN, 2 * feature)],
        [columns, *columns_received, labels, bias, qkv_weight, out_weight, inner, row_qkv],
        specs=[VMEM] * 8 + [ANY],
        scratch=[pltpu.VMEM((count, width * feature), BF16) for count, width in
                 ((every, 1), (side_cells + corner_cells, 1), (side_cells + corner_cells, 1), (every, 2), (side_cells, 1))],
        mib=12,
    )
    (corner,) = run(
        functools.partial(corner_kernel, strips),
        [shape(WLAT, WLON, feature)],
        [columns, *columns_received, *corners_received, ends_received, labels, corner_queries, corner_keys, bias, qkv_weight, out_weight],
        scratch=[pltpu.VMEM((count, width * feature), BF16) for count, width in ((2 * WIN, 1), (2 * WIN, 2), (corner_cells, 1))],
        mib=12,
    )
    (out,) = run(
        functools.partial(last_kernel, strips),
        [whole],
        [inner_rows, rows_received, row_qkv, labels, bias, qkv_weight, out_weight, corner, between],
        out_specs=[HBM],
        mib=12,
        scratch=[pltpu.VMEM((row_cells, width * feature), BF16) for width in (1, 2, 1)]
        + [pltpu.VMEM((WLAT, column_count, feature), BF16), dma((WLAT + 1,))],
    )
    return out


def solution(mesh):
    in_specs = (P("lat", "lon", None), P(), P(), P(), P(), P("lat", "lon"))
    out_specs = P("lat", "lon", None)
    return jax.shard_map(shards, mesh=mesh, in_specs=in_specs, out_specs=out_specs, check_vma=False)
```
